32 devices in a mesh: parts: 2 (over y), lat: 8 (over z, x), tok: 2 (over core).
Axes of the slice: x: 2, y: 2, z: 4, core: 2. Of those that a mesh axis runs over, the one named last changes fastest.
Arguments:
- residual: bfloat16 [512, 3584], P(('parts', 'tok'), 'lat'), parts along dimension 0, may hold values from -6 to 6
- enc_weight: bfloat16 [3584, 4096], P(None, 'lat'), may hold values from -0.09375 to 0.09375
- enc_bias: float32 [4096], P('lat'), may hold values from -3 to 3
- threshold: float32 [4096], P('lat'), may hold values from 0.15 to 0.7
- partners: int32 [8, 4], replicated, may hold values from 0 to 8, as said below
Outputs:
- gram_tiles: bfloat16 [16, 4, 512, 512], P(('parts', 'lat'), None, 'tok'), parts along dimension 0
The draws below stay inside these ranges and needn't reach their ends.
There are 2 independent parts, one for each index of `parts`. The reference program is written for one: setup_inputs(seed, part) draws one part's arguments, and reference() takes and returns one part's arrays. A program takes and returns all parts, laid end to end along the dimension named above; an argument that names none is the same for every part. Nothing has to cross between parts.
Inputs may be any that keep to these rules, and one draw needn't show every extreme that they name: `partners`: row d lists the partner blocks of latent block d in 4 slots: slot 0 is d itself, the live slots come first and hold distinct block numbers, the others hold the null value 8; every row has one live slot or more, and some row has all 4 slots live.
All inputs are finite; a program needn't handle non-finite values.
Results may differ from the reference program's by a relative error of at most 0.0023.
Values may be sent and summed in bfloat16 or wider, within the bound.
No kernel may reach another device: no remote copies, remote signals or barrier semaphores. Data moves between devices by JAX's collectives and lax.ppermute only.
A program may use at most 64 MiB of HBM per device.

```python
import jax
import jax.numpy as jnp
from jax import lax

D = 3584
LAT_DEV = 512
PAIRS = 4
BLOCKS = 8
LATENTS = 4096
TOKENS = 256


def draw_partners(key, part):
    key = jax.random.fold_in(key, 7)
    row_ids = jnp.arange(BLOCKS, dtype=jnp.int32)

    def one_row(row_id):
        row_key = jax.random.fold_in(key, row_id)
        shuffled = jax.random.permutation(row_key, BLOCKS - 1)[:PAIRS - 1].astype(jnp.int32)
        others = (row_id + 1 + shuffled) % BLOCKS
        return jnp.concatenate([row_id[None], others])
    table = jax.vmap(one_row)(row_ids)
    live_count = jax.random.randint(jax.random.fold_in(key, 100003), (BLOCKS,), 1, PAIRS + 1)
    full_row = jax.random.randint(jax.random.fold_in(key, 100019), (), 0, BLOCKS)
    live_count = jnp.where(row_ids == full_row, PAIRS, live_count)
    slot_ids = jnp.arange(PAIRS, dtype=jnp.int32)
    return jnp.where(slot_ids[None, :] < live_count[:, None], table, BLOCKS).astype(jnp.int32)


def steps_of(stream_key, dims, shards, smallest, top_value):
    gain = 1.0
    for position, parts in shards:
        heights = jax.random.uniform(jax.random.fold_in(jax.random.fold_in(stream_key, 6), position), (parts,), jnp.float32, smallest / len(shards), top_value / len(shards))
        gain = gain * jnp.repeat(jnp.exp(heights), dims[position] // parts).reshape((-1,) + (1,) * (len(dims) - 1 - position))
    return gain


def normal_values(rng, extent, deviation, limit, cuts=(), kind=jnp.bfloat16):
    result = jax.random.normal(rng, extent, jnp.float32) * deviation
    if len(cuts) > 0:
        result = steps_of(rng, extent, cuts, -0.22, 0.18) * result
    return jnp.clip(result, min=-limit, max=limit).astype(kind)


def setup_inputs(seed: int = 0, part: int = 0) -> dict:
    streams_of = jax.random.split(jax.random.key(seed), 6)
    own_keys = jax.random.split(jax.random.fold_in(streams_of[5], part), 6)
    return {
        "residual": normal_values(own_keys[0], (TOKENS, D), 1.0, 6.0, ((0, 2), (1, 8))),
        "enc_weight": normal_values(streams_of[1], (D, LATENTS), D ** -0.5, 0.09375, ((1, 8),)),
        "enc_bias": normal_values(streams_of[2], (LATENTS,), 0.5, 3.0, ((0, 8),), jnp.float32),
        "threshold": jnp.clip(0.15 + 0.54999998 * jax.random.uniform(streams_of[3], (LATENTS,), jnp.float32) ** steps_of(streams_of[3], (LATENTS,), ((0, 8),), -0.2, 0.2), 0.15, 0.7),
        "partners": draw_partners(jax.random.fold_in(streams_of[5], 71), part),
    }


ramp_width = 0.25


def reference(residual, enc_weight, enc_bias, threshold, partners):
    pre_acts = jnp.dot(residual, enc_weight, preferred_element_type=jnp.float32) + enc_bias
    activations = (pre_acts * jnp.clip((pre_acts - threshold) / ramp_width + 0.5, 0.0, 1.0)).astype(jnp.bfloat16)
    blocks = activations.reshape(TOKENS, BLOCKS, LAT_DEV).transpose(1, 0, 2)
    tok_scale = 1.0 / TOKENS

    def one_owner(inputs):
        own_block, pair_row = inputs

        def one_pair(partner):
            clamped = jnp.minimum(partner, BLOCKS - 1).astype(jnp.int32)
            partner_block = blocks[clamped]
            tile_sum = jnp.dot(own_block.T, partner_block, preferred_element_type=jnp.float32)
            is_live = (partner < BLOCKS).astype(jnp.float32)
            return (tile_sum * is_live * tok_scale).astype(jnp.bfloat16)

        return lax.map(one_pair, pair_row)

    return lax.map(one_owner, (blocks, partners))
```

```python
import functools

import jax
import jax.numpy as jnp
import numpy as np
from jax import lax
from jax.experimental import pallas as pl
from jax.experimental.pallas import tpu as pltpu
from jax.sharding import PartitionSpec as P

ramp_width = 0.25
ring_limit = 16
vmem_limit = 32 * 1024 * 1024

rows_by_rows = (((0,), (0,)), ((), ()))


def ring_order(n):
    return list(range(0, n, 2)) + list(range(1, n, 2))[::-1]


def activate(pre_acts, threshold):
    gate = jnp.clip((pre_acts - threshold) / ramp_width + 0.5, 0.0, 1.0)
    return (pre_acts * gate).astype(jnp.bfloat16)


def project(x, w):
    return lax.dot_general(x, w, rows_by_rows, preferred_element_type=jnp.float32)


def first_step(_, x, w, total):
    total[...] = project(x[...], w[0])


def middle_step(_, x_f, x_b, w_f, w_b, before, total):
    total[...] = before[...] + project(x_f[...], w_f[0]) + project(x_b[...], w_b[0])


def last_step(_, x_f, x_b, w, before, bias, threshold, acts):
    half = x_f.shape[0]
    pre_acts = (
        before[...] + project(x_f[...], w[0, :half]) + project(x_b[...], w[0, half:]) + bias[...]
    )
    acts[...] = activate(pre_acts, threshold[...])


def whole(shape):
    return pl.BlockSpec(shape, lambda i, ids: (0,) * len(shape))


def step_call(kernel, ids, places, xs, weights, others, out):
    depth, width = weights.shape[1:]
    picks = [
        pl.BlockSpec((1, depth, width), functools.partial(lambda k, i, ids: (ids[k], 0, 0), k))
        for k in places
    ]
    rows = sum(x.shape[0] for x in xs)
    return pl.pallas_call(
        kernel,
        out_shape=out,
        grid_spec=pltpu.PrefetchScalarGridSpec(
            num_scalar_prefetch=1,
            grid=(1,),
            in_specs=[whole(x.shape) for x in xs] + picks + [whole(o.shape) for o in others],
            out_specs=whole(out.shape),
        ),
        compiler_params=pltpu.CompilerParams(vmem_limit_bytes=vmem_limit),
        cost_estimate=pl.CostEstimate(
            flops=2 * rows * xs[0].shape[1] * width,
            bytes_accessed=2 * rows * width + 8 * xs[0].shape[1] * width,
            transcendentals=0,
        ),
    )(ids, *xs, *([weights] * len(places)), *others)


def encode_on_ring(residual, enc_weight, enc_bias, threshold, n):
    tok_rows, depth = residual.shape
    width = enc_weight.shape[1]
    order = ring_order(n)
    forward = [(order[i], order[(i + 1) % n]) for i in range(n)]
    backward = [(d, s) for s, d in forward]
    position = {b: i for i, b in enumerate(order)}
    origins = np.array(
        [[order[(position[b] - h) % n] for h in range(n)] for b in range(n)], np.int32
    )
    ids = jnp.asarray(origins)[lax.axis_index("lat")]
    x = residual.T
    weights = enc_weight.reshape(n, depth, width)
    total_shape = jax.ShapeDtypeStruct((tok_rows, width), jnp.float32)
    ahead = behind = x
    total = None
    for hop in range(1, n // 2):
        ahead = lax.ppermute(ahead, "lat", forward)
        behind = lax.ppermute(behind, "lat", backward)
        if hop == 1:
            total = step_call(first_step, ids, [0], [x], weights, [], total_shape)
        total = step_call(
            middle_step, ids, [hop, n - hop], [ahead, behind], weights, [total], total_shape
        )
    half = depth // 2
    ahead = lax.ppermute(ahead[:half], "lat", forward)
    behind = lax.ppermute(behind[half:], "lat", backward)
    return step_call(
        last_step,
        ids,
        [n // 2],
        [ahead, behind],
        weights,
        [total, enc_bias.reshape(1, width), threshold.reshape(1, width)],
        jax.ShapeDtypeStruct((tok_rows, width), jnp.bfloat16),
    )


def encode_gathered(residual, enc_weight, enc_bias, threshold):
    pre_acts = (
        jnp.dot(
            lax.all_gather(residual, "lat", axis=1, tiled=True),
            enc_weight,
            preferred_element_type=jnp.float32,
        )
        + enc_bias
    )
    return activate(pre_acts, threshold)


def select_kernel(partners, slices, outgoing):
    blocks, slots = partners.shape
    for d in range(blocks):
        for k in range(1, slots):
            outgoing[d, k - 1] = slices[jnp.minimum(partners[d, k], blocks - 1)]


def select(slices, partners):
    blocks, rows, width = slices.shape
    slots = partners.shape[1]
    out = (blocks, slots - 1, rows, width)
    if rows % 16:
        return jnp.take(slices, jnp.minimum(partners[:, 1:], blocks - 1), axis=0)
    return pl.pallas_call(
        select_kernel,
        out_shape=jax.ShapeDtypeStruct(out, slices.dtype),
        grid_spec=pltpu.PrefetchScalarGridSpec(
            num_scalar_prefetch=1,
            grid=(1,),
            in_specs=[whole(slices.shape)],
            out_specs=whole(out),
        ),
        compiler_params=pltpu.CompilerParams(vmem_limit_bytes=vmem_limit),
    )(partners, slices)


def gram_kernel(tok_scale, place, own, own_twin, got, got_twin, tiles):
    slots, rows, width = tiles.shape[1:]
    columns = pl.ds(pl.multiple_of(place[0] * rows, rows), rows)
    left, left_twin = own[:, columns], own_twin[:, columns]
    tiles[0, 0] = (
        (project(left, own[...]) + project(left_twin, own_twin[...])) * tok_scale
    ).astype(tiles.dtype)
    for k in range(1, slots):

        @pl.when(place[k] != 0)
        def _():
            tile = project(left, got[k - 1]) + project(left_twin, got_twin[k - 1])
            tiles[0, k] = (tile * tok_scale).astype(tiles.dtype)

        @pl.when(place[k] == 0)
        def _():
            tiles[0, k] = jnp.zeros((rows, width), tiles.dtype)


def gram(own, own_twin, got, got_twin, place, tok_scale, halves):
    tok_rows, width = own.shape
    slots = got.shape[0] + 1
    out = (1, slots, width // halves, width)
    return pl.pallas_call(
        functools.partial(gram_kernel, tok_scale),
        out_shape=jax.ShapeDtypeStruct(out, own.dtype),
        grid_spec=pltpu.PrefetchScalarGridSpec(
            num_scalar_prefetch=1,
            grid=(1,),
            in_specs=[whole(a.shape) for a in (own, own_twin, got, got_twin)],
            out_specs=whole(out),
        ),
        compiler_params=pltpu.CompilerParams(vmem_limit_bytes=vmem_limit),
    )(place, own, own_twin, got, got_twin)


def body(residual, enc_weight, enc_bias, threshold, partners):
    n = lax.axis_size("lat")
    halves = lax.axis_size("tok")
    tok_rows = residual.shape[0]
    width = enc_weight.shape[1]
    slots = partners.shape[1]
    tok_scale = 1.0 / (tok_rows * halves)
    swap = [(i, 1 - i) for i in range(2)]
    if n <= ring_limit:
        acts = encode_on_ring(residual, enc_weight, enc_bias, threshold, n)
    else:
        acts = encode_gathered(residual, enc_weight, enc_bias, threshold)
    acts_twin = lax.ppermute(acts, "tok", swap)
    slices = lax.all_to_all(acts.reshape(n, tok_rows // n, width), "lat", 0, 0)
    got = lax.all_to_all(select(slices, partners), "lat", 0, 0)
    got = got.transpose(1, 0, 2, 3).reshape(slots - 1, tok_rows, width)
    got_twin = lax.ppermute(got, "tok", swap)
    row = lax.dynamic_index_in_dim(partners, lax.axis_index("lat"), 0, keepdims=False)
    place = jnp.where(
        jnp.arange(slots) == 0, lax.axis_index("tok"), (row < n).astype(jnp.int32)
    ).astype(jnp.int32)
    return gram(acts, acts_twin, got, got_twin, place, tok_scale, halves)


def solution(mesh):
    return jax.shard_map(
        body,
        mesh=mesh,
        in_specs=(P(("parts", "tok"), "lat"), P(None, "lat"), P("lat"), P("lat"), P()),
        out_specs=P(("parts", "lat"), None, "tok", None),
        check_vma=False,
    )
```

```python
import functools

import jax
import jax.numpy as jnp
import numpy as np
from jax import lax
from jax.experimental import pallas as pl
from jax.experimental.pallas import tpu as pltpu
from jax.sharding import PartitionSpec as P

ramp_width = 0.25
ring_limit = 16
vmem_limit = 32 * 1024 * 1024

rows_by_rows = (((0,), (0,)), ((), ()))


def ring_order(n):
    return list(range(0, n, 2)) + list(range(1, n, 2))[::-1]


def activate(pre_acts, threshold):
    gate = jnp.clip((pre_acts - threshold) / ramp_width + 0.5, 0.0, 1.0)
    return (pre_acts * gate).astype(jnp.bfloat16)


def project(x, w):
    return lax.dot_general(x, w, rows_by_rows, preferred_element_type=jnp.float32)


def first_step(_, x, x_f, x_b, w, w_f, w_b, total):
    total[...] = project(x[...], w[0]) + project(x_f[...], w_f[0]) + project(x_b[...], w_b[0])


def middle_step(_, x_f, x_b, w_f, w_b, before, total):
    total[...] = before[...] + project(x_f[...], w_f[0]) + project(x_b[...], w_b[0])


def last_step(_, x_f, x_b, x_far, w_f, w_b, w_far, before, bias, threshold, acts):
    pre_acts = before[...] + project(x_f[...], w_f[0]) + project(x_b[...], w_b[0])
    pre_acts = pre_acts + project(x_far[...], w_far[0]) + bias[...]
    acts[...] = activate(pre_acts, threshold[...])


def whole(shape):
    return pl.BlockSpec(shape, lambda i, ids: (0,) * len(shape))


def step_call(kernel, ids, places, xs, weights, others, out):
    depth, width = weights.shape[1:]
    picks = [
        pl.BlockSpec((1, depth, width), functools.partial(lambda k, i, ids: (ids[k], 0, 0), k))
        for k in places
    ]
    rows = sum(x.shape[0] for x in xs)
    return pl.pallas_call(
        kernel,
        out_shape=out,
        grid_spec=pltpu.PrefetchScalarGridSpec(
            num_scalar_prefetch=1,
            grid=(1,),
            in_specs=[whole(x.shape) for x in xs] + picks + [whole(o.shape) for o in others],
            out_specs=whole(out.shape),
        ),
        compiler_params=pltpu.CompilerParams(vmem_limit_bytes=vmem_limit),
        cost_estimate=pl.CostEstimate(
            flops=2 * rows * xs[0].shape[1] * width,
            bytes_accessed=2 * rows * width + 8 * xs[0].shape[1] * width,
            transcendentals=0,
        ),
    )(ids, *xs, *([weights] * len(places)), *others)


class Ring:
    def __init__(self, n):
        order = ring_order(n)
        position = {b: i for i, b in enumerate(order)}
        self.n = n
        self.hops = n // 2 - 1
        self.forward = [(order[i], order[(i + 1) % n]) for i in range(n)]
        self.backward = [(d, s) for s, d in self.forward]
        self.across = [(order[i], order[(i + n // 2) % n]) for i in range(n)]
        self.origins = np.array(
            [[order[(position[b] - h) % n] for h in range(n)] for b in range(n)], np.int32
        )

    def ids(self):
        return jnp.asarray(self.origins)[lax.axis_index("lat")]

    def gather(self, x, arrived):
        ahead = lax.ppermute(x, "lat", self.forward)
        behind = lax.ppermute(x, "lat", self.backward)
        far = lax.ppermute(x, "lat", self.across)
        state = None
        for hop in range(1, self.hops):
            now_ahead, now_behind = ahead, behind
            ahead = lax.ppermute(ahead, "lat", self.forward)
            behind = lax.ppermute(behind, "lat", self.backward)
            state = arrived(hop, now_ahead, now_behind, state)
            if hop + 1 < self.hops:
                state, ahead, behind = lax.optimization_barrier((state, ahead, behind))
        return state, ahead, behind, far


def encode_on_ring(residual, enc_weight, enc_bias, threshold, ring, ids):
    tok_rows, depth = residual.shape
    width = enc_weight.shape[1]
    n = ring.n
    x = residual.T
    weights = enc_weight.reshape(n, depth, width)
    total_shape = jax.ShapeDtypeStruct((tok_rows, width), jnp.float32)

    def arrived(hop, ahead, behind, total):
        if hop == 1:
            places, xs, others = [0, 1, n - 1], [x, ahead, behind], []
        else:
            places, xs, others = [hop, n - hop], [ahead, behind], [total]
        kernel = first_step if hop == 1 else middle_step
        return step_call(kernel, ids, places, xs, weights, others, total_shape)

    total, ahead, behind, far = ring.gather(x, arrived)
    return step_call(
        last_step,
        ids,
        [ring.hops, n - ring.hops, n // 2],
        [ahead, behind, far],
        weights,
        [total, enc_bias.reshape(1, width), threshold.reshape(1, width)],
        jax.ShapeDtypeStruct((tok_rows, width), jnp.bfloat16),
    )


def encode_gathered(residual, enc_weight, enc_bias, threshold):
    pre_acts = (
        jnp.dot(
            lax.all_gather(residual, "lat", axis=1, tiled=True),
            enc_weight,
            preferred_element_type=jnp.float32,
        )
        + enc_bias
    )
    return activate(pre_acts, threshold)


def select(slices, partners):
    return jnp.take(slices, jnp.minimum(partners[:, 1:], slices.shape[0] - 1), axis=0)


def choose_kernel(picks, *refs):
    blocks, chosen = refs[:-1], refs[-1]
    for k in range(chosen.shape[0]):
        for i, block in enumerate(blocks):

            @pl.when(picks[k + 1] == i)
            def _():
                chosen[k] = block[...]


def choose(picks, blocks):
    out = (picks.shape[0] - 1,) + blocks[0].shape
    return pl.pallas_call(
        choose_kernel,
        out_shape=jax.ShapeDtypeStruct(out, blocks[0].dtype),
        grid_spec=pltpu.PrefetchScalarGridSpec(
            num_scalar_prefetch=1,
            grid=(1,),
            in_specs=[whole(b.shape) for b in blocks],
            out_specs=whole(out),
        ),
        compiler_params=pltpu.CompilerParams(vmem_limit_bytes=vmem_limit),
    )(picks, *blocks)


def gram_kernel(tok_scale, place, own, own_twin, got, got_twin, tiles):
    rows, width = tiles.shape[2:]
    columns = pl.ds(pl.multiple_of(place[0] * rows, rows), rows)
    k = pl.program_id(0)

    def tile_of(right, right_twin):
        tile = project(own[:, columns], right) + project(own_twin[:, columns], right_twin)
        tiles[0, 0] = (tile * tok_scale).astype(tiles.dtype)

    @pl.when(k == 0)
    def _():
        tile_of(own[...], own_twin[...])

    @pl.when((k > 0) & (place[k] != 0))
    def _():
        tile_of(got[k - 1], got_twin[k - 1])

    @pl.when((k > 0) & (place[k] == 0))
    def _():
        tiles[0, 0] = jnp.zeros((rows, width), tiles.dtype)


def gram(own, own_twin, got, got_twin, place, tok_scale, halves):
    tok_rows, width = own.shape
    slots = got.shape[0] + 1
    rows = width // halves
    return pl.pallas_call(
        functools.partial(gram_kernel, tok_scale),
        out_shape=jax.ShapeDtypeStruct((1, slots, rows, width), own.dtype),
        grid_spec=pltpu.PrefetchScalarGridSpec(
            num_scalar_prefetch=1,
            grid=(slots,),
            in_specs=[whole(a.shape) for a in (own, own_twin, got, got_twin)],
            out_specs=pl.BlockSpec((1, 1, rows, width), lambda i, place: (0, i, 0, 0)),
        ),
        compiler_params=pltpu.CompilerParams(vmem_limit_bytes=vmem_limit),
    )(place, own, own_twin, got, got_twin)


def body(residual, enc_weight, enc_bias, threshold, partners):
    n = lax.axis_size("lat")
    halves = lax.axis_size("tok")
    tok_rows = residual.shape[0]
    width = enc_weight.shape[1]
    slots = partners.shape[1]
    tok_scale = 1.0 / (tok_rows * halves)
    swap = [(i, 1 - i) for i in range(2)]
    row = lax.dynamic_index_in_dim(partners, lax.axis_index("lat"), 0, keepdims=False)
    place = jnp.where(
        jnp.arange(slots) == 0, lax.axis_index("tok"), (row < n).astype(jnp.int32)
    ).astype(jnp.int32)
    if n <= ring_limit:
        ring = Ring(n)
        ids = ring.ids()
        acts = encode_on_ring(residual, enc_weight, enc_bias, threshold, ring, ids)
        acts_twin = lax.ppermute(acts, "tok", swap)
        blocks = {0: acts}

        def arrived(hop, ahead, behind, state):
            blocks[hop], blocks[n - hop] = ahead, behind
            return acts_twin

        acts_twin, ahead, behind, far = ring.gather(acts, arrived)
        blocks[ring.hops], blocks[n - ring.hops], blocks[n // 2] = ahead, behind, far
        picks = jnp.sum(jnp.where(row[:, None] == ids[None, :], jnp.arange(n), 0), axis=1)
        got = choose(picks.astype(jnp.int32), [blocks[i] for i in range(n)])
    else:
        acts = encode_gathered(residual, enc_weight, enc_bias, threshold)
        acts_twin = lax.ppermute(acts, "tok", swap)
        slices = lax.all_to_all(acts.reshape(n, tok_rows // n, width), "lat", 0, 0)
        got = lax.all_to_all(select(slices, partners), "lat", 0, 0)
        got = got.transpose(1, 0, 2, 3).reshape(slots - 1, tok_rows, width)
    got_twin = lax.ppermute(got, "tok", swap)
    return gram(acts, acts_twin, got, got_twin, place, tok_scale, halves)


def solution(mesh):
    return jax.shard_map(
        body,
        mesh=mesh,
        in_specs=(P(("parts", "tok"), "lat"), P(None, "lat"), P("lat"), P("lat"), P()),
        out_specs=P(("parts", "lat"), None, "tok", None),
        check_vma=False,
    )
```

```python
import functools

import jax
import jax.numpy as jnp
from jax import lax
from jax.experimental import pallas as pl
from jax.experimental.pallas import tpu as pltpu
from jax.sharding import PartitionSpec as P

ramp_width = 0.25
ring_limit = 16

in_vmem = pl.BlockSpec(memory_space=pltpu.VMEM)
in_smem = pl.BlockSpec(memory_space=pltpu.SMEM)
in_hbm = pl.BlockSpec(memory_space=pltpu.HBM)
params = pltpu.CompilerParams(vmem_limit_bytes=24 * 1024 * 1024)

rows_by_rows = (((0,), (0,)), ((), ()))


def place_on_ring(block, n):
    half = block // 2
    return half + (block % 2) * (n - 1 - 2 * half)


def block_at(place, n):
    up = 2 * place
    if isinstance(place, int):
        return up if place < n // 2 else 2 * n - 1 - up
    return jnp.where(place < n // 2, up, 2 * n - 1 - up)


def origin(hop, n):
    me = place_on_ring(lax.axis_index("lat"), n)
    return block_at(lax.rem(me + n - hop, n), n)


def activate(pre_acts, threshold):
    gate = jnp.clip((pre_acts - threshold) / ramp_width + 0.5, 0.0, 1.0)
    return (pre_acts * gate).astype(jnp.bfloat16)


def project(x, w):
    return lax.dot_general(x, w, rows_by_rows, preferred_element_type=jnp.float32)


def first_step(x_f, x_b, weights, total):
    n = weights.shape[0]
    total[...] = project(x_f[...], weights[origin(1, n)]) + project(x_b[...], weights[origin(-1, n)])


def middle_step(hops, x, x_f, x_b, before, weights, total):
    n = weights.shape[0]
    total[...] = before[...]
    for hop, arrived in zip(hops, (x_f, x_b, x)):
        total[...] += project(arrived[...], weights[origin(hop, n)])


def last_step(hops, x_f, x_b, x_far, before, weights, bias, threshold, acts):
    n = weights.shape[0]
    pre_acts = before[...] + bias[...]
    for hop, arrived in zip(hops, (x_f, x_b, x_far)):
        pre_acts = pre_acts + project(arrived[...], weights[origin(hop, n)])
    acts[...] = activate(pre_acts, threshold[...])


def cost(rows, depth, width, blocks):
    return pl.CostEstimate(
        flops=2 * rows * depth * width * blocks,
        bytes_accessed=2 * depth * (rows + width) * blocks + 8 * rows * width,
        transcendentals=0,
    )


class Ring:
    def __init__(self, n):
        walk = [block_at(i, n) for i in range(n)]
        self.n = n
        self.hops = n // 2 - 1
        self.forward = [(walk[i], walk[(i + 1) % n]) for i in range(n)]
        self.backward = [(d, s) for s, d in self.forward]
        self.across = [(walk[i], walk[(i + n // 2) % n]) for i in range(n)]

    def gather(self, x, arrived):
        ahead = lax.ppermute(x, "lat", self.forward)
        behind = lax.ppermute(x, "lat", self.backward)
        far = lax.ppermute(x, "lat", self.across)
        state = None
        for hop in range(1, self.hops):
            now_ahead, now_behind = ahead, behind
            ahead = lax.ppermute(ahead, "lat", self.forward)
            behind = lax.ppermute(behind, "lat", self.backward)
            state = arrived(hop, now_ahead, now_behind, state)
            if hop + 1 < self.hops:
                state, ahead, behind, far = lax.optimization_barrier(
                    (state, ahead, behind, far)
                )
        return state, ahead, behind, far


def encode_on_ring(residual, enc_weight, enc_bias, threshold, ring):
    tok_rows, depth = residual.shape
    width = enc_weight.shape[1]
    n = ring.n
    x = residual.T
    weights = enc_weight.reshape(n, depth, width)
    total_shape = jax.ShapeDtypeStruct((tok_rows, width), jnp.float32)

    def arrived(hop, ahead, behind, total):
        if hop == 1:
            kernel, operands = first_step, (ahead, behind, weights)
        elif hop == 2:
            kernel = functools.partial(middle_step, (2, -2, 0))
            operands = (x, ahead, behind, total, weights)
        else:
            kernel = functools.partial(middle_step, (hop, -hop))
            operands = (x, ahead, behind, total, weights)
        return pl.pallas_call(
            kernel,
            out_shape=total_shape,
            in_specs=[in_vmem] * len(operands),
            out_specs=in_vmem,
            compiler_params=params,
            cost_estimate=cost(tok_rows, depth, width, 3),
        )(*operands)

    total, ahead, behind, far = ring.gather(x, arrived)
    return pl.pallas_call(
        functools.partial(last_step, (ring.hops, -ring.hops, n // 2)),
        out_shape=jax.ShapeDtypeStruct((tok_rows, width), jnp.bfloat16),
        in_specs=[in_vmem] * 7,
        out_specs=in_vmem,
        compiler_params=params,
        cost_estimate=cost(tok_rows, depth, width, 3),
    )(
        ahead,
        behind,
        far,
        total,
        weights,
        enc_bias.reshape(1, width),
        threshold.reshape(1, width),
    )


def encode_gathered(residual, enc_weight, enc_bias, threshold):
    pre_acts = (
        jnp.dot(
            lax.all_gather(residual, "lat", axis=1, tiled=True),
            enc_weight,
            preferred_element_type=jnp.float32,
        )
        + enc_bias
    )
    return activate(pre_acts, threshold)


def choose_kernel(partners, *refs):
    blocks, chosen = refs[:-1], refs[-1]
    n = len(blocks)
    me = lax.axis_index("lat")
    for k in range(chosen.shape[0]):
        listed = partners[k + 1, me]
        hop = lax.rem(place_on_ring(me, n) + n - place_on_ring(jnp.minimum(listed, n - 1), n), n)
        for i, block in enumerate(blocks):

            @pl.when(hop == i)
            def _():
                chosen[k] = block[...]


def choose(partners, blocks):
    return pl.pallas_call(
        choose_kernel,
        out_shape=jax.ShapeDtypeStruct((partners.shape[0] - 1,) + blocks[0].shape, blocks[0].dtype),
        in_specs=[in_smem] + [in_vmem] * len(blocks),
        out_specs=in_vmem,
        compiler_params=params,
    )(partners, *blocks)


def gram_kernel(tok_scale, n, partners, own, own_twin, got, got_twin, out, tiles, sems):
    slots, rows, width = tiles.shape
    me = lax.axis_index("lat")
    columns = pl.ds(pl.multiple_of(lax.axis_index("tok") * rows, rows), rows)
    left = jnp.concatenate([own[:, columns], own_twin[:, columns]], axis=0)

    def tile_of(right, right_twin):
        tile = project(left, jnp.concatenate([right, right_twin], axis=0))
        return (tile * tok_scale).astype(tiles.dtype)

    copies = [pltpu.make_async_copy(tiles.at[k], out.at[0, k], sems.at[k]) for k in range(slots)]
    tiles[0] = tile_of(own[...], own_twin[...])
    copies[0].start()
    for k in range(1, slots):
        live = partners[k, me] < n

        @pl.when(live)
        def _():
            tiles[k] = tile_of(got[k - 1], got_twin[k - 1])

        @pl.when(jnp.logical_not(live))
        def _():
            tiles[k] = jnp.zeros((rows, width), tiles.dtype)

        copies[k].start()
    for copy in copies:
        copy.wait()


def gram(partners, own, own_twin, got, got_twin, tok_scale, halves, n):
    tok_rows, width = own.shape
    slots = partners.shape[0]
    rows = width // halves
    return pl.pallas_call(
        functools.partial(gram_kernel, tok_scale, n),
        out_shape=jax.ShapeDtypeStruct((1, slots, rows, width), own.dtype),
        in_specs=[in_smem] + [in_vmem] * 4,
        out_specs=in_hbm,
        scratch_shapes=[
            pltpu.VMEM((slots, rows, width), own.dtype),
            pltpu.SemaphoreType.DMA((slots,)),
        ],
        compiler_params=params,
    )(partners, own, own_twin, got, got_twin)


def body(residual, enc_weight, enc_bias, threshold, partners):
    n = lax.axis_size("lat")
    halves = lax.axis_size("tok")
    tok_rows = residual.shape[0]
    width = enc_weight.shape[1]
    slots = partners.shape[1]
    tok_scale = 1.0 / (tok_rows * halves)
    swap = [(i, 1 - i) for i in range(2)]
    by_slot = partners.T
    if 8 <= n <= ring_limit:
        ring = Ring(n)
        acts = encode_on_ring(residual, enc_weight, enc_bias, threshold, ring)
        acts_twin = lax.ppermute(acts, "tok", swap)
        blocks = {0: acts}

        def arrived(hop, ahead, behind, state):
            blocks[hop], blocks[n - hop] = ahead, behind
            return acts_twin

        acts_twin, ahead, behind, far = ring.gather(acts, arrived)
        blocks[ring.hops], blocks[n - ring.hops], blocks[n // 2] = ahead, behind, far
        got = choose(by_slot, [blocks[i] for i in range(n)])
    else:
        acts = encode_gathered(residual, enc_weight, enc_bias, threshold)
        acts_twin = lax.ppermute(acts, "tok", swap)
        slices = lax.all_to_all(acts.reshape(n, tok_rows // n, width), "lat", 0, 0)
        outgoing = jnp.take(slices, jnp.minimum(partners[:, 1:], n - 1), axis=0)
        got = lax.all_to_all(outgoing, "lat", 0, 0)
        got = got.transpose(1, 0, 2, 3).reshape(slots - 1, tok_rows, width)
    got_twin = lax.ppermute(got, "tok", swap)
    return gram(by_slot, acts, acts_twin, got, got_twin, tok_scale, halves, n)


def solution(mesh):
    return jax.shard_map(
        body,
        mesh=mesh,
        in_specs=(P(("parts", "tok"), "lat"), P(None, "lat"), P("lat"), P("lat"), P()),
        out_specs=P(("parts", "lat"), None, "tok", None),
        check_vma=False,
    )
```

```python
import functools

import jax
import jax.numpy as jnp
from jax import lax
from jax.experimental import pallas as pl
from jax.experimental.pallas import tpu as pltpu
from jax.sharding import PartitionSpec as P

ramp_width = 0.25
ring_size = 8

in_vmem = pl.BlockSpec(memory_space=pltpu.VMEM)
in_smem = pl.BlockSpec(memory_space=pltpu.SMEM)
in_hbm = pl.BlockSpec(memory_space=pltpu.HBM)
params = pltpu.CompilerParams(vmem_limit_bytes=24 * 1024 * 1024)

rows_by_rows = (((0,), (0,)), ((), ()))


def place_on_ring(block, n):
    half = block // 2
    return half + (block % 2) * (n - 1 - 2 * half)


def block_at(place, n):
    up = 2 * place
    if isinstance(place, int):
        return up if place < n // 2 else 2 * n - 1 - up
    return jnp.where(place < n // 2, up, 2 * n - 1 - up)


def origin(hop, n):
    me = place_on_ring(lax.axis_index("lat"), n)
    return block_at(lax.rem(me + n - hop, n), n)


def activate(pre_acts, threshold):
    gate = jnp.clip((pre_acts - threshold) / ramp_width + 0.5, 0.0, 1.0)
    return (pre_acts * gate).astype(jnp.bfloat16)


def project(x, w):
    return lax.dot_general(x, w, rows_by_rows, preferred_element_type=jnp.float32)


def first_step(x_f, x_b, weights, total):
    n = weights.shape[0]
    total[...] = project(x_f[...], weights[origin(1, n)]) + project(x_b[...], weights[origin(-1, n)])


def middle_step(hops, x, x_f, x_b, before, weights, total):
    n = weights.shape[0]
    total[...] = before[...]
    for hop, arrived in zip(hops, (x_f, x_b, x)):
        total[...] += project(arrived[...], weights[origin(hop, n)])


def last_step(hops, x_f, x_b, x_far, before, weights, bias, threshold, acts):
    n = weights.shape[0]
    pre_acts = before[...] + bias[...]
    for hop, arrived in zip(hops, (x_f, x_b, x_far)):
        pre_acts = pre_acts + project(arrived[...], weights[origin(hop, n)])
    acts[...] = activate(pre_acts, threshold[...])


def cost(rows, depth, width, blocks):
    return pl.CostEstimate(
        flops=2 * rows * depth * width * blocks,
        bytes_accessed=2 * depth * (rows + width) * blocks + 8 * rows * width,
        transcendentals=0,
    )


class Ring:
    def __init__(self, n):
        walk = [block_at(i, n) for i in range(n)]
        self.n = n
        self.hops = n // 2 - 1
        self.forward = [(walk[i], walk[(i + 1) % n]) for i in range(n)]
        self.backward = [(d, s) for s, d in self.forward]
        mates = {i: (i + 4) % n if i % 4 in (0, 3) else n - 1 - i for i in range(n)}
        self.across = [(walk[i], walk[mates[i]]) for i in range(n)]

    def to_cross(self, x, ahead, behind):
        place = place_on_ring(lax.axis_index("lat"), self.n) % 4
        return jnp.where(place == 1, behind, jnp.where(place == 2, ahead, x))

    def gather(self, x, arrived):
        ahead = lax.ppermute(x, "lat", self.forward)
        behind = lax.ppermute(x, "lat", self.backward)
        state = None
        for hop in range(1, self.hops):
            now_ahead, now_behind = ahead, behind
            ahead = lax.ppermute(ahead, "lat", self.forward)
            behind = lax.ppermute(behind, "lat", self.backward)
            if hop == 1:
                cross = self.to_cross(x, now_ahead, now_behind)
                far = lax.ppermute(cross, "lat", self.across)
            state = arrived(hop, now_ahead, now_behind, state)
            if hop + 1 < self.hops:
                state, ahead, behind = lax.optimization_barrier((state, ahead, behind))
        return state, ahead, behind, far


def encode_on_ring(residual, enc_weight, enc_bias, threshold, ring):
    tok_rows, depth = residual.shape
    width = enc_weight.shape[1]
    n = ring.n
    x = residual.T
    weights = enc_weight.reshape(n, depth, width)
    total_shape = jax.ShapeDtypeStruct((tok_rows, width), jnp.float32)

    def arrived(hop, ahead, behind, total):
        if hop == 1:
            kernel, operands = first_step, (ahead, behind, weights)
        elif hop == 2:
            kernel = functools.partial(middle_step, (2, -2, 0))
            operands = (x, ahead, behind, total, weights)
        else:
            kernel = functools.partial(middle_step, (hop, -hop))
            operands = (x, ahead, behind, total, weights)
        return pl.pallas_call(
            kernel,
            out_shape=total_shape,
            in_specs=[in_vmem] * len(operands),
            out_specs=in_vmem,
            compiler_params=params,
            cost_estimate=cost(tok_rows, depth, width, 3),
        )(*operands)

    total, ahead, behind, far = ring.gather(x, arrived)
    return pl.pallas_call(
        functools.partial(last_step, (ring.hops, -ring.hops, n // 2)),
        out_shape=jax.ShapeDtypeStruct((tok_rows, width), jnp.bfloat16),
        in_specs=[in_vmem] * 7,
        out_specs=in_vmem,
        compiler_params=params,
        cost_estimate=cost(tok_rows, depth, width, 3),
    )(
        ahead,
        behind,
        far,
        total,
        weights,
        enc_bias.reshape(1, width),
        threshold.reshape(1, width),
    )


def encode_gathered(residual, enc_weight, enc_bias, threshold):
    pre_acts = (
        jnp.dot(
            lax.all_gather(residual, "lat", axis=1, tiled=True),
            enc_weight,
            preferred_element_type=jnp.float32,
        )
        + enc_bias
    )
    return activate(pre_acts, threshold)


def choose_kernel(partners, *refs):
    blocks, chosen = refs[:-1], refs[-1]
    n = len(blocks)
    me = lax.axis_index("lat")
    for k in range(chosen.shape[0]):
        listed = partners[k + 1, me]
        hop = lax.rem(place_on_ring(me, n) + n - place_on_ring(jnp.minimum(listed, n - 1), n), n)
        for i, block in enumerate(blocks):

            @pl.when(hop == i)
            def _():
                chosen[k] = block[...]


def choose(partners, blocks):
    return pl.pallas_call(
        choose_kernel,
        out_shape=jax.ShapeDtypeStruct((partners.shape[0] - 1,) + blocks[0].shape, blocks[0].dtype),
        in_specs=[in_smem] + [in_vmem] * len(blocks),
        out_specs=in_vmem,
        compiler_params=params,
    )(partners, *blocks)


def gram_kernel(tok_scale, n, partners, own, own_twin, got, got_twin, out, tiles, sems):
    slots, rows, width = tiles.shape
    me = lax.axis_index("lat")
    columns = pl.ds(pl.multiple_of(lax.axis_index("tok") * rows, rows), rows)
    left = jnp.concatenate([own[:, columns], own_twin[:, columns]], axis=0)

    def tile_of(right, right_twin):
        tile = project(left, jnp.concatenate([right, right_twin], axis=0))
        return (tile * tok_scale).astype(tiles.dtype)

    copies = [pltpu.make_async_copy(tiles.at[k], out.at[0, k], sems.at[k]) for k in range(slots)]
    tiles[0] = tile_of(own[...], own_twin[...])
    copies[0].start()
    for k in range(1, slots):
        live = partners[k, me] < n

        @pl.when(live)
        def _():
            tiles[k] = tile_of(got[k - 1], got_twin[k - 1])

        @pl.when(jnp.logical_not(live))
        def _():
            tiles[k] = jnp.zeros((rows, width), tiles.dtype)

        copies[k].start()
    for copy in copies:
        copy.wait()


def gram(partners, own, own_twin, got, got_twin, tok_scale, halves, n):
    tok_rows, width = own.shape
    slots = partners.shape[0]
    rows = width // halves
    return pl.pallas_call(
        functools.partial(gram_kernel, tok_scale, n),
        out_shape=jax.ShapeDtypeStruct((1, slots, rows, width), own.dtype),
        in_specs=[in_smem] + [in_vmem] * 4,
        out_specs=in_hbm,
        scratch_shapes=[
            pltpu.VMEM((slots, rows, width), own.dtype),
            pltpu.SemaphoreType.DMA((slots,)),
        ],
        compiler_params=params,
    )(partners, own, own_twin, got, got_twin)


def body(residual, enc_weight, enc_bias, threshold, partners):
    n = lax.axis_size("lat")
    halves = lax.axis_size("tok")
    tok_rows = residual.shape[0]
    width = enc_weight.shape[1]
    slots = partners.shape[1]
    tok_scale = 1.0 / (tok_rows * halves)
    swap = [(i, 1 - i) for i in range(2)]
    by_slot = partners.T
    if n == ring_size:
        ring = Ring(n)
        acts = encode_on_ring(residual, enc_weight, enc_bias, threshold, ring)
        acts_twin = lax.ppermute(acts, "tok", swap)
        blocks = {0: acts}

        def arrived(hop, ahead, behind, state):
            blocks[hop], blocks[n - hop] = ahead, behind
            return acts_twin

        acts_twin, ahead, behind, far = ring.gather(acts, arrived)
        blocks[ring.hops], blocks[n - ring.hops], blocks[n // 2] = ahead, behind, far
        got = choose(by_slot, [blocks[i] for i in range(n)])
    else:
        acts = encode_gathered(residual, enc_weight, enc_bias, threshold)
        acts_twin = lax.ppermute(acts, "tok", swap)
        slices = lax.all_to_all(acts.reshape(n, tok_rows // n, width), "lat", 0, 0)
        outgoing = jnp.take(slices, jnp.minimum(partners[:, 1:], n - 1), axis=0)
        got = lax.all_to_all(outgoing, "lat", 0, 0)
        got = got.transpose(1, 0, 2, 3).reshape(slots - 1, tok_rows, width)
    got_twin = lax.ppermute(got, "tok", swap)
    return gram(by_slot, acts, acts_twin, got, got_twin, tok_scale, halves, n)


def solution(mesh):
    return jax.shard_map(
        body,
        mesh=mesh,
        in_specs=(P(("parts", "tok"), "lat"), P(None, "lat"), P("lat"), P("lat"), P()),
        out_specs=P(("parts", "lat"), None, "tok", None),
        check_vma=False,
    )
```

```python
import functools

import jax
import jax.numpy as jnp
from jax import lax
from jax.experimental import pallas as pl
from jax.experimental.pallas import tpu as pltpu
from jax.sharding import PartitionSpec as P

ramp_width = 0.25
ring_size = 8

in_vmem = pl.BlockSpec(memory_space=pltpu.VMEM)
in_smem = pl.BlockSpec(memory_space=pltpu.SMEM)
in_hbm = pl.BlockSpec(memory_space=pltpu.HBM)
params = pltpu.CompilerParams(vmem_limit_bytes=24 * 1024 * 1024)

rows_by_rows = (((0,), (0,)), ((), ()))


def place_on_ring(block, n):
    half = block // 2
    return half + (block % 2) * (n - 1 - 2 * half)


def block_at(place, n):
    up = 2 * place
    if isinstance(place, int):
        return up if place < n // 2 else 2 * n - 1 - up
    return jnp.where(place < n // 2, up, 2 * n - 1 - up)


def origin(hop, n):
    me = place_on_ring(lax.axis_index("lat"), n)
    return block_at(lax.rem(me + n - hop, n), n)


def activate(pre_acts, threshold):
    gate = jnp.clip((pre_acts - threshold) / ramp_width + 0.5, 0.0, 1.0)
    return (pre_acts * gate).astype(jnp.bfloat16)


def project(x, w):
    return lax.dot_general(x, w, rows_by_rows, preferred_element_type=jnp.float32)


def on_corner(n):
    return place_on_ring(lax.axis_index("lat"), n) % (n // 2) % (n // 2 - 1) == 0


def first_step(hops, *refs):
    xs, weights, total = refs[:-2], refs[-2], refs[-1]
    n = weights.shape[0]
    total[...] = project(xs[0][...], weights[origin(hops[0], n)])
    for hop, x in zip(hops[1:], xs[1:]):
        total[...] += project(x[...], weights[origin(hop, n)])


def last_step(x, x_f, x_b, x_corner, x_middle, before, weights, bias, threshold, acts):
    n = weights.shape[0]
    hops = n // 2 - 1
    x_far = jnp.where(on_corner(n), x_corner[...], x_middle[...])
    pre_acts = before[...] + bias[...]
    for hop, part in ((0, x[...]), (hops, x_f[...]), (-hops, x_b[...]), (n // 2, x_far)):
        pre_acts = pre_acts + project(part, weights[origin(hop, n)])
    acts[...] = activate(pre_acts, threshold[...])


def cost(rows, depth, width, blocks):
    return pl.CostEstimate(
        flops=2 * rows * depth * width * blocks,
        bytes_accessed=2 * depth * (rows + width) * blocks + 8 * rows * width,
        transcendentals=0,
    )


class Ring:
    def __init__(self, n):
        walk = [block_at(i, n) for i in range(n)]
        self.n = n
        self.forward = [(walk[i], walk[(i + 1) % n]) for i in range(n)]
        self.backward = [(d, s) for s, d in self.forward]
        beside = [(i, n - 1 - i) for i in range(n) if i % 4 in (1, 2)]
        across = [(i, (i + 4) % n) for i in range(n) if i % 4 in (0, 3)]
        self.beside = [(walk[i], walk[j]) for i, j in beside]
        self.across = [(walk[i], walk[j]) for i, j in across + beside]

    def gather(self, x, beside_last):
        ahead = lax.ppermute(x, "lat", self.forward)
        behind = lax.ppermute(x, "lat", self.backward)
        corner = lax.ppermute(x, "lat", self.across)
        ahead_2 = lax.ppermute(ahead, "lat", self.forward)
        behind_2 = lax.ppermute(behind, "lat", self.backward)
        odd = place_on_ring(lax.axis_index("lat"), self.n) % 2 == 1
        middle = lax.ppermute(jnp.where(odd, behind, ahead), "lat", self.beside)
        ahead_2, behind_2, corner = lax.optimization_barrier((ahead_2, behind_2, corner))
        ahead_3 = lax.ppermute(ahead_2, "lat", self.forward)
        behind_3 = lax.ppermute(behind_2, "lat", self.backward)
        done = beside_last(x, ahead, behind, ahead_2, behind_2)
        return done, ahead_3, behind_3, corner, middle


def encode_on_ring(residual, enc_weight, enc_bias, threshold, ring):
    tok_rows, depth = residual.shape
    width = enc_weight.shape[1]
    n = ring.n
    weights = enc_weight.reshape(n, depth, width)

    def beside_last(_, *blocks):
        return pl.pallas_call(
            functools.partial(first_step, (1, -1, 2, -2)),
            out_shape=jax.ShapeDtypeStruct((tok_rows, width), jnp.float32),
            in_specs=[in_vmem] * (len(blocks) + 1),
            out_specs=in_vmem,
            compiler_params=params,
            cost_estimate=cost(tok_rows, depth, width, 4),
        )(*blocks, weights)

    x = residual.T
    total, ahead, behind, corner, middle = ring.gather(x, beside_last)
    return pl.pallas_call(
        last_step,
        out_shape=jax.ShapeDtypeStruct((tok_rows, width), jnp.bfloat16),
        in_specs=[in_vmem] * 9,
        out_specs=in_vmem,
        compiler_params=params,
        cost_estimate=cost(tok_rows, depth, width, 4),
    )(
        x,
        ahead,
        behind,
        corner,
        middle,
        total,
        weights,
        enc_bias.reshape(1, width),
        threshold.reshape(1, width),
    )


def encode_gathered(residual, enc_weight, enc_bias, threshold):
    pre_acts = (
        jnp.dot(
            lax.all_gather(residual, "lat", axis=1, tiled=True),
            enc_weight,
            preferred_element_type=jnp.float32,
        )
        + enc_bias
    )
    return activate(pre_acts, threshold)


def choose_kernel(hops, partners, *refs):
    blocks, chosen = refs[:-1], refs[-1]
    n = ring_size
    me = lax.axis_index("lat")
    corner = on_corner(n)
    for k in range(chosen.shape[0]):
        listed = jnp.minimum(partners[k + 1, me], n - 1)
        hop = lax.rem(place_on_ring(me, n) + n - place_on_ring(listed, n), n)
        hop = jnp.where((hop == n // 2) & jnp.logical_not(corner), n, hop)
        for i, block in zip(hops, blocks):

            @pl.when(hop == i)
            def _():
                chosen[k] = block[...]


def choose(partners, hops, blocks):
    return pl.pallas_call(
        functools.partial(choose_kernel, hops),
        out_shape=jax.ShapeDtypeStruct((partners.shape[0] - 1,) + blocks[0].shape, blocks[0].dtype),
        in_specs=[in_smem] + [in_vmem] * len(blocks),
        out_specs=in_vmem,
        compiler_params=params,
    )(partners, *blocks)


def gram_kernel(tok_scale, n, partners, own, own_twin, got, got_twin, out, tiles, sems):
    slots, rows, width = tiles.shape
    me = lax.axis_index("lat")
    columns = pl.ds(pl.multiple_of(lax.axis_index("tok") * rows, rows), rows)
    left = jnp.concatenate([own[:, columns], own_twin[:, columns]], axis=0)

    def tile_of(right, right_twin):
        tile = project(left, jnp.concatenate([right, right_twin], axis=0))
        return (tile * tok_scale).astype(tiles.dtype)

    copies = [pltpu.make_async_copy(tiles.at[k], out.at[0, k], sems.at[k]) for k in range(slots)]
    tiles[0] = tile_of(own[...], own_twin[...])
    copies[0].start()
    for k in range(1, slots):
        live = partners[k, me] < n

        @pl.when(live)
        def _():
            tiles[k] = tile_of(got[k - 1], got_twin[k - 1])

        @pl.when(jnp.logical_not(live))
        def _():
            tiles[k] = jnp.zeros((rows, width), tiles.dtype)

        copies[k].start()
    for copy in copies:
        copy.wait()


def gram(partners, own, own_twin, got, got_twin, tok_scale, halves, n):
    tok_rows, width = own.shape
    slots = partners.shape[0]
    rows = width // halves
    return pl.pallas_call(
        functools.partial(gram_kernel, tok_scale, n),
        out_shape=jax.ShapeDtypeStruct((1, slots, rows, width), own.dtype),
        in_specs=[in_smem] + [in_vmem] * 4,
        out_specs=in_hbm,
        scratch_shapes=[
            pltpu.VMEM((slots, rows, width), own.dtype),
            pltpu.SemaphoreType.DMA((slots,)),
        ],
        compiler_params=params,
    )(partners, own, own_twin, got, got_twin)


def body(residual, enc_weight, enc_bias, threshold, partners):
    n = lax.axis_size("lat")
    halves = lax.axis_size("tok")
    tok_rows = residual.shape[0]
    width = enc_weight.shape[1]
    slots = partners.shape[1]
    tok_scale = 1.0 / (tok_rows * halves)
    swap = [(i, 1 - i) for i in range(2)]
    by_slot = partners.T
    if n == ring_size:
        ring = Ring(n)
        acts = encode_on_ring(residual, enc_weight, enc_bias, threshold, ring)
        acts_twin = lax.ppermute(acts, "tok", swap)
        early, *late = ring.gather(acts, lambda *blocks: blocks)
        got = choose(by_slot, (0, 1, n - 1, 2, n - 2, 3, n - 3, 4, n), [*early, *late])
    else:
        acts = encode_gathered(residual, enc_weight, enc_bias, threshold)
        acts_twin = lax.ppermute(acts, "tok", swap)
        slices = lax.all_to_all(acts.reshape(n, tok_rows // n, width), "lat", 0, 0)
        outgoing = jnp.take(slices, jnp.minimum(partners[:, 1:], n - 1), axis=0)
        got = lax.all_to_all(outgoing, "lat", 0, 0)
        got = got.transpose(1, 0, 2, 3).reshape(slots - 1, tok_rows, width)
    got_twin = lax.ppermute(got, "tok", swap)
    return gram(by_slot, acts, acts_twin, got, got_twin, tok_scale, halves, n)


def solution(mesh):
    return jax.shard_map(
        body,
        mesh=mesh,
        in_specs=(P(("parts", "tok"), "lat"), P(None, "lat"), P("lat"), P("lat"), P()),
        out_specs=P(("parts", "lat"), None, "tok", None),
        check_vma=False,
    )
```

```python
import functools

import jax
import jax.numpy as jnp
from jax import lax
from jax.experimental import pallas as pl
from jax.experimental.pallas import tpu as pltpu
from jax.sharding import PartitionSpec as P

ramp_width = 0.25
ring_size = 8

in_vmem = pl.BlockSpec(memory_space=pltpu.VMEM)
in_smem = pl.BlockSpec(memory_space=pltpu.SMEM)
in_hbm = pl.BlockSpec(memory_space=pltpu.HBM)
params = pltpu.CompilerParams(vmem_limit_bytes=24 * 1024 * 1024)

rows_by_rows = (((0,), (0,)), ((), ()))


def place_on_ring(block, n):
    half = block // 2
    return half + (block % 2) * (n - 1 - 2 * half)


def block_at(place, n):
    up = 2 * place
    if isinstance(place, int):
        return up if place < n // 2 else 2 * n - 1 - up
    return jnp.where(place < n // 2, up, 2 * n - 1 - up)


def origin(hop, n):
    me = place_on_ring(lax.axis_index("lat"), n)
    return block_at(lax.rem(me + n - hop, n), n)


def activate(pre_acts, threshold):
    gate = jnp.clip((pre_acts - threshold) / ramp_width + 0.5, 0.0, 1.0)
    return (pre_acts * gate).astype(jnp.bfloat16)


def project(x, w):
    return lax.dot_general(x, w, rows_by_rows, preferred_element_type=jnp.float32)


def on_corner(n):
    return place_on_ring(lax.axis_index("lat"), n) % (n // 2) % (n // 2 - 1) == 0


def first_step(hops, *refs):
    xs, weights, total = refs[:-2], refs[-2], refs[-1]
    n = weights.shape[0]
    total[...] = project(xs[0][...], weights[origin(hops[0], n)])
    for hop, x in zip(hops[1:], xs[1:]):
        total[...] += project(x[...], weights[origin(hop, n)])


def last_step(x, x_f, x_b, x_corner, x_middle, before, weights, bias, threshold, acts):
    n = weights.shape[0]
    hops = n // 2 - 1
    x_far = jnp.where(on_corner(n), x_corner[...], x_middle[...])
    pre_acts = before[...] + bias[...]
    for hop, part in ((0, x[...]), (hops, x_f[...]), (-hops, x_b[...]), (n // 2, x_far)):
        pre_acts = pre_acts + project(part, weights[origin(hop, n)])
    acts[...] = activate(pre_acts, threshold[...])


def cost(rows, depth, width, blocks):
    return pl.CostEstimate(
        flops=2 * rows * depth * width * blocks,
        bytes_accessed=2 * depth * (rows + width) * blocks + 8 * rows * width,
        transcendentals=0,
    )


class Ring:
    def __init__(self, n):
        walk = [block_at(i, n) for i in range(n)]
        self.n = n
        self.forward = [(walk[i], walk[(i + 1) % n]) for i in range(n)]
        self.backward = [(d, s) for s, d in self.forward]
        beside = [(i, n - 1 - i) for i in range(n) if i % 4 in (1, 2)]
        across = [(i, (i + 4) % n) for i in range(n) if i % 4 in (0, 3)]
        self.beside = [(walk[i], walk[j]) for i, j in beside]
        self.across = [(walk[i], walk[j]) for i, j in across + beside]

    def gather(self, x, beside_second=None, beside_third=None):
        ahead = lax.ppermute(x, "lat", self.forward)
        behind = lax.ppermute(x, "lat", self.backward)
        corner = lax.ppermute(x, "lat", self.across)
        ahead_2 = lax.ppermute(ahead, "lat", self.forward)
        behind_2 = lax.ppermute(behind, "lat", self.backward)
        odd = place_on_ring(lax.axis_index("lat"), self.n) % 2 == 1
        middle = lax.ppermute(jnp.where(odd, behind, ahead), "lat", self.beside)
        done = beside_second(ahead, behind) if beside_second else ()
        ahead_2, behind_2, corner, done = lax.optimization_barrier(
            (ahead_2, behind_2, corner, done)
        )
        ahead_3 = lax.ppermute(ahead_2, "lat", self.forward)
        behind_3 = lax.ppermute(behind_2, "lat", self.backward)
        done = beside_third(ahead, behind, ahead_2, behind_2, corner, done)
        return done, ahead_3, behind_3, corner, middle


def encode_on_ring(residual, enc_weight, enc_bias, threshold, ring):
    tok_rows, depth = residual.shape
    width = enc_weight.shape[1]
    n = ring.n
    weights = enc_weight.reshape(n, depth, width)

    def beside_third(*blocks):
        blocks = blocks[:4]
        return pl.pallas_call(
            functools.partial(first_step, (1, -1, 2, -2)),
            out_shape=jax.ShapeDtypeStruct((tok_rows, width), jnp.float32),
            in_specs=[in_vmem] * (len(blocks) + 1),
            out_specs=in_vmem,
            compiler_params=params,
            cost_estimate=cost(tok_rows, depth, width, 4),
        )(*blocks, weights)

    x = residual.T
    total, ahead, behind, corner, middle = ring.gather(x, beside_third=beside_third)
    return pl.pallas_call(
        last_step,
        out_shape=jax.ShapeDtypeStruct((tok_rows, width), jnp.bfloat16),
        in_specs=[in_vmem] * 9,
        out_specs=in_vmem,
        compiler_params=params,
        cost_estimate=cost(tok_rows, depth, width, 4),
    )(
        x,
        ahead,
        behind,
        corner,
        middle,
        total,
        weights,
        enc_bias.reshape(1, width),
        threshold.reshape(1, width),
    )


def encode_gathered(residual, enc_weight, enc_bias, threshold):
    pre_acts = (
        jnp.dot(
            lax.all_gather(residual, "lat", axis=1, tiled=True),
            enc_weight,
            preferred_element_type=jnp.float32,
        )
        + enc_bias
    )
    return activate(pre_acts, threshold)


def gram_kernel(tok_scale, n, partners, own, own_twin, got, got_twin, out, tiles, sems):
    slots, rows, width = tiles.shape
    me = lax.axis_index("lat")
    columns = pl.ds(pl.multiple_of(lax.axis_index("tok") * rows, rows), rows)
    left = jnp.concatenate([own[:, columns], own_twin[:, columns]], axis=0)

    def tile_of(right, right_twin):
        tile = project(left, jnp.concatenate([right, right_twin], axis=0))
        return (tile * tok_scale).astype(tiles.dtype)

    copies = [pltpu.make_async_copy(tiles.at[k], out.at[0, k], sems.at[k]) for k in range(slots)]
    tiles[0] = tile_of(own[...], own_twin[...])
    copies[0].start()
    for k in range(1, slots):
        live = partners[k, me] < n

        @pl.when(live)
        def _():
            tiles[k] = tile_of(got[k - 1], got_twin[k - 1])

        @pl.when(jnp.logical_not(live))
        def _():
            tiles[k] = jnp.zeros((rows, width), tiles.dtype)

        copies[k].start()
    for copy in copies:
        copy.wait()


def gram(partners, own, own_twin, got, got_twin, tok_scale, halves, n):
    tok_rows, width = own.shape
    slots = partners.shape[0]
    rows = width // halves
    return pl.pallas_call(
        functools.partial(gram_kernel, tok_scale, n),
        out_shape=jax.ShapeDtypeStruct((1, slots, rows, width), own.dtype),
        in_specs=[in_smem] + [in_vmem] * 4,
        out_specs=in_hbm,
        scratch_shapes=[
            pltpu.VMEM((slots, rows, width), own.dtype),
            pltpu.SemaphoreType.DMA((slots,)),
        ],
        compiler_params=params,
    )(partners, own, own_twin, got, got_twin)


def hop_of_slot(partners, k, n):
    me = lax.axis_index("lat")
    listed = partners[k, me]
    hop = lax.rem(place_on_ring(me, n) + n - place_on_ring(jnp.minimum(listed, n - 1), n), n)
    hop = jnp.where((hop == n // 2) & jnp.logical_not(on_corner(n)), n, hop)
    return jnp.where(listed < n, hop, -1)


def tiles_kernel(tok_scale, n, hops, is_first, partners, own, own_twin, *refs):
    count = len(hops)
    blocks, twins = refs[:count], refs[count : 2 * count]
    out, tiles, sems = refs[-3:]
    rows, width = tiles.shape[1:]
    slots = partners.shape[0]
    columns = pl.ds(pl.multiple_of(lax.axis_index("tok") * rows, rows), rows)
    left = jnp.concatenate([own[:, columns], own_twin[:, columns]], axis=0)

    def tile_of(right, right_twin):
        tile = project(left, jnp.concatenate([right[...], right_twin[...]], axis=0))
        return (tile * tok_scale).astype(tiles.dtype)

    slot_hops = [hop_of_slot(partners, k, n) for k in range(1, slots)]
    copies = []

    def send(place, slot, when, value):
        copy = pltpu.make_async_copy(tiles.at[place], out.at[0, slot], sems.at[len(copies)])
        copies.append((copy, when))

        @pl.when(when)
        def _():
            if value is not None:
                tiles[place] = value()
            copy.start()

    if is_first:
        always = lax.axis_index("lat") >= 0
        send(count, 0, always, lambda: tile_of(own, own_twin))
        tiles[count + 1] = jnp.zeros((rows, width), tiles.dtype)
        for k, hop in enumerate(slot_hops):
            send(count + 1, k + 1, hop < 0, None)
    for j, hop in enumerate(hops):
        slot = jnp.int32(0)
        for k, h in enumerate(slot_hops):
            slot = jnp.where(h == hop, jnp.int32(k + 1), slot)
        send(j, slot, slot > 0, functools.partial(tile_of, blocks[j], twins[j]))
    for copy, when in copies:
        pl.when(when)(copy.wait)


def tiles_of(partners, own, own_twin, hops, blocks, twins, before, tok_scale, halves, n):
    width = own.shape[1]
    slots = partners.shape[0]
    rows = width // halves
    first = before is None
    operands = (partners, own, own_twin, *blocks, *twins) + (() if first else (before,))
    specs = [in_smem] + [in_vmem] * (2 + 2 * len(hops)) + ([] if first else [in_hbm])
    return pl.pallas_call(
        functools.partial(tiles_kernel, tok_scale, n, hops, first),
        out_shape=jax.ShapeDtypeStruct((1, slots, rows, width), own.dtype),
        in_specs=specs,
        out_specs=in_hbm,
        input_output_aliases={} if first else {len(operands) - 1: 0},
        scratch_shapes=[
            pltpu.VMEM((len(hops) + (2 if first else 0), rows, width), own.dtype),
            pltpu.SemaphoreType.DMA((len(hops) + (slots if first else 0),)),
        ],
        compiler_params=params,
        cost_estimate=pl.CostEstimate(
            flops=4 * rows * width * own.shape[0] * len(hops),
            bytes_accessed=4 * rows * width * len(hops),
            transcendentals=0,
        ),
    )(*operands)


def body(residual, enc_weight, enc_bias, threshold, partners):
    n = lax.axis_size("lat")
    halves = lax.axis_size("tok")
    tok_rows = residual.shape[0]
    width = enc_weight.shape[1]
    slots = partners.shape[1]
    tok_scale = 1.0 / (tok_rows * halves)
    swap = [(i, 1 - i) for i in range(2)]
    by_slot = partners.T
    if n == ring_size:
        ring = Ring(n)
        acts = encode_on_ring(residual, enc_weight, enc_bias, threshold, ring)
        acts_twin = lax.ppermute(acts, "tok", swap)

        def add_tiles(before, hops, blocks):
            twins = [lax.ppermute(block, "tok", swap) for block in blocks]
            return tiles_of(
                by_slot, acts, acts_twin, hops, blocks, twins, before, tok_scale, halves, n
            )

        def beside_second(ahead, behind):
            return add_tiles(None, (1, n - 1), (ahead, behind))

        def beside_third(ahead, behind, ahead_2, behind_2, corner, before):
            return add_tiles(before, (2, n - 2, n // 2), (ahead_2, behind_2, corner))

        out, ahead, behind, _, middle = ring.gather(acts, beside_second, beside_third)
        return add_tiles(out, (3, n - 3, n), (ahead, behind, middle))
    acts = encode_gathered(residual, enc_weight, enc_bias, threshold)
    acts_twin = lax.ppermute(acts, "tok", swap)
    slices = lax.all_to_all(acts.reshape(n, tok_rows // n, width), "lat", 0, 0)
    outgoing = jnp.take(slices, jnp.minimum(partners[:, 1:], n - 1), axis=0)
    got = lax.all_to_all(outgoing, "lat", 0, 0)
    got = got.transpose(1, 0, 2, 3).reshape(slots - 1, tok_rows, width)
    got_twin = lax.ppermute(got, "tok", swap)
    return gram(by_slot, acts, acts_twin, got, got_twin, tok_scale, halves, n)


def solution(mesh):
    return jax.shard_map(
        body,
        mesh=mesh,
        in_specs=(P(("parts", "tok"), "lat"), P(None, "lat"), P("lat"), P("lat"), P()),
        out_specs=P(("parts", "lat"), None, "tok", None),
        check_vma=False,
    )
```

```python
import functools

import jax
import jax.numpy as jnp
from jax import lax
from jax.experimental import pallas as pl
from jax.experimental.pallas import tpu as pltpu
from jax.sharding import PartitionSpec as P

ramp_width = 0.25
ring_size = 8

in_vmem = pl.BlockSpec(memory_space=pltpu.VMEM)
in_smem = pl.BlockSpec(memory_space=pltpu.SMEM)
in_hbm = pl.BlockSpec(memory_space=pltpu.HBM)
params = pltpu.CompilerParams(vmem_limit_bytes=24 * 1024 * 1024)

rows_by_rows = (((0,), (0,)), ((), ()))


def place_on_ring(block, n):
    half = block // 2
    return half + (block % 2) * (n - 1 - 2 * half)


def block_at(place, n):
    up = 2 * place
    if isinstance(place, int):
        return up if place < n // 2 else 2 * n - 1 - up
    return jnp.where(place < n // 2, up, 2 * n - 1 - up)


def origin(hop, n):
    me = place_on_ring(lax.axis_index("lat"), n)
    return block_at(lax.rem(me + n - hop, n), n)


def activate(pre_acts, threshold):
    gate = jnp.clip((pre_acts - threshold) / ramp_width + 0.5, 0.0, 1.0)
    return (pre_acts * gate).astype(jnp.bfloat16)


def project(x, w):
    return lax.dot_general(x, w, rows_by_rows, preferred_element_type=jnp.float32)


def first_step(hops, *refs):
    xs, weights, total = refs[:-2], refs[-2], refs[-1]
    n = weights.shape[0]
    total[...] = project(xs[0][...], weights[origin(hops[0], n)])
    for hop, x in zip(hops[1:], xs[1:]):
        total[...] += project(x[...], weights[origin(hop, n)])


def last_step(x, x_f, x_b, x_far, before, weights, bias, threshold, acts):
    n = weights.shape[0]
    hops = n // 2 - 1
    pre_acts = before[...] + bias[...]
    for hop, part in ((0, x), (hops, x_f), (-hops, x_b), (n // 2, x_far)):
        pre_acts = pre_acts + project(part[...], weights[origin(hop, n)])
    acts[...] = activate(pre_acts, threshold[...])


def cost(rows, depth, width, blocks):
    return pl.CostEstimate(
        flops=2 * rows * depth * width * blocks,
        bytes_accessed=2 * depth * (rows + width) * blocks + 8 * rows * width,
        transcendentals=0,
    )


class Ring:
    def __init__(self, n):
        walk = [block_at(i, n) for i in range(n)]
        self.n = n
        self.forward = [(walk[i], walk[(i + 1) % n]) for i in range(n)]
        self.backward = [(d, s) for s, d in self.forward]
        self.aslant = [(walk[i], walk[(i + (-2 if i % 4 < 2 else 2)) % n]) for i in range(n)]

    def gather(self, x, beside_second=None, beside_third=None):
        ahead = lax.ppermute(x, "lat", self.forward)
        behind = lax.ppermute(x, "lat", self.backward)
        ahead_2 = lax.ppermute(ahead, "lat", self.forward)
        behind_2 = lax.ppermute(behind, "lat", self.backward)
        done = beside_second(ahead, behind) if beside_second else ()
        ahead_2, behind_2, done = lax.optimization_barrier((ahead_2, behind_2, done))
        ahead_3 = lax.ppermute(ahead_2, "lat", self.forward)
        behind_3 = lax.ppermute(behind_2, "lat", self.backward)
        low = place_on_ring(lax.axis_index("lat"), self.n) % 4 < 2
        far = lax.ppermute(jnp.where(low, behind_2, ahead_2), "lat", self.aslant)
        done = beside_third(ahead, behind, ahead_2, behind_2, done)
        return done, ahead_3, behind_3, far


def encode_on_ring(residual, enc_weight, enc_bias, threshold, ring):
    tok_rows, depth = residual.shape
    width = enc_weight.shape[1]
    n = ring.n
    weights = enc_weight.reshape(n, depth, width)

    def beside_third(*blocks):
        blocks = blocks[:4]
        return pl.pallas_call(
            functools.partial(first_step, (1, -1, 2, -2)),
            out_shape=jax.ShapeDtypeStruct((tok_rows, width), jnp.float32),
            in_specs=[in_vmem] * (len(blocks) + 1),
            out_specs=in_vmem,
            compiler_params=params,
            cost_estimate=cost(tok_rows, depth, width, 4),
        )(*blocks, weights)

    x = residual.T
    total, ahead, behind, far = ring.gather(x, beside_third=beside_third)
    return pl.pallas_call(
        last_step,
        out_shape=jax.ShapeDtypeStruct((tok_rows, width), jnp.bfloat16),
        in_specs=[in_vmem] * 8,
        out_specs=in_vmem,
        compiler_params=params,
        cost_estimate=cost(tok_rows, depth, width, 4),
    )(
        x,
        ahead,
        behind,
        far,
        total,
        weights,
        enc_bias.reshape(1, width),
        threshold.reshape(1, width),
    )


def encode_gathered(residual, enc_weight, enc_bias, threshold):
    pre_acts = (
        jnp.dot(
            lax.all_gather(residual, "lat", axis=1, tiled=True),
            enc_weight,
            preferred_element_type=jnp.float32,
        )
        + enc_bias
    )
    return activate(pre_acts, threshold)


def gram_kernel(tok_scale, n, partners, own, own_twin, got, got_twin, out, tiles, sems):
    slots, rows, width = tiles.shape
    me = lax.axis_index("lat")
    columns = pl.ds(pl.multiple_of(lax.axis_index("tok") * rows, rows), rows)
    left = jnp.concatenate([own[:, columns], own_twin[:, columns]], axis=0)

    def tile_of(right, right_twin):
        tile = project(left, jnp.concatenate([right, right_twin], axis=0))
        return (tile * tok_scale).astype(tiles.dtype)

    copies = [pltpu.make_async_copy(tiles.at[k], out.at[0, k], sems.at[k]) for k in range(slots)]
    tiles[0] = tile_of(own[...], own_twin[...])
    copies[0].start()
    for k in range(1, slots):
        live = partners[k, me] < n

        @pl.when(live)
        def _():
            tiles[k] = tile_of(got[k - 1], got_twin[k - 1])

        @pl.when(jnp.logical_not(live))
        def _():
            tiles[k] = jnp.zeros((rows, width), tiles.dtype)

        copies[k].start()
    for copy in copies:
        copy.wait()


def gram(partners, own, own_twin, got, got_twin, tok_scale, halves, n):
    tok_rows, width = own.shape
    slots = partners.shape[0]
    rows = width // halves
    return pl.pallas_call(
        functools.partial(gram_kernel, tok_scale, n),
        out_shape=jax.ShapeDtypeStruct((1, slots, rows, width), own.dtype),
        in_specs=[in_smem] + [in_vmem] * 4,
        out_specs=in_hbm,
        scratch_shapes=[
            pltpu.VMEM((slots, rows, width), own.dtype),
            pltpu.SemaphoreType.DMA((slots,)),
        ],
        compiler_params=params,
    )(partners, own, own_twin, got, got_twin)


def hop_of_slot(partners, k, n):
    me = lax.axis_index("lat")
    listed = partners[k, me]
    hop = lax.rem(place_on_ring(me, n) + n - place_on_ring(jnp.minimum(listed, n - 1), n), n)
    return jnp.where(listed < n, hop, -1)


def tiles_kernel(tok_scale, n, hops, is_first, partners, own, own_twin, *refs):
    count = len(hops)
    blocks, twins = refs[:count], refs[count : 2 * count]
    out, tiles, sems = refs[-3:]
    rows, width = tiles.shape[1:]
    slots = partners.shape[0]
    columns = pl.ds(pl.multiple_of(lax.axis_index("tok") * rows, rows), rows)
    left = jnp.concatenate([own[:, columns], own_twin[:, columns]], axis=0)

    def tile_of(right, right_twin):
        tile = project(left, jnp.concatenate([right[...], right_twin[...]], axis=0))
        return (tile * tok_scale).astype(tiles.dtype)

    slot_hops = [hop_of_slot(partners, k, n) for k in range(1, slots)]
    copies = []

    def send(place, slot, when, value):
        copy = pltpu.make_async_copy(tiles.at[place], out.at[0, slot], sems.at[len(copies)])
        copies.append((copy, when))

        @pl.when(when)
        def _():
            if value is not None:
                tiles[place] = value()
            copy.start()

    if is_first:
        always = lax.axis_index("lat") >= 0
        send(count, 0, always, lambda: tile_of(own, own_twin))
        tiles[count + 1] = jnp.zeros((rows, width), tiles.dtype)
        for k, hop in enumerate(slot_hops):
            send(count + 1, k + 1, hop < 0, None)
    for j, hop in enumerate(hops):
        slot = jnp.int32(0)
        for k, h in enumerate(slot_hops):
            slot = jnp.where(h == hop, jnp.int32(k + 1), slot)
        send(j, slot, slot > 0, functools.partial(tile_of, blocks[j], twins[j]))
    for copy, when in copies:
        pl.when(when)(copy.wait)


def tiles_of(partners, own, own_twin, hops, blocks, twins, before, tok_scale, halves, n):
    width = own.shape[1]
    slots = partners.shape[0]
    rows = width // halves
    first = before is None
    operands = (partners, own, own_twin, *blocks, *twins) + (() if first else (before,))
    specs = [in_smem] + [in_vmem] * (2 + 2 * len(hops)) + ([] if first else [in_hbm])
    return pl.pallas_call(
        functools.partial(tiles_kernel, tok_scale, n, hops, first),
        out_shape=jax.ShapeDtypeStruct((1, slots, rows, width), own.dtype),
        in_specs=specs,
        out_specs=in_hbm,
        input_output_aliases={} if first else {len(operands) - 1: 0},
        scratch_shapes=[
            pltpu.VMEM((len(hops) + (2 if first else 0), rows, width), own.dtype),
            pltpu.SemaphoreType.DMA((len(hops) + (slots if first else 0),)),
        ],
        compiler_params=params,
        cost_estimate=pl.CostEstimate(
            flops=4 * rows * width * own.shape[0] * len(hops),
            bytes_accessed=4 * rows * width * len(hops),
            transcendentals=0,
        ),
    )(*operands)


def body(residual, enc_weight, enc_bias, threshold, partners):
    n = lax.axis_size("lat")
    halves = lax.axis_size("tok")
    tok_rows = residual.shape[0]
    width = enc_weight.shape[1]
    slots = partners.shape[1]
    tok_scale = 1.0 / (tok_rows * halves)
    swap = [(i, 1 - i) for i in range(2)]
    by_slot = partners.T
    if n == ring_size:
        ring = Ring(n)
        acts = encode_on_ring(residual, enc_weight, enc_bias, threshold, ring)
        acts_twin = lax.ppermute(acts, "tok", swap)

        def add_tiles(before, hops, blocks):
            twins = [lax.ppermute(block, "tok", swap) for block in blocks]
            return tiles_of(
                by_slot, acts, acts_twin, hops, blocks, twins, before, tok_scale, halves, n
            )

        def beside_second(ahead, behind):
            return add_tiles(None, (1, n - 1), (ahead, behind))

        def beside_third(ahead, behind, ahead_2, behind_2, before):
            return add_tiles(before, (2, n - 2), (ahead_2, behind_2))

        out, ahead, behind, far = ring.gather(acts, beside_second, beside_third)
        return add_tiles(out, (3, n - 3, n // 2), (ahead, behind, far))
    acts = encode_gathered(residual, enc_weight, enc_bias, threshold)
    acts_twin = lax.ppermute(acts, "tok", swap)
    slices = lax.all_to_all(acts.reshape(n, tok_rows // n, width), "lat", 0, 0)
    outgoing = jnp.take(slices, jnp.minimum(partners[:, 1:], n - 1), axis=0)
    got = lax.all_to_all(outgoing, "lat", 0, 0)
    got = got.transpose(1, 0, 2, 3).reshape(slots - 1, tok_rows, width)
    got_twin = lax.ppermute(got, "tok", swap)
    return gram(by_slot, acts, acts_twin, got, got_twin, tok_scale, halves, n)


def solution(mesh):
    return jax.shard_map(
        body,
        mesh=mesh,
        in_specs=(P(("parts", "tok"), "lat"), P(None, "lat"), P("lat"), P("lat"), P()),
        out_specs=P(("parts", "lat"), None, "tok", None),
        check_vma=False,
    )
```

```python
import functools

import jax
import jax.numpy as jnp
from jax import lax
from jax.experimental import pallas as pl
from jax.experimental.pallas import tpu as pltpu
from jax.sharding import PartitionSpec as P

ramp_width = 0.25
ring_size = 8

in_vmem = pl.BlockSpec(memory_space=pltpu.VMEM)
in_smem = pl.BlockSpec(memory_space=pltpu.SMEM)
in_hbm = pl.BlockSpec(memory_space=pltpu.HBM)
params = pltpu.CompilerParams(vmem_limit_bytes=24 * 1024 * 1024)
streaming_params = pltpu.CompilerParams(vmem_limit_bytes=53000000)

rows_by_rows = (((0,), (0,)), ((), ()))


def place_on_ring(block, n):
    half = block // 2
    return half + (block % 2) * (n - 1 - 2 * half)


def block_at(place, n):
    up = 2 * place
    if isinstance(place, int):
        return up if place < n // 2 else 2 * n - 1 - up
    return jnp.where(place < n // 2, up, 2 * n - 1 - up)


def origin(hop, n):
    me = place_on_ring(lax.axis_index("lat"), n)
    return block_at(lax.rem(me + n - hop, n), n)


def activate(pre_acts, threshold):
    gate = jnp.clip((pre_acts - threshold) / ramp_width + 0.5, 0.0, 1.0)
    return (pre_acts * gate).astype(jnp.bfloat16)


def project(x, w):
    return lax.dot_general(x, w, rows_by_rows, preferred_element_type=jnp.float32)


def on_corner(n):
    return place_on_ring(lax.axis_index("lat"), n) % (n // 2) % (n // 2 - 1) == 0


def first_step(hops, later, *refs):
    xs, (weights, total, kept, blocks, sems) = refs[:-5], refs[-5:]
    n = weights.shape[0]
    copies = [
        pltpu.make_async_copy(weights.at[origin(hop, n)], into.at[j], sems.at[j + base])
        for into, base, some in ((blocks, 0, hops), (kept, len(hops), later))
        for j, hop in enumerate(some)
    ]
    for copy in copies:
        copy.start()
    for j, x in enumerate(xs):
        copies[j].wait()
        part = project(x[...], blocks[j])
        total[...] = part if j == 0 else total[...] + part
    for copy in copies[len(hops) :]:
        copy.wait()


def last_step(x, x_f, x_b, x_corner, x_middle, before, blocks, bias, threshold, acts):
    x_far = jnp.where(on_corner(2 * blocks.shape[0]), x_corner[...], x_middle[...])
    pre_acts = before[...] + bias[...]
    for j, part in enumerate((x[...], x_f[...], x_b[...], x_far)):
        pre_acts = pre_acts + project(part, blocks[j])
    acts[...] = activate(pre_acts, threshold[...])


def cost(rows, depth, width, blocks):
    return pl.CostEstimate(
        flops=2 * rows * depth * width * blocks,
        bytes_accessed=2 * depth * (rows + width) * blocks + 8 * rows * width,
        transcendentals=0,
    )


class Ring:
    def __init__(self, n):
        walk = [block_at(i, n) for i in range(n)]
        self.n = n
        self.forward = [(walk[i], walk[(i + 1) % n]) for i in range(n)]
        self.backward = [(d, s) for s, d in self.forward]
        beside = [(i, n - 1 - i) for i in range(n) if i % 4 in (1, 2)]
        across = [(i, (i + 4) % n) for i in range(n) if i % 4 in (0, 3)]
        self.beside = [(walk[i], walk[j]) for i, j in beside]
        self.across = [(walk[i], walk[j]) for i, j in across + beside]

    def gather(self, x, beside_second=None, beside_third=None):
        ahead = lax.ppermute(x, "lat", self.forward)
        behind = lax.ppermute(x, "lat", self.backward)
        corner = lax.ppermute(x, "lat", self.across)
        ahead_2 = lax.ppermute(ahead, "lat", self.forward)
        behind_2 = lax.ppermute(behind, "lat", self.backward)
        odd = place_on_ring(lax.axis_index("lat"), self.n) % 2 == 1
        middle = lax.ppermute(jnp.where(odd, behind, ahead), "lat", self.beside)
        done = beside_second(ahead, behind) if beside_second else ()
        ahead_2, behind_2, corner, done = lax.optimization_barrier(
            (ahead_2, behind_2, corner, done)
        )
        ahead_3 = lax.ppermute(ahead_2, "lat", self.forward)
        behind_3 = lax.ppermute(behind_2, "lat", self.backward)
        done = beside_third(ahead, behind, ahead_2, behind_2, corner, done)
        return done, ahead_3, behind_3, corner, middle


def encode_on_ring(residual, enc_weight, enc_bias, threshold, ring):
    tok_rows, depth = residual.shape
    width = enc_weight.shape[1]
    n = ring.n
    weights = enc_weight.reshape(n, depth, width)

    def beside_third(*blocks):
        blocks = blocks[:4]
        hops, later = (1, -1, 2, -2), (0, 3, -3, n // 2)
        kept = jax.ShapeDtypeStruct((len(later),) + weights.shape[1:], weights.dtype)
        return pl.pallas_call(
            functools.partial(first_step, hops, later),
            out_shape=(jax.ShapeDtypeStruct((tok_rows, width), jnp.float32), kept),
            in_specs=[in_vmem] * len(blocks) + [in_hbm],
            out_specs=(in_vmem, in_vmem),
            scratch_shapes=[
                pltpu.VMEM((len(hops),) + weights.shape[1:], weights.dtype),
                pltpu.SemaphoreType.DMA((len(hops) + len(later),)),
            ],
            compiler_params=streaming_params,
            cost_estimate=cost(tok_rows, depth, width, 4),
        )(*blocks, weights)

    x = residual.T
    (total, kept), ahead, behind, corner, middle = ring.gather(x, beside_third=beside_third)
    return pl.pallas_call(
        last_step,
        out_shape=jax.ShapeDtypeStruct((tok_rows, width), jnp.bfloat16),
        in_specs=[in_vmem] * 9,
        out_specs=in_vmem,
        compiler_params=params,
        cost_estimate=cost(tok_rows, depth, width, 4),
    )(
        x,
        ahead,
        behind,
        corner,
        middle,
        total,
        kept,
        enc_bias.reshape(1, width),
        threshold.reshape(1, width),
    )


def encode_gathered(residual, enc_weight, enc_bias, threshold):
    pre_acts = (
        jnp.dot(
            lax.all_gather(residual, "lat", axis=1, tiled=True),
            enc_weight,
            preferred_element_type=jnp.float32,
        )
        + enc_bias
    )
    return activate(pre_acts, threshold)


def gram_kernel(tok_scale, n, partners, own, own_twin, got, got_twin, out, tiles, sems):
    slots, rows, width = tiles.shape
    me = lax.axis_index("lat")
    columns = pl.ds(pl.multiple_of(lax.axis_index("tok") * rows, rows), rows)
    left = jnp.concatenate([own[:, columns], own_twin[:, columns]], axis=0)

    def tile_of(right, right_twin):
        tile = project(left, jnp.concatenate([right, right_twin], axis=0))
        return (tile * tok_scale).astype(tiles.dtype)

    copies = [pltpu.make_async_copy(tiles.at[k], out.at[0, k], sems.at[k]) for k in range(slots)]
    tiles[0] = tile_of(own[...], own_twin[...])
    copies[0].start()
    for k in range(1, slots):
        live = partners[k, me] < n

        @pl.when(live)
        def _():
            tiles[k] = tile_of(got[k - 1], got_twin[k - 1])

        @pl.when(jnp.logical_not(live))
        def _():
            tiles[k] = jnp.zeros((rows, width), tiles.dtype)

        copies[k].start()
    for copy in copies:
        copy.wait()


def gram(partners, own, own_twin, got, got_twin, tok_scale, halves, n):
    tok_rows, width = own.shape
    slots = partners.shape[0]
    rows = width // halves
    return pl.pallas_call(
        functools.partial(gram_kernel, tok_scale, n),
        out_shape=jax.ShapeDtypeStruct((1, slots, rows, width), own.dtype),
        in_specs=[in_smem] + [in_vmem] * 4,
        out_specs=in_hbm,
        scratch_shapes=[
            pltpu.VMEM((slots, rows, width), own.dtype),
            pltpu.SemaphoreType.DMA((slots,)),
        ],
        compiler_params=params,
    )(partners, own, own_twin, got, got_twin)


def hop_of_slot(partners, k, n):
    me = lax.axis_index("lat")
    listed = partners[k, me]
    hop = lax.rem(place_on_ring(me, n) + n - place_on_ring(jnp.minimum(listed, n - 1), n), n)
    hop = jnp.where((hop == n // 2) & jnp.logical_not(on_corner(n)), n, hop)
    return jnp.where(listed < n, hop, -1)


def tiles_kernel(tok_scale, n, hops, is_first, partners, own, own_twin, *refs):
    count = len(hops)
    blocks, twins = refs[:count], refs[count : 2 * count]
    out, tiles, sems = refs[-3:]
    rows, width = tiles.shape[1:]
    slots = partners.shape[0]
    columns = pl.ds(pl.multiple_of(lax.axis_index("tok") * rows, rows), rows)
    left = jnp.concatenate([own[:, columns], own_twin[:, columns]], axis=0)

    def tile_of(right, right_twin):
        tile = project(left, jnp.concatenate([right[...], right_twin[...]], axis=0))
        return (tile * tok_scale).astype(tiles.dtype)

    slot_hops = [hop_of_slot(partners, k, n) for k in range(1, slots)]
    copies = []

    def send(place, slot, when, value):
        copy = pltpu.make_async_copy(tiles.at[place], out.at[0, slot], sems.at[len(copies)])
        copies.append((copy, when))

        @pl.when(when)
        def _():
            if value is not None:
                tiles[place] = value()
            copy.start()

    if is_first:
        always = lax.axis_index("lat") >= 0
        send(count, 0, always, lambda: tile_of(own, own_twin))
        tiles[count + 1] = jnp.zeros((rows, width), tiles.dtype)
        for k, hop in enumerate(slot_hops):
            send(count + 1, k + 1, hop < 0, None)
    for j, hop in enumerate(hops):
        slot = jnp.int32(0)
        for k, h in enumerate(slot_hops):
            slot = jnp.where(h == hop, jnp.int32(k + 1), slot)
        send(j, slot, slot > 0, functools.partial(tile_of, blocks[j], twins[j]))
    for copy, when in copies:
        pl.when(when)(copy.wait)


def tiles_of(partners, own, own_twin, hops, blocks, twins, before, tok_scale, halves, n):
    width = own.shape[1]
    slots = partners.shape[0]
    rows = width // halves
    first = before is None
    operands = (partners, own, own_twin, *blocks, *twins) + (() if first else (before,))
    specs = [in_smem] + [in_vmem] * (2 + 2 * len(hops)) + ([] if first else [in_hbm])
    return pl.pallas_call(
        functools.partial(tiles_kernel, tok_scale, n, hops, first),
        out_shape=jax.ShapeDtypeStruct((1, slots, rows, width), own.dtype),
        in_specs=specs,
        out_specs=in_hbm,
        input_output_aliases={} if first else {len(operands) - 1: 0},
        scratch_shapes=[
            pltpu.VMEM((len(hops) + (2 if first else 0), rows, width), own.dtype),
            pltpu.SemaphoreType.DMA((len(hops) + (slots if first else 0),)),
        ],
        compiler_params=params,
        cost_estimate=pl.CostEstimate(
            flops=4 * rows * width * own.shape[0] * len(hops),
            bytes_accessed=4 * rows * width * len(hops),
            transcendentals=0,
        ),
    )(*operands)


def body(residual, enc_weight, enc_bias, threshold, partners):
    n = lax.axis_size("lat")
    halves = lax.axis_size("tok")
    tok_rows = residual.shape[0]
    width = enc_weight.shape[1]
    slots = partners.shape[1]
    tok_scale = 1.0 / (tok_rows * halves)
    swap = [(i, 1 - i) for i in range(2)]
    by_slot = partners.T
    if n == ring_size:
        ring = Ring(n)
        acts = encode_on_ring(residual, enc_weight, enc_bias, threshold, ring)
        acts_twin = lax.ppermute(acts, "tok", swap)

        def add_tiles(before, hops, blocks):
            twins = [lax.ppermute(block, "tok", swap) for block in blocks]
            return tiles_of(
                by_slot, acts, acts_twin, hops, blocks, twins, before, tok_scale, halves, n
            )

        def beside_second(ahead, behind):
            return add_tiles(None, (1, n - 1), (ahead, behind))

        def beside_third(ahead, behind, ahead_2, behind_2, corner, before):
            return add_tiles(before, (2, n - 2, n // 2), (ahead_2, behind_2, corner))

        out, ahead, behind, _, middle = ring.gather(acts, beside_second, beside_third)
        out, ahead, behind = lax.optimization_barrier((out, ahead, behind))
        return add_tiles(out, (3, n - 3, n), (ahead, behind, middle))
    acts = encode_gathered(residual, enc_weight, enc_bias, threshold)
    acts_twin = lax.ppermute(acts, "tok", swap)
    slices = lax.all_to_all(acts.reshape(n, tok_rows // n, width), "lat", 0, 0)
    outgoing = jnp.take(slices, jnp.minimum(partners[:, 1:], n - 1), axis=0)
    got = lax.all_to_all(outgoing, "lat", 0, 0)
    got = got.transpose(1, 0, 2, 3).reshape(slots - 1, tok_rows, width)
    got_twin = lax.ppermute(got, "tok", swap)
    return gram(by_slot, acts, acts_twin, got, got_twin, tok_scale, halves, n)


def solution(mesh):
    return jax.shard_map(
        body,
        mesh=mesh,
        in_specs=(P(("parts", "tok"), "lat"), P(None, "lat"), P("lat"), P("lat"), P()),
        out_specs=P(("parts", "lat"), None, "tok", None),
        check_vma=False,
    )
```

```python
import functools

import jax
import jax.numpy as jnp
from jax import lax
from jax.experimental import pallas as pl
from jax.experimental.pallas import tpu as pltpu
from jax.sharding import PartitionSpec as P

ramp_width = 0.25
ring_size = 8

in_vmem = pl.BlockSpec(memory_space=pltpu.VMEM)
in_smem = pl.BlockSpec(memory_space=pltpu.SMEM)
in_hbm = pl.BlockSpec(memory_space=pltpu.HBM)
params = pltpu.CompilerParams(vmem_limit_bytes=24 * 1024 * 1024)
streaming_params = pltpu.CompilerParams(vmem_limit_bytes=53000000)

rows_by_rows = (((0,), (0,)), ((), ()))


def place_on_ring(block, n):
    half = block // 2
    return half + (block % 2) * (n - 1 - 2 * half)


def block_at(place, n):
    up = 2 * place
    if isinstance(place, int):
        return up if place < n // 2 else 2 * n - 1 - up
    return jnp.where(place < n // 2, up, 2 * n - 1 - up)


def origin(hop, n):
    me = place_on_ring(lax.axis_index("lat"), n)
    return block_at(lax.rem(me + n - hop, n), n)


def activate(pre_acts, threshold):
    gate = jnp.clip((pre_acts - threshold) / ramp_width + 0.5, 0.0, 1.0)
    return (pre_acts * gate).astype(jnp.bfloat16)


def project(x, w):
    return lax.dot_general(x, w, rows_by_rows, preferred_element_type=jnp.float32)


def on_corner(n):
    return place_on_ring(lax.axis_index("lat"), n) % (n // 2) % (n // 2 - 1) == 0


def first_step(hops, later, *refs):
    xs, (weights, total, kept, blocks, sems) = refs[:-5], refs[-5:]
    n = weights.shape[0]
    copies = [
        pltpu.make_async_copy(weights.at[origin(hop, n)], into.at[j], sems.at[j + base])
        for into, base, some in ((blocks, 0, hops), (kept, len(hops), later))
        for j, hop in enumerate(some)
    ]
    for copy in copies:
        copy.start()
    for j, x in enumerate(xs):
        copies[j].wait()
        part = project(x[...], blocks[j])
        total[...] = part if j == 0 else total[...] + part
    for copy in copies[len(hops) :]:
        copy.wait()


def last_step(x, x_f, x_b, x_corner, x_middle, before, blocks, bias, threshold, acts):
    x_far = jnp.where(on_corner(2 * blocks.shape[0]), x_corner[...], x_middle[...])
    pre_acts = before[...] + bias[...]
    for j, part in enumerate((x[...], x_f[...], x_b[...], x_far)):
        pre_acts = pre_acts + project(part, blocks[j])
    acts[...] = activate(pre_acts, threshold[...])


def cost(rows, depth, width, blocks):
    return pl.CostEstimate(
        flops=2 * rows * depth * width * blocks,
        bytes_accessed=2 * depth * (rows + width) * blocks + 8 * rows * width,
        transcendentals=0,
    )


class Ring:
    def __init__(self, n):
        walk = [block_at(i, n) for i in range(n)]
        self.n = n
        self.forward = [(walk[i], walk[(i + 1) % n]) for i in range(n)]
        self.backward = [(d, s) for s, d in self.forward]
        beside = [(i, n - 1 - i) for i in range(n) if i % 4 in (1, 2)]
        across = [(i, (i + 4) % n) for i in range(n) if i % 4 in (0, 3)]
        self.beside = [(walk[i], walk[j]) for i, j in beside]
        self.across = [(walk[i], walk[j]) for i, j in across + beside]

    def gather(self, x, beside_second=None, beside_third=None):
        ahead = lax.ppermute(x, "lat", self.forward)
        behind = lax.ppermute(x, "lat", self.backward)
        corner = lax.ppermute(x, "lat", self.across)
        ahead_2 = lax.ppermute(ahead, "lat", self.forward)
        behind_2 = lax.ppermute(behind, "lat", self.backward)
        odd = place_on_ring(lax.axis_index("lat"), self.n) % 2 == 1
        middle = lax.ppermute(jnp.where(odd, behind, ahead), "lat", self.beside)
        done = beside_second(ahead, behind) if beside_second else ()
        ahead_2, behind_2, corner, done = lax.optimization_barrier(
            (ahead_2, behind_2, corner, done)
        )
        ahead_3 = lax.ppermute(ahead_2, "lat", self.forward)
        behind_3 = lax.ppermute(behind_2, "lat", self.backward)
        done = beside_third(ahead, behind, ahead_2, behind_2, corner, done)
        return done, ahead_3, behind_3, corner, middle


def encode_on_ring(residual, enc_weight, enc_bias, threshold, ring):
    tok_rows, depth = residual.shape
    width = enc_weight.shape[1]
    n = ring.n
    weights = enc_weight.reshape(n, depth, width)

    def beside_third(*blocks):
        blocks = blocks[:4]
        hops, later = (1, -1, 2, -2), (0, 3, -3, n // 2)
        kept = jax.ShapeDtypeStruct((len(later),) + weights.shape[1:], weights.dtype)
        return pl.pallas_call(
            functools.partial(first_step, hops, later),
            out_shape=(jax.ShapeDtypeStruct((tok_rows, width), jnp.float32), kept),
            in_specs=[in_vmem] * len(blocks) + [in_hbm],
            out_specs=(in_vmem, in_vmem),
            scratch_shapes=[
                pltpu.VMEM((len(hops),) + weights.shape[1:], weights.dtype),
                pltpu.SemaphoreType.DMA((len(hops) + len(later),)),
            ],
            compiler_params=streaming_params,
            cost_estimate=cost(tok_rows, depth, width, 4),
        )(*blocks, weights)

    x = residual.T
    (total, kept), ahead, behind, corner, middle = ring.gather(x, beside_third=beside_third)
    return pl.pallas_call(
        last_step,
        out_shape=jax.ShapeDtypeStruct((tok_rows, width), jnp.bfloat16),
        in_specs=[in_vmem] * 9,
        out_specs=in_vmem,
        compiler_params=params,
        cost_estimate=cost(tok_rows, depth, width, 4),
    )(
        x,
        ahead,
        behind,
        corner,
        middle,
        total,
        kept,
        enc_bias.reshape(1, width),
        threshold.reshape(1, width),
    )


def encode_gathered(residual, enc_weight, enc_bias, threshold):
    pre_acts = (
        jnp.dot(
            lax.all_gather(residual, "lat", axis=1, tiled=True),
            enc_weight,
            preferred_element_type=jnp.float32,
        )
        + enc_bias
    )
    return activate(pre_acts, threshold)


def gram_kernel(tok_scale, n, partners, own, own_twin, got, got_twin, out, tiles, sems):
    slots, rows, width = tiles.shape
    me = lax.axis_index("lat")
    columns = pl.ds(pl.multiple_of(lax.axis_index("tok") * rows, rows), rows)
    left = jnp.concatenate([own[:, columns], own_twin[:, columns]], axis=0)

    def tile_of(right, right_twin):
        tile = project(left, jnp.concatenate([right, right_twin], axis=0))
        return (tile * tok_scale).astype(tiles.dtype)

    copies = [pltpu.make_async_copy(tiles.at[k], out.at[0, k], sems.at[k]) for k in range(slots)]
    tiles[0] = tile_of(own[...], own_twin[...])
    copies[0].start()
    for k in range(1, slots):
        live = partners[k, me] < n

        @pl.when(live)
        def _():
            tiles[k] = tile_of(got[k - 1], got_twin[k - 1])

        @pl.when(jnp.logical_not(live))
        def _():
            tiles[k] = jnp.zeros((rows, width), tiles.dtype)

        copies[k].start()
    for copy in copies:
        copy.wait()


def gram(partners, own, own_twin, got, got_twin, tok_scale, halves, n):
    tok_rows, width = own.shape
    slots = partners.shape[0]
    rows = width // halves
    return pl.pallas_call(
        functools.partial(gram_kernel, tok_scale, n),
        out_shape=jax.ShapeDtypeStruct((1, slots, rows, width), own.dtype),
        in_specs=[in_smem] + [in_vmem] * 4,
        out_specs=in_hbm,
        scratch_shapes=[
            pltpu.VMEM((slots, rows, width), own.dtype),
            pltpu.SemaphoreType.DMA((slots,)),
        ],
        compiler_params=params,
    )(partners, own, own_twin, got, got_twin)


def hop_of_slot(partners, k, n):
    me = lax.axis_index("lat")
    listed = partners[k, me]
    hop = lax.rem(place_on_ring(me, n) + n - place_on_ring(jnp.minimum(listed, n - 1), n), n)
    hop = jnp.where((hop == n // 2) & jnp.logical_not(on_corner(n)), n, hop)
    return jnp.where(listed < n, hop, -1)


def tiles_kernel(tok_scale, n, hops, is_first, partners, *refs):
    count = len(hops)
    if is_first:
        own, own_twin, refs = refs[0], refs[1], refs[2:]
        left, refs = refs[-4], refs[:-4] + refs[-3:]
    else:
        left, refs = refs[0], refs[1:]
    blocks, twins = refs[:count], refs[count : 2 * count]
    out, tiles, sems = refs[-3:]
    rows, width = tiles.shape[1:]
    half = rows // 2
    slots = partners.shape[0]
    if is_first:
        columns = pl.ds(pl.multiple_of(lax.axis_index("tok") * rows, rows), rows)
        left[...] = jnp.concatenate([own[:, columns], own_twin[:, columns]], axis=0).T

    slot_hops = [hop_of_slot(partners, k, n) for k in range(1, slots)]
    copies = []

    def send(place, slot, when, pair):
        both = []
        for i in range(2):
            part = pl.ds(i * half, half)
            sem = sems.at[len(copies), i]
            both.append(
                pltpu.make_async_copy(tiles.at[place, part], out.at[0, slot, part], sem)
            )
        copies.append((both, when))

        @pl.when(when)
        def _():
            if pair is not None:
                right = jnp.concatenate([pair[0][...], pair[1][...]], axis=0)
            for i in range(2):
                part = pl.ds(i * half, half)
                if pair is not None:
                    tile = jnp.dot(left[part, :], right, preferred_element_type=jnp.float32)
                    tiles[place, part, :] = (tile * tok_scale).astype(tiles.dtype)
                both[i].start()

    if is_first:
        always = lax.axis_index("lat") >= 0
        send(count, 0, always, (own, own_twin))
        tiles[count + 1] = jnp.zeros((rows, width), tiles.dtype)
        for k, hop in enumerate(slot_hops):
            send(count + 1, k + 1, hop < 0, None)
    for j, hop in enumerate(hops):
        slot = jnp.int32(0)
        for k, h in enumerate(slot_hops):
            slot = jnp.where(h == hop, jnp.int32(k + 1), slot)
        send(j, slot, slot > 0, (blocks[j], twins[j]))
    for both, when in copies:

        @pl.when(when)
        def _():
            for copy in both:
                copy.wait()


def tiles_of(partners, owns, before, hops, blocks, twins, tok_scale, halves, n):
    tok_rows, width = blocks[0].shape
    slots = partners.shape[0]
    rows = width // halves
    first = before is None
    dtype = blocks[0].dtype
    out_shape = jax.ShapeDtypeStruct((1, slots, rows, width), dtype)
    left_shape = jax.ShapeDtypeStruct((rows, tok_rows * halves), dtype)
    if first:
        operands = (partners, *owns, *blocks, *twins)
    else:
        operands = (partners, before[0], *blocks, *twins, before[1])
    specs = [in_smem] + [in_vmem] * (len(operands) - 1)
    done = pl.pallas_call(
        functools.partial(tiles_kernel, tok_scale, n, hops, first),
        out_shape=(left_shape, out_shape) if first else out_shape,
        in_specs=specs if first else specs[:-1] + [in_hbm],
        out_specs=(in_vmem, in_hbm) if first else in_hbm,
        input_output_aliases={} if first else {len(operands) - 1: 0},
        scratch_shapes=[
            pltpu.VMEM((len(hops) + (2 if first else 0), rows, width), dtype),
            pltpu.SemaphoreType.DMA((len(hops) + (slots if first else 0), 2)),
        ],
        compiler_params=params,
        cost_estimate=pl.CostEstimate(
            flops=4 * rows * width * tok_rows * len(hops),
            bytes_accessed=4 * rows * width * len(hops),
            transcendentals=0,
        ),
    )(*operands)
    return done if first else (before[0], done)


def body(residual, enc_weight, enc_bias, threshold, partners):
    n = lax.axis_size("lat")
    halves = lax.axis_size("tok")
    tok_rows = residual.shape[0]
    width = enc_weight.shape[1]
    slots = partners.shape[1]
    tok_scale = 1.0 / (tok_rows * halves)
    swap = [(i, 1 - i) for i in range(2)]
    by_slot = partners.T
    if n == ring_size:
        ring = Ring(n)
        acts = encode_on_ring(residual, enc_weight, enc_bias, threshold, ring)
        acts_twin = lax.ppermute(acts, "tok", swap)

        def add_tiles(before, hops, blocks):
            twins = [lax.ppermute(block, "tok", swap) for block in blocks]
            owns = (acts, acts_twin)
            return tiles_of(by_slot, owns, before, hops, blocks, twins, tok_scale, halves, n)

        def beside_second(ahead, behind):
            return add_tiles(None, (1, n - 1), (ahead, behind))

        def beside_third(ahead, behind, ahead_2, behind_2, corner, before):
            return add_tiles(before, (2, n - 2, n // 2), (ahead_2, behind_2, corner))

        out, ahead, behind, _, middle = ring.gather(acts, beside_second, beside_third)
        out, ahead, behind = lax.optimization_barrier((out, ahead, behind))
        return add_tiles(out, (3, n - 3, n), (ahead, behind, middle))[1]
    acts = encode_gathered(residual, enc_weight, enc_bias, threshold)
    acts_twin = lax.ppermute(acts, "tok", swap)
    slices = lax.all_to_all(acts.reshape(n, tok_rows // n, width), "lat", 0, 0)
    outgoing = jnp.take(slices, jnp.minimum(partners[:, 1:], n - 1), axis=0)
    got = lax.all_to_all(outgoing, "lat", 0, 0)
    got = got.transpose(1, 0, 2, 3).reshape(slots - 1, tok_rows, width)
    got_twin = lax.ppermute(got, "tok", swap)
    return gram(by_slot, acts, acts_twin, got, got_twin, tok_scale, halves, n)


def solution(mesh):
    return jax.shard_map(
        body,
        mesh=mesh,
        in_specs=(P(("parts", "tok"), "lat"), P(None, "lat"), P("lat"), P("lat"), P()),
        out_specs=P(("parts", "lat"), None, "tok", None),
        check_vma=False,
    )
```

```python
import functools

import jax
import jax.numpy as jnp
from jax import lax
from jax.experimental import pallas as pl
from jax.experimental.pallas import tpu as pltpu
from jax.sharding import PartitionSpec as P

ramp_width = 0.25
ring_size = 8

in_vmem = pl.BlockSpec(memory_space=pltpu.VMEM)
in_smem = pl.BlockSpec(memory_space=pltpu.SMEM)
in_hbm = pl.BlockSpec(memory_space=pltpu.HBM)
params = pltpu.CompilerParams(vmem_limit_bytes=24 * 1024 * 1024)
streaming_params = pltpu.CompilerParams(vmem_limit_bytes=53000000)

rows_by_rows = (((0,), (0,)), ((), ()))


def place_on_ring(block, n):
    half = block // 2
    return half + (block % 2) * (n - 1 - 2 * half)


def block_at(place, n):
    up = 2 * place
    if isinstance(place, int):
        return up if place < n // 2 else 2 * n - 1 - up
    return jnp.where(place < n // 2, up, 2 * n - 1 - up)


def origin(hop, n):
    me = place_on_ring(lax.axis_index("lat"), n)
    return block_at(lax.rem(me + n - hop, n), n)


def activate(pre_acts, threshold):
    gate = jnp.clip((pre_acts - threshold) / ramp_width + 0.5, 0.0, 1.0)
    return (pre_acts * gate).astype(jnp.bfloat16)


def project(x, w):
    return lax.dot_general(x, w, rows_by_rows, preferred_element_type=jnp.float32)


def on_corner(n):
    return place_on_ring(lax.axis_index("lat"), n) % (n // 2) % (n // 2 - 1) == 0


def first_step(hops, later, *refs):
    xs, (weights, total, kept, blocks, sems) = refs[:-5], refs[-5:]
    n = weights.shape[0]
    copies = [
        pltpu.make_async_copy(weights.at[origin(hop, n)], into.at[j], sems.at[j + base])
        for into, base, some in ((blocks, 0, hops), (kept, len(hops), later))
        for j, hop in enumerate(some)
    ]
    for copy in copies:
        copy.start()
    for j, x in enumerate(xs):
        copies[j].wait()
        part = project(x[...], blocks[j])
        total[...] = part if j == 0 else total[...] + part
    for copy in copies[len(hops) :]:
        copy.wait()


def last_step(x, x_f, x_b, x_corner, x_middle, before, blocks, bias, threshold, acts):
    x_far = jnp.where(on_corner(2 * blocks.shape[0]), x_corner[...], x_middle[...])
    pre_acts = before[...] + bias[...]
    for j, part in enumerate((x[...], x_f[...], x_b[...], x_far)):
        pre_acts = pre_acts + project(part, blocks[j])
    acts[...] = activate(pre_acts, threshold[...])


def cost(rows, depth, width, blocks):
    return pl.CostEstimate(
        flops=2 * rows * depth * width * blocks,
        bytes_accessed=2 * depth * (rows + width) * blocks + 8 * rows * width,
        transcendentals=0,
    )


class Ring:
    def __init__(self, n):
        walk = [block_at(i, n) for i in range(n)]
        self.n = n
        self.forward = [(walk[i], walk[(i + 1) % n]) for i in range(n)]
        self.backward = [(d, s) for s, d in self.forward]
        beside = [(i, n - 1 - i) for i in range(n) if i % 4 in (1, 2)]
        across = [(i, (i + 4) % n) for i in range(n) if i % 4 in (0, 3)]
        aside = [(2 * walk[i] + t, 2 * walk[j] + t) for i, j in beside for t in range(2)]
        stay = [(2 * walk[i] + t, 2 * walk[i] + 1 - t) for i, _ in across for t in range(2)]
        self.beside = aside + stay
        self.across = [(walk[i], walk[j]) for i, j in across + beside]

    def gather(self, x, beside_second=None, beside_third=None):
        ahead = lax.ppermute(x, "lat", self.forward)
        behind = lax.ppermute(x, "lat", self.backward)
        corner = lax.ppermute(x, "lat", self.across)
        ahead_2 = lax.ppermute(ahead, "lat", self.forward)
        behind_2 = lax.ppermute(behind, "lat", self.backward)
        odd = place_on_ring(lax.axis_index("lat"), self.n) % 2 == 1
        middle = lax.ppermute(jnp.where(odd, behind, ahead), ("lat", "tok"), self.beside)
        done = beside_second(ahead, behind) if beside_second else ()
        ahead_2, behind_2, corner, done = lax.optimization_barrier(
            (ahead_2, behind_2, corner, done)
        )
        ahead_3 = lax.ppermute(ahead_2, "lat", self.forward)
        behind_3 = lax.ppermute(behind_2, "lat", self.backward)
        done, middle = lax.optimization_barrier((done, middle))
        done = beside_third(ahead, behind, ahead_2, behind_2, corner, done)
        return done, ahead_3, behind_3, corner, middle


def encode_on_ring(residual, enc_weight, enc_bias, threshold, ring):
    tok_rows, depth = residual.shape
    width = enc_weight.shape[1]
    n = ring.n
    weights = enc_weight.reshape(n, depth, width)

    def beside_third(*blocks):
        blocks = blocks[:4]
        hops, later = (1, -1, 2, -2), (0, 3, -3, n // 2)
        kept = jax.ShapeDtypeStruct((len(later),) + weights.shape[1:], weights.dtype)
        return pl.pallas_call(
            functools.partial(first_step, hops, later),
            out_shape=(jax.ShapeDtypeStruct((tok_rows, width), jnp.float32), kept),
            in_specs=[in_vmem] * len(blocks) + [in_hbm],
            out_specs=(in_vmem, in_vmem),
            scratch_shapes=[
                pltpu.VMEM((len(hops),) + weights.shape[1:], weights.dtype),
                pltpu.SemaphoreType.DMA((len(hops) + len(later),)),
            ],
            compiler_params=streaming_params,
            cost_estimate=cost(tok_rows, depth, width, 4),
        )(*blocks, weights)

    x = residual.T
    (total, kept), ahead, behind, corner, middle = ring.gather(x, beside_third=beside_third)
    return pl.pallas_call(
        last_step,
        out_shape=jax.ShapeDtypeStruct((tok_rows, width), jnp.bfloat16),
        in_specs=[in_vmem] * 9,
        out_specs=in_vmem,
        compiler_params=params,
        cost_estimate=cost(tok_rows, depth, width, 4),
    )(
        x,
        ahead,
        behind,
        corner,
        middle,
        total,
        kept,
        enc_bias.reshape(1, width),
        threshold.reshape(1, width),
    )


def encode_gathered(residual, enc_weight, enc_bias, threshold):
    pre_acts = (
        jnp.dot(
            lax.all_gather(residual, "lat", axis=1, tiled=True),
            enc_weight,
            preferred_element_type=jnp.float32,
        )
        + enc_bias
    )
    return activate(pre_acts, threshold)


def gram_kernel(tok_scale, n, partners, own, own_twin, got, got_twin, out, tiles, sems):
    slots, rows, width = tiles.shape
    me = lax.axis_index("lat")
    columns = pl.ds(pl.multiple_of(lax.axis_index("tok") * rows, rows), rows)
    left = jnp.concatenate([own[:, columns], own_twin[:, columns]], axis=0)

    def tile_of(right, right_twin):
        tile = project(left, jnp.concatenate([right, right_twin], axis=0))
        return (tile * tok_scale).astype(tiles.dtype)

    copies = [pltpu.make_async_copy(tiles.at[k], out.at[0, k], sems.at[k]) for k in range(slots)]
    tiles[0] = tile_of(own[...], own_twin[...])
    copies[0].start()
    for k in range(1, slots):
        live = partners[k, me] < n

        @pl.when(live)
        def _():
            tiles[k] = tile_of(got[k - 1], got_twin[k - 1])

        @pl.when(jnp.logical_not(live))
        def _():
            tiles[k] = jnp.zeros((rows, width), tiles.dtype)

        copies[k].start()
    for copy in copies:
        copy.wait()


def gram(partners, own, own_twin, got, got_twin, tok_scale, halves, n):
    tok_rows, width = own.shape
    slots = partners.shape[0]
    rows = width // halves
    return pl.pallas_call(
        functools.partial(gram_kernel, tok_scale, n),
        out_shape=jax.ShapeDtypeStruct((1, slots, rows, width), own.dtype),
        in_specs=[in_smem] + [in_vmem] * 4,
        out_specs=in_hbm,
        scratch_shapes=[
            pltpu.VMEM((slots, rows, width), own.dtype),
            pltpu.SemaphoreType.DMA((slots,)),
        ],
        compiler_params=params,
    )(partners, own, own_twin, got, got_twin)


def hop_of_slot(partners, k, n):
    me = lax.axis_index("lat")
    listed = partners[k, me]
    hop = lax.rem(place_on_ring(me, n) + n - place_on_ring(jnp.minimum(listed, n - 1), n), n)
    hop = jnp.where((hop == n // 2) & jnp.logical_not(on_corner(n)), n, hop)
    return jnp.where(listed < n, hop, -1)


def tiles_kernel(tok_scale, n, hops, is_first, partners, *refs):
    count = len(hops)
    if is_first:
        own, own_twin, refs = refs[0], refs[1], refs[2:]
        left, refs = refs[-4], refs[:-4] + refs[-3:]
    else:
        left, refs = refs[0], refs[1:]
    blocks, twins = refs[:count], refs[count : 2 * count]
    out, tiles, sems = refs[-3:]
    rows, width = tiles.shape[1:]
    half = rows // 2
    slots = partners.shape[0]
    if is_first:
        columns = pl.ds(pl.multiple_of(lax.axis_index("tok") * rows, rows), rows)
        left[...] = jnp.concatenate([own[:, columns], own_twin[:, columns]], axis=0).T

    slot_hops = [hop_of_slot(partners, k, n) for k in range(1, slots)]
    copies = []

    def send(place, slot, when, pair):
        both = []
        for i in range(2):
            part = pl.ds(i * half, half)
            sem = sems.at[len(copies), i]
            both.append(
                pltpu.make_async_copy(tiles.at[place, part], out.at[0, slot, part], sem)
            )
        copies.append((both, when))

        @pl.when(when)
        def _():
            if pair is not None:
                right = jnp.concatenate([pair[0][...], pair[1][...]], axis=0)
            for i in range(2):
                part = pl.ds(i * half, half)
                if pair is not None:
                    tile = jnp.dot(left[part, :], right, preferred_element_type=jnp.float32)
                    tiles[place, part, :] = (tile * tok_scale).astype(tiles.dtype)
                both[i].start()

    if is_first:
        always = lax.axis_index("lat") >= 0
        send(count, 0, always, (own, own_twin))
        tiles[count + 1] = jnp.zeros((rows, width), tiles.dtype)
        for k, hop in enumerate(slot_hops):
            send(count + 1, k + 1, hop < 0, None)
    for j, hop in enumerate(hops):
        slot = jnp.int32(0)
        for k, h in enumerate(slot_hops):
            slot = jnp.where(h == hop, jnp.int32(k + 1), slot)
        send(j, slot, slot > 0, (blocks[j], twins[j]))
    for both, when in copies:

        @pl.when(when)
        def _():
            for copy in both:
                copy.wait()


def tiles_of(partners, owns, before, hops, blocks, twins, tok_scale, halves, n):
    tok_rows, width = blocks[0].shape
    slots = partners.shape[0]
    rows = width // halves
    first = before is None
    dtype = blocks[0].dtype
    out_shape = jax.ShapeDtypeStruct((1, slots, rows, width), dtype)
    left_shape = jax.ShapeDtypeStruct((rows, tok_rows * halves), dtype)
    if first:
        operands = (partners, *owns, *blocks, *twins)
    else:
        operands = (partners, before[0], *blocks, *twins, before[1])
    specs = [in_smem] + [in_vmem] * (len(operands) - 1)
    done = pl.pallas_call(
        functools.partial(tiles_kernel, tok_scale, n, hops, first),
        out_shape=(left_shape, out_shape) if first else out_shape,
        in_specs=specs if first else specs[:-1] + [in_hbm],
        out_specs=(in_vmem, in_hbm) if first else in_hbm,
        input_output_aliases={} if first else {len(operands) - 1: 0},
        scratch_shapes=[
            pltpu.VMEM((len(hops) + (2 if first else 0), rows, width), dtype),
            pltpu.SemaphoreType.DMA((len(hops) + (slots if first else 0), 2)),
        ],
        compiler_params=params,
        cost_estimate=pl.CostEstimate(
            flops=4 * rows * width * tok_rows * len(hops),
            bytes_accessed=4 * rows * width * len(hops),
            transcendentals=0,
        ),
    )(*operands)
    return done if first else (before[0], done)


def body(residual, enc_weight, enc_bias, threshold, partners):
    n = lax.axis_size("lat")
    halves = lax.axis_size("tok")
    tok_rows = residual.shape[0]
    width = enc_weight.shape[1]
    slots = partners.shape[1]
    tok_scale = 1.0 / (tok_rows * halves)
    swap = [(i, 1 - i) for i in range(2)]
    by_slot = partners.T
    if n == ring_size:
        ring = Ring(n)
        acts = encode_on_ring(residual, enc_weight, enc_bias, threshold, ring)
        acts_twin = lax.ppermute(acts, "tok", swap)

        def add_tiles(before, hops, blocks):
            twins = [lax.ppermute(block, "tok", swap) for block in blocks]
            owns = (acts, acts_twin)
            return tiles_of(by_slot, owns, before, hops, blocks, twins, tok_scale, halves, n)

        def beside_second(ahead, behind):
            return add_tiles(None, (1, n - 1), (ahead, behind))

        def beside_third(ahead, behind, ahead_2, behind_2, corner, before):
            return add_tiles(before, (2, n - 2, n // 2), (ahead_2, behind_2, corner))

        out, *late = ring.gather(acts, beside_second, beside_third)
        out, (ahead, behind, _, middle) = lax.optimization_barrier((out, late))
        return add_tiles(out, (3, n - 3, n), (ahead, behind, middle))[1]
    acts = encode_gathered(residual, enc_weight, enc_bias, threshold)
    acts_twin = lax.ppermute(acts, "tok", swap)
    slices = lax.all_to_all(acts.reshape(n, tok_rows // n, width), "lat", 0, 0)
    outgoing = jnp.take(slices, jnp.minimum(partners[:, 1:], n - 1), axis=0)
    got = lax.all_to_all(outgoing, "lat", 0, 0)
    got = got.transpose(1, 0, 2, 3).reshape(slots - 1, tok_rows, width)
    got_twin = lax.ppermute(got, "tok", swap)
    return gram(by_slot, acts, acts_twin, got, got_twin, tok_scale, halves, n)


def solution(mesh):
    return jax.shard_map(
        body,
        mesh=mesh,
        in_specs=(P(("parts", "tok"), "lat"), P(None, "lat"), P("lat"), P("lat"), P()),
        out_specs=P(("parts", "lat"), None, "tok", None),
        check_vma=False,
    )
```

```python
import functools

import jax
import jax.numpy as jnp
from jax import lax
from jax.experimental import pallas as pl
from jax.experimental.pallas import tpu as pltpu
from jax.sharding import PartitionSpec as P

ramp_width = 0.25
ring_size = 8

in_vmem = pl.BlockSpec(memory_space=pltpu.VMEM)
in_smem = pl.BlockSpec(memory_space=pltpu.SMEM)
in_hbm = pl.BlockSpec(memory_space=pltpu.HBM)
params = pltpu.CompilerParams(vmem_limit_bytes=24 * 1024 * 1024)
streaming_params = pltpu.CompilerParams(vmem_limit_bytes=53000000)

rows_by_rows = (((0,), (0,)), ((), ()))


def place_on_ring(block, n):
    half = block // 2
    return half + (block % 2) * (n - 1 - 2 * half)


def block_at(place, n):
    up = 2 * place
    if isinstance(place, int):
        return up if place < n // 2 else 2 * n - 1 - up
    return jnp.where(place < n // 2, up, 2 * n - 1 - up)


def origin(hop, n):
    me = place_on_ring(lax.axis_index("lat"), n)
    return block_at(lax.rem(me + n - hop, n), n)


def activate(pre_acts, threshold):
    gate = jnp.clip((pre_acts - threshold) / ramp_width + 0.5, 0.0, 1.0)
    return (pre_acts * gate).astype(jnp.bfloat16)


def project(x, w):
    return lax.dot_general(x, w, rows_by_rows, preferred_element_type=jnp.float32)


def on_corner(n):
    return place_on_ring(lax.axis_index("lat"), n) % (n // 2) % (n // 2 - 1) == 0


def first_step(hops, later, *refs):
    xs, (weights, total, kept, blocks, sems) = refs[:-5], refs[-5:]
    n = weights.shape[0]
    copies = [
        pltpu.make_async_copy(weights.at[origin(hop, n)], into.at[j], sems.at[j + base])
        for into, base, some in ((blocks, 0, hops), (kept, len(hops), later))
        for j, hop in enumerate(some)
    ]
    for copy in copies:
        copy.start()
    for j, x in enumerate(xs):
        copies[j].wait()
        part = project(x[...], blocks[j])
        total[...] = part if j == 0 else total[...] + part
    for copy in copies[len(hops) :]:
        copy.wait()


def last_step(x, x_f, x_b, x_corner, x_middle, before, blocks, bias, threshold, acts):
    x_far = jnp.where(on_corner(2 * blocks.shape[0]), x_corner[...], x_middle[...])
    pre_acts = before[...] + bias[...]
    for j, part in enumerate((x[...], x_f[...], x_b[...], x_far)):
        pre_acts = pre_acts + project(part, blocks[j])
    acts[...] = activate(pre_acts, threshold[...])


def cost(rows, depth, width, blocks):
    return pl.CostEstimate(
        flops=2 * rows * depth * width * blocks,
        bytes_accessed=2 * depth * (rows + width) * blocks + 8 * rows * width,
        transcendentals=0,
    )


class Ring:
    def __init__(self, n):
        walk = [block_at(i, n) for i in range(n)]
        self.n = n
        self.forward = [(walk[i], walk[(i + 1) % n]) for i in range(n)]
        self.backward = [(d, s) for s, d in self.forward]
        beside = [(i, n - 1 - i) for i in range(n) if i % 4 in (1, 2)]
        across = [(i, (i + 4) % n) for i in range(n) if i % 4 in (0, 3)]
        aside = [(2 * walk[i] + t, 2 * walk[j] + t) for i, j in beside for t in range(2)]
        stay = [(2 * walk[i] + t, 2 * walk[i] + 1 - t) for i, _ in across for t in range(2)]
        self.beside = aside + stay
        self.across = [(walk[i], walk[j]) for i, j in across + beside]

    def gather(self, x, beside_second=None, beside_third=None):
        ahead = lax.ppermute(x, "lat", self.forward)
        behind = lax.ppermute(x, "lat", self.backward)
        corner = lax.ppermute(x, "lat", self.across)
        ahead_2 = lax.ppermute(ahead, "lat", self.forward)
        behind_2 = lax.ppermute(behind, "lat", self.backward)
        odd = place_on_ring(lax.axis_index("lat"), self.n) % 2 == 1
        middle = lax.ppermute(jnp.where(odd, behind, ahead), ("lat", "tok"), self.beside)
        done = beside_second(ahead, behind) if beside_second else ()
        ahead_2, behind_2, corner, done = lax.optimization_barrier(
            (ahead_2, behind_2, corner, done)
        )
        ahead_3 = lax.ppermute(ahead_2, "lat", self.forward)
        behind_3 = lax.ppermute(behind_2, "lat", self.backward)
        done, middle = lax.optimization_barrier((done, middle))
        done = beside_third(ahead, behind, ahead_2, behind_2, corner, done)
        return done, ahead_3, behind_3, corner, middle


def encode_on_ring(residual, enc_weight, enc_bias, threshold, ring):
    tok_rows, depth = residual.shape
    width = enc_weight.shape[1]
    n = ring.n
    weights = enc_weight.reshape(n, depth, width)

    def beside_third(*blocks):
        blocks = blocks[:4]
        hops, later = (1, -1, 2, -2), (0, 3, -3, n // 2)
        kept = jax.ShapeDtypeStruct((len(later),) + weights.shape[1:], weights.dtype)
        return pl.pallas_call(
            functools.partial(first_step, hops, later),
            out_shape=(jax.ShapeDtypeStruct((tok_rows, width), jnp.float32), kept),
            in_specs=[in_vmem] * len(blocks) + [in_hbm],
            out_specs=(in_vmem, in_vmem),
            scratch_shapes=[
                pltpu.VMEM((len(hops),) + weights.shape[1:], weights.dtype),
                pltpu.SemaphoreType.DMA((len(hops) + len(later),)),
            ],
            compiler_params=streaming_params,
            cost_estimate=cost(tok_rows, depth, width, 4),
        )(*blocks, weights)

    x = residual.T
    (total, kept), ahead, behind, corner, middle = ring.gather(x, beside_third=beside_third)
    return pl.pallas_call(
        last_step,
        out_shape=jax.ShapeDtypeStruct((tok_rows, width), jnp.bfloat16),
        in_specs=[in_vmem] * 9,
        out_specs=in_vmem,
        compiler_params=params,
        cost_estimate=cost(tok_rows, depth, width, 4),
    )(
        x,
        ahead,
        behind,
        corner,
        middle,
        total,
        kept,
        enc_bias.reshape(1, width),
        threshold.reshape(1, width),
    )


def encode_gathered(residual, enc_weight, enc_bias, threshold):
    pre_acts = (
        jnp.dot(
            lax.all_gather(residual, "lat", axis=1, tiled=True),
            enc_weight,
            preferred_element_type=jnp.float32,
        )
        + enc_bias
    )
    return activate(pre_acts, threshold)


def gram_kernel(tok_scale, n, partners, own, own_twin, got, got_twin, out, tiles, sems):
    slots, rows, width = tiles.shape
    me = lax.axis_index("lat")
    columns = pl.ds(pl.multiple_of(lax.axis_index("tok") * rows, rows), rows)
    left = jnp.concatenate([own[:, columns], own_twin[:, columns]], axis=0)

    def tile_of(right, right_twin):
        tile = project(left, jnp.concatenate([right, right_twin], axis=0))
        return (tile * tok_scale).astype(tiles.dtype)

    copies = [pltpu.make_async_copy(tiles.at[k], out.at[0, k], sems.at[k]) for k in range(slots)]
    tiles[0] = tile_of(own[...], own_twin[...])
    copies[0].start()
    for k in range(1, slots):
        live = partners[k, me] < n

        @pl.when(live)
        def _():
            tiles[k] = tile_of(got[k - 1], got_twin[k - 1])

        @pl.when(jnp.logical_not(live))
        def _():
            tiles[k] = jnp.zeros((rows, width), tiles.dtype)

        copies[k].start()
    for copy in copies:
        copy.wait()


def gram(partners, own, own_twin, got, got_twin, tok_scale, halves, n):
    tok_rows, width = own.shape
    slots = partners.shape[0]
    rows = width // halves
    return pl.pallas_call(
        functools.partial(gram_kernel, tok_scale, n),
        out_shape=jax.ShapeDtypeStruct((1, slots, rows, width), own.dtype),
        in_specs=[in_smem] + [in_vmem] * 4,
        out_specs=in_hbm,
        scratch_shapes=[
            pltpu.VMEM((slots, rows, width), own.dtype),
            pltpu.SemaphoreType.DMA((slots,)),
        ],
        compiler_params=params,
    )(partners, own, own_twin, got, got_twin)


def hop_of_slot(partners, k, n):
    me = lax.axis_index("lat")
    listed = partners[k, me]
    hop = lax.rem(place_on_ring(me, n) + n - place_on_ring(jnp.minimum(listed, n - 1), n), n)
    return jnp.where(listed < n, hop, -1)


def tiles_kernel(tok_scale, n, hops, is_first, partners, *refs):
    count = len(hops)
    if is_first:
        own, own_twin, refs = refs[0], refs[1], refs[2:]
        left, refs = refs[-4], refs[:-4] + refs[-3:]
    else:
        left, refs = refs[0], refs[1:]
    blocks, twins = refs[:count], refs[count : 2 * count]
    out, tiles, sems = refs[-3:]
    rows, width = tiles.shape[1:]
    half = rows // 2
    slots = partners.shape[0]
    if is_first:
        columns = pl.ds(pl.multiple_of(lax.axis_index("tok") * rows, rows), rows)
        left[...] = jnp.concatenate([own[:, columns], own_twin[:, columns]], axis=0).T

    slot_hops = [hop_of_slot(partners, k, n) for k in range(1, slots)]
    copies = []

    def send(place, slot, when, pair):
        both = []
        for i in range(2):
            part = pl.ds(i * half, half)
            sem = sems.at[len(copies), i]
            both.append(
                pltpu.make_async_copy(tiles.at[place, part], out.at[0, slot, part], sem)
            )
        copies.append((both, when))

        @pl.when(when)
        def _():
            if pair is not None:
                right = jnp.concatenate([pair[0][...], pair[1][...]], axis=0)
            for i in range(2):
                part = pl.ds(i * half, half)
                if pair is not None:
                    tile = jnp.dot(left[part, :], right, preferred_element_type=jnp.float32)
                    tiles[place, part, :] = (tile * tok_scale).astype(tiles.dtype)
                both[i].start()

    if is_first:
        always = lax.axis_index("lat") >= 0
        send(count, 0, always, (own, own_twin))
        tiles[count + 1] = jnp.zeros((rows, width), tiles.dtype)
        for k, hop in enumerate(slot_hops):
            send(count + 1, k + 1, hop < 0, None)
    for j, hop in enumerate(hops):
        slot = jnp.int32(0)
        for k, h in enumerate(slot_hops):
            slot = jnp.where(h == hop, jnp.int32(k + 1), slot)
        send(j, slot, slot > 0, (blocks[j], twins[j]))
    for both, when in copies:

        @pl.when(when)
        def _():
            for copy in both:
                copy.wait()


def tiles_of(partners, owns, before, hops, blocks, twins, tok_scale, halves, n):
    tok_rows, width = blocks[0].shape
    slots = partners.shape[0]
    rows = width // halves
    first = before is None
    dtype = blocks[0].dtype
    out_shape = jax.ShapeDtypeStruct((1, slots, rows, width), dtype)
    left_shape = jax.ShapeDtypeStruct((rows, tok_rows * halves), dtype)
    if first:
        operands = (partners, *owns, *blocks, *twins)
    else:
        operands = (partners, before[0], *blocks, *twins, before[1])
    specs = [in_smem] + [in_vmem] * (len(operands) - 1)
    done = pl.pallas_call(
        functools.partial(tiles_kernel, tok_scale, n, hops, first),
        out_shape=(left_shape, out_shape) if first else out_shape,
        in_specs=specs if first else specs[:-1] + [in_hbm],
        out_specs=(in_vmem, in_hbm) if first else in_hbm,
        input_output_aliases={} if first else {len(operands) - 1: 0},
        scratch_shapes=[
            pltpu.VMEM((len(hops) + (2 if first else 0), rows, width), dtype),
            pltpu.SemaphoreType.DMA((len(hops) + (slots if first else 0), 2)),
        ],
        compiler_params=params,
        cost_estimate=pl.CostEstimate(
            flops=4 * rows * width * tok_rows * len(hops),
            bytes_accessed=4 * rows * width * len(hops),
            transcendentals=0,
        ),
    )(*operands)
    return done if first else (before[0], done)


def body(residual, enc_weight, enc_bias, threshold, partners):
    n = lax.axis_size("lat")
    halves = lax.axis_size("tok")
    tok_rows = residual.shape[0]
    width = enc_weight.shape[1]
    slots = partners.shape[1]
    tok_scale = 1.0 / (tok_rows * halves)
    swap = [(i, 1 - i) for i in range(2)]
    by_slot = partners.T
    if n == ring_size:
        ring = Ring(n)
        acts = encode_on_ring(residual, enc_weight, enc_bias, threshold, ring)
        acts_twin = lax.ppermute(acts, "tok", swap)

        def add_tiles(before, hops, blocks):
            twins = [lax.ppermute(block, "tok", swap) for block in blocks]
            owns = (acts, acts_twin)
            return tiles_of(by_slot, owns, before, hops, blocks, twins, tok_scale, halves, n)

        def beside_second(ahead, behind):
            return add_tiles(None, (1, n - 1), (ahead, behind))

        def beside_third(ahead, behind, ahead_2, behind_2, _, before):
            return add_tiles(before, (2, n - 2), (ahead_2, behind_2))

        out, *late = ring.gather(acts, beside_second, beside_third)
        ahead, behind, corner, middle = late
        far = jnp.where(on_corner(n), corner, middle)
        out, ahead, behind = lax.optimization_barrier((out, ahead, behind))
        return add_tiles(out, (3, n - 3, n // 2), (ahead, behind, far))[1]
    acts = encode_gathered(residual, enc_weight, enc_bias, threshold)
    acts_twin = lax.ppermute(acts, "tok", swap)
    slices = lax.all_to_all(acts.reshape(n, tok_rows // n, width), "lat", 0, 0)
    outgoing = jnp.take(slices, jnp.minimum(partners[:, 1:], n - 1), axis=0)
    got = lax.all_to_all(outgoing, "lat", 0, 0)
    got = got.transpose(1, 0, 2, 3).reshape(slots - 1, tok_rows, width)
    got_twin = lax.ppermute(got, "tok", swap)
    return gram(by_slot, acts, acts_twin, got, got_twin, tok_scale, halves, n)


def solution(mesh):
    return jax.shard_map(
        body,
        mesh=mesh,
        in_specs=(P(("parts", "tok"), "lat"), P(None, "lat"), P("lat"), P("lat"), P()),
        out_specs=P(("parts", "lat"), None, "tok", None),
        check_vma=False,
    )
```

```python
import functools

import jax
import jax.numpy as jnp
from jax import lax
from jax.experimental import pallas as pl
from jax.experimental.pallas import tpu as pltpu
from jax.sharding import PartitionSpec as P

ramp_width = 0.25
ring_size = 8

in_vmem = pl.BlockSpec(memory_space=pltpu.VMEM)
in_smem = pl.BlockSpec(memory_space=pltpu.SMEM)
in_hbm = pl.BlockSpec(memory_space=pltpu.HBM)
params = pltpu.CompilerParams(vmem_limit_bytes=24 * 1024 * 1024)
streaming_params = pltpu.CompilerParams(vmem_limit_bytes=53000000)

rows_by_rows = (((0,), (0,)), ((), ()))


def place_on_ring(block, n):
    half = block // 2
    return half + (block % 2) * (n - 1 - 2 * half)


def block_at(place, n):
    up = 2 * place
    if isinstance(place, int):
        return up if place < n // 2 else 2 * n - 1 - up
    return jnp.where(place < n // 2, up, 2 * n - 1 - up)


def origin(hop, n):
    me = place_on_ring(lax.axis_index("lat"), n)
    return block_at(lax.rem(me + n - hop, n), n)


def activate(pre_acts, threshold):
    gate = jnp.clip((pre_acts - threshold) / ramp_width + 0.5, 0.0, 1.0)
    return (pre_acts * gate).astype(jnp.bfloat16)


def project(x, w):
    return lax.dot_general(x, w, rows_by_rows, preferred_element_type=jnp.float32)


def on_corner(n):
    return place_on_ring(lax.axis_index("lat"), n) % (n // 2) % (n // 2 - 1) == 0


def first_step(hops, later, *refs):
    xs, (weights, total, kept, blocks, sems) = refs[:-5], refs[-5:]
    n = weights.shape[0]
    copies = [
        pltpu.make_async_copy(weights.at[origin(hop, n)], into.at[j], sems.at[j + base])
        for into, base, some in ((blocks, 0, hops), (kept, len(hops), later))
        for j, hop in enumerate(some)
    ]
    for copy in copies:
        copy.start()
    for j, x in enumerate(xs):
        copies[j].wait()
        part = project(x[...], blocks[j])
        total[...] = part if j == 0 else total[...] + part
    for copy in copies[len(hops) :]:
        copy.wait()


def last_step(x, x_f, x_b, x_corner, x_middle, before, blocks, bias, threshold, acts):
    x_far = jnp.where(on_corner(2 * blocks.shape[0]), x_corner[...], x_middle[...])
    pre_acts = before[...] + bias[...]
    for j, part in enumerate((x[...], x_f[...], x_b[...], x_far)):
        pre_acts = pre_acts + project(part, blocks[j])
    acts[...] = activate(pre_acts, threshold[...])


def cost(rows, depth, width, blocks):
    return pl.CostEstimate(
        flops=2 * rows * depth * width * blocks,
        bytes_accessed=2 * depth * (rows + width) * blocks + 8 * rows * width,
        transcendentals=0,
    )


class Ring:
    def __init__(self, n):
        walk = [block_at(i, n) for i in range(n)]
        self.n = n
        self.forward = [(walk[i], walk[(i + 1) % n]) for i in range(n)]
        self.backward = [(d, s) for s, d in self.forward]
        beside = [(i, n - 1 - i) for i in range(n) if i % 4 in (1, 2)]
        across = [(i, (i + 4) % n) for i in range(n) if i % 4 in (0, 3)]
        aside = [(2 * walk[i] + t, 2 * walk[j] + t) for i, j in beside for t in range(2)]
        stay = [(2 * walk[i] + t, 2 * walk[i] + 1 - t) for i, _ in across for t in range(2)]
        self.beside = aside + stay
        self.across = [(walk[i], walk[j]) for i, j in across + beside]

    def gather(self, x, beside_second=None, beside_third=None):
        ahead = lax.ppermute(x, "lat", self.forward)
        behind = lax.ppermute(x, "lat", self.backward)
        corner = lax.ppermute(x, "lat", self.across)
        ahead_2 = lax.ppermute(ahead, "lat", self.forward)
        behind_2 = lax.ppermute(behind, "lat", self.backward)
        odd = place_on_ring(lax.axis_index("lat"), self.n) % 2 == 1
        middle = lax.ppermute(jnp.where(odd, behind, ahead), ("lat", "tok"), self.beside)
        done = beside_second(ahead, behind) if beside_second else ()
        ahead_2, behind_2, corner, done = lax.optimization_barrier(
            (ahead_2, behind_2, corner, done)
        )
        ahead_3 = lax.ppermute(ahead_2, "lat", self.forward)
        behind_3 = lax.ppermute(behind_2, "lat", self.backward)
        done, middle = lax.optimization_barrier((done, middle))
        done = beside_third(ahead, behind, ahead_2, behind_2, corner, done)
        return done, ahead_3, behind_3, corner, middle


def encode_on_ring(residual, enc_weight, enc_bias, threshold, ring):
    tok_rows, depth = residual.shape
    width = enc_weight.shape[1]
    n = ring.n
    weights = enc_weight.reshape(n, depth, width)

    def beside_third(*blocks):
        blocks = blocks[:4]
        hops, later = (1, -1, 2, -2), (0, 3, -3, n // 2)
        kept = jax.ShapeDtypeStruct((len(later),) + weights.shape[1:], weights.dtype)
        return pl.pallas_call(
            functools.partial(first_step, hops, later),
            out_shape=(jax.ShapeDtypeStruct((tok_rows, width), jnp.float32), kept),
            in_specs=[in_vmem] * len(blocks) + [in_hbm],
            out_specs=(in_vmem, in_vmem),
            scratch_shapes=[
                pltpu.VMEM((len(hops),) + weights.shape[1:], weights.dtype),
                pltpu.SemaphoreType.DMA((len(hops) + len(later),)),
            ],
            compiler_params=streaming_params,
            cost_estimate=cost(tok_rows, depth, width, 4),
        )(*blocks, weights)

    x = residual.T
    (total, kept), ahead, behind, corner, middle = ring.gather(x, beside_third=beside_third)
    return pl.pallas_call(
        last_step,
        out_shape=jax.ShapeDtypeStruct((tok_rows, width), jnp.bfloat16),
        in_specs=[in_vmem] * 9,
        out_specs=in_vmem,
        compiler_params=params,
        cost_estimate=cost(tok_rows, depth, width, 4),
    )(
        x,
        ahead,
        behind,
        corner,
        middle,
        total,
        kept,
        enc_bias.reshape(1, width),
        threshold.reshape(1, width),
    )


def encode_gathered(residual, enc_weight, enc_bias, threshold):
    pre_acts = (
        jnp.dot(
            lax.all_gather(residual, "lat", axis=1, tiled=True),
            enc_weight,
            preferred_element_type=jnp.float32,
        )
        + enc_bias
    )
    return activate(pre_acts, threshold)


def gram_kernel(tok_scale, n, partners, own, own_twin, got, got_twin, out, tiles, sems):
    slots, rows, width = tiles.shape
    me = lax.axis_index("lat")
    columns = pl.ds(pl.multiple_of(lax.axis_index("tok") * rows, rows), rows)
    left = jnp.concatenate([own[:, columns], own_twin[:, columns]], axis=0)

    def tile_of(right, right_twin):
        tile = project(left, jnp.concatenate([right, right_twin], axis=0))
        return (tile * tok_scale).astype(tiles.dtype)

    copies = [pltpu.make_async_copy(tiles.at[k], out.at[0, k], sems.at[k]) for k in range(slots)]
    tiles[0] = tile_of(own[...], own_twin[...])
    copies[0].start()
    for k in range(1, slots):
        live = partners[k, me] < n

        @pl.when(live)
        def _():
            tiles[k] = tile_of(got[k - 1], got_twin[k - 1])

        @pl.when(jnp.logical_not(live))
        def _():
            tiles[k] = jnp.zeros((rows, width), tiles.dtype)

        copies[k].start()
    for copy in copies:
        copy.wait()


def gram(partners, own, own_twin, got, got_twin, tok_scale, halves, n):
    tok_rows, width = own.shape
    slots = partners.shape[0]
    rows = width // halves
    return pl.pallas_call(
        functools.partial(gram_kernel, tok_scale, n),
        out_shape=jax.ShapeDtypeStruct((1, slots, rows, width), own.dtype),
        in_specs=[in_smem] + [in_vmem] * 4,
        out_specs=in_hbm,
        scratch_shapes=[
            pltpu.VMEM((slots, rows, width), own.dtype),
            pltpu.SemaphoreType.DMA((slots,)),
        ],
        compiler_params=params,
    )(partners, own, own_twin, got, got_twin)


def hop_of_slot(partners, k, n):
    me = lax.axis_index("lat")
    row = partners[k : k + 1, :]
    mine = lax.broadcasted_iota(jnp.int32, row.shape, 1) == me
    listed = jnp.sum(jnp.where(mine, row, 0))
    hop = lax.rem(place_on_ring(me, n) + n - place_on_ring(jnp.minimum(listed, n - 1), n), n)
    return jnp.where(listed < n, hop, -1)


def tiles_kernel(tok_scale, n, hops, is_first, partners, *refs):
    count = len(hops)
    if is_first:
        own, own_twin, refs = refs[0], refs[1], refs[2:]
        left, refs = refs[-4], refs[:-4] + refs[-3:]
    else:
        left, refs = refs[0], refs[1:]
    blocks, twins = refs[:count], refs[count : 2 * count]
    out, tiles, sems = refs[-3:]
    rows, width = tiles.shape[1:]
    half = rows // 2
    slots = partners.shape[0]
    if is_first:
        columns = pl.ds(pl.multiple_of(lax.axis_index("tok") * rows, rows), rows)
        left[...] = jnp.concatenate([own[:, columns], own_twin[:, columns]], axis=0).T

    slot_hops = [hop_of_slot(partners, k, n) for k in range(1, slots)]
    copies = []

    def send(place, slot, when, pair):
        both = []
        for i in range(2):
            part = pl.ds(i * half, half)
            sem = sems.at[len(copies), i]
            both.append(
                pltpu.make_async_copy(tiles.at[place, part], out.at[0, slot, part], sem)
            )
        copies.append((both, when))

        @pl.when(when)
        def _():
            if pair is not None:
                right = jnp.concatenate([pair[0][...], pair[1][...]], axis=0)
            for i in range(2):
                part = pl.ds(i * half, half)
                if pair is not None:
                    tile = jnp.dot(left[part, :], right, preferred_element_type=jnp.float32)
                    tiles[place, part, :] = (tile * tok_scale).astype(tiles.dtype)
                both[i].start()

    if is_first:
        always = lax.axis_index("lat") >= 0
        send(count, 0, always, (own, own_twin))
        tiles[count + 1] = jnp.zeros((rows, width), tiles.dtype)
        for k, hop in enumerate(slot_hops):
            send(count + 1, k + 1, hop < 0, None)
    for j, hop in enumerate(hops):
        slot = jnp.int32(0)
        for k, h in enumerate(slot_hops):
            slot = jnp.where(h == hop, jnp.int32(k + 1), slot)
        send(j, slot, slot > 0, (blocks[j], twins[j]))
    for both, when in copies:

        @pl.when(when)
        def _():
            for copy in both:
                copy.wait()


def tiles_of(partners, owns, before, hops, blocks, twins, tok_scale, halves, n):
    tok_rows, width = blocks[0].shape
    slots = partners.shape[0]
    rows = width // halves
    first = before is None
    dtype = blocks[0].dtype
    out_shape = jax.ShapeDtypeStruct((1, slots, rows, width), dtype)
    left_shape = jax.ShapeDtypeStruct((rows, tok_rows * halves), dtype)
    if first:
        operands = (partners, *owns, *blocks, *twins)
    else:
        operands = (partners, before[0], *blocks, *twins, before[1])
    specs = [in_vmem] * len(operands)
    done = pl.pallas_call(
        functools.partial(tiles_kernel, tok_scale, n, hops, first),
        out_shape=(left_shape, out_shape) if first else out_shape,
        in_specs=specs if first else specs[:-1] + [in_hbm],
        out_specs=(in_vmem, in_hbm) if first else in_hbm,
        input_output_aliases={} if first else {len(operands) - 1: 0},
        scratch_shapes=[
            pltpu.VMEM((len(hops) + (2 if first else 0), rows, width), dtype),
            pltpu.SemaphoreType.DMA((len(hops) + (slots if first else 0), 2)),
        ],
        compiler_params=params,
        cost_estimate=pl.CostEstimate(
            flops=4 * rows * width * tok_rows * len(hops),
            bytes_accessed=4 * rows * width * len(hops),
            transcendentals=0,
        ),
    )(*operands)
    return done if first else (before[0], done)


def body(residual, enc_weight, enc_bias, threshold, partners):
    n = lax.axis_size("lat")
    halves = lax.axis_size("tok")
    tok_rows = residual.shape[0]
    width = enc_weight.shape[1]
    slots = partners.shape[1]
    tok_scale = 1.0 / (tok_rows * halves)
    swap = [(i, 1 - i) for i in range(2)]
    by_slot = partners.T
    if n == ring_size:
        ring = Ring(n)
        acts = encode_on_ring(residual, enc_weight, enc_bias, threshold, ring)
        acts_twin = lax.ppermute(acts, "tok", swap)

        def add_tiles(before, hops, blocks):
            twins = [lax.ppermute(block, "tok", swap) for block in blocks]
            owns = (acts, acts_twin)
            return tiles_of(by_slot, owns, before, hops, blocks, twins, tok_scale, halves, n)

        def beside_second(ahead, behind):
            return add_tiles(None, (1, n - 1), (ahead, behind))

        def beside_third(ahead, behind, ahead_2, behind_2, _, before):
            return add_tiles(before, (2, n - 2), (ahead_2, behind_2))

        out, *late = ring.gather(acts, beside_second, beside_third)
        ahead, behind, corner, middle = late
        far = jnp.where(on_corner(n), corner, middle)
        out, ahead, behind = lax.optimization_barrier((out, ahead, behind))
        return add_tiles(out, (3, n - 3, n // 2), (ahead, behind, far))[1]
    acts = encode_gathered(residual, enc_weight, enc_bias, threshold)
    acts_twin = lax.ppermute(acts, "tok", swap)
    slices = lax.all_to_all(acts.reshape(n, tok_rows // n, width), "lat", 0, 0)
    outgoing = jnp.take(slices, jnp.minimum(partners[:, 1:], n - 1), axis=0)
    got = lax.all_to_all(outgoing, "lat", 0, 0)
    got = got.transpose(1, 0, 2, 3).reshape(slots - 1, tok_rows, width)
    got_twin = lax.ppermute(got, "tok", swap)
    return gram(by_slot, acts, acts_twin, got, got_twin, tok_scale, halves, n)


def solution(mesh):
    return jax.shard_map(
        body,
        mesh=mesh,
        in_specs=(P(("parts", "tok"), "lat"), P(None, "lat"), P("lat"), P("lat"), P()),
        out_specs=P(("parts", "lat"), None, "tok", None),
        check_vma=False,
    )
```

```python
import functools

import jax
import jax.numpy as jnp
from jax import lax
from jax.experimental import pallas as pl
from jax.experimental.pallas import tpu as pltpu
from jax.sharding import PartitionSpec as P

ramp_width = 0.25
ring_size = 8

in_vmem = pl.BlockSpec(memory_space=pltpu.VMEM)
in_smem = pl.BlockSpec(memory_space=pltpu.SMEM)
in_hbm = pl.BlockSpec(memory_space=pltpu.HBM)
params = pltpu.CompilerParams(vmem_limit_bytes=24 * 1024 * 1024)
streaming_params = pltpu.CompilerParams(vmem_limit_bytes=53000000)

rows_by_rows = (((0,), (0,)), ((), ()))


def place_on_ring(block, n):
    half = block // 2
    return half + (block % 2) * (n - 1 - 2 * half)


def block_at(place, n):
    up = 2 * place
    if isinstance(place, int):
        return up if place < n // 2 else 2 * n - 1 - up
    return jnp.where(place < n // 2, up, 2 * n - 1 - up)


def origin(hop, n):
    me = place_on_ring(lax.axis_index("lat"), n)
    return block_at(lax.rem(me + n - hop, n), n)


def activate(pre_acts, threshold):
    gate = jnp.clip((pre_acts - threshold) / ramp_width + 0.5, 0.0, 1.0)
    return (pre_acts * gate).astype(jnp.bfloat16)


def project(x, w):
    return lax.dot_general(x, w, rows_by_rows, preferred_element_type=jnp.float32)


def on_corner(n):
    return place_on_ring(lax.axis_index("lat"), n) % (n // 2) % (n // 2 - 1) == 0


def first_step(hops, later, *refs):
    xs, (weights, total, kept, blocks, sems) = refs[:-5], refs[-5:]
    n = weights.shape[0]
    copies = [
        pltpu.make_async_copy(weights.at[origin(hop, n)], into.at[j], sems.at[j + base])
        for into, base, some in ((blocks, 0, hops), (kept, len(hops), later))
        for j, hop in enumerate(some)
    ]
    for copy in copies:
        copy.start()
    for j, x in enumerate(xs):
        copies[j].wait()
        part = project(x[...], blocks[j])
        total[...] = part if j == 0 else total[...] + part
    for copy in copies[len(hops) :]:
        copy.wait()


def last_step(x, x_f, x_b, x_corner, x_middle, before, blocks, bias, threshold, acts):
    x_far = jnp.where(on_corner(2 * blocks.shape[0]), x_corner[...], x_middle[...])
    pre_acts = before[...] + bias[...]
    for j, part in enumerate((x[...], x_f[...], x_b[...], x_far)):
        pre_acts = pre_acts + project(part, blocks[j])
    acts[...] = activate(pre_acts, threshold[...])


def cost(rows, depth, width, blocks):
    return pl.CostEstimate(
        flops=2 * rows * depth * width * blocks,
        bytes_accessed=2 * depth * (rows + width) * blocks + 8 * rows * width,
        transcendentals=0,
    )


class Ring:
    def __init__(self, n):
        walk = [block_at(i, n) for i in range(n)]
        self.n = n
        self.forward = [(walk[i], walk[(i + 1) % n]) for i in range(n)]
        self.backward = [(d, s) for s, d in self.forward]
        beside = [(i, n - 1 - i) for i in range(n) if i % 4 in (1, 2)]
        across = [(i, (i + 4) % n) for i in range(n) if i % 4 in (0, 3)]
        aside = [(2 * walk[i] + t, 2 * walk[j] + t) for i, j in beside for t in range(2)]
        stay = [(2 * walk[i] + t, 2 * walk[i] + 1 - t) for i, _ in across for t in range(2)]
        self.beside = aside + stay
        self.across = [(walk[i], walk[j]) for i, j in across + beside]

    def gather(self, x, beside_third):
        ahead = lax.ppermute(x, "lat", self.forward)
        behind = lax.ppermute(x, "lat", self.backward)
        corner = lax.ppermute(x, "lat", self.across)
        ahead_2 = lax.ppermute(ahead, "lat", self.forward)
        behind_2 = lax.ppermute(behind, "lat", self.backward)
        odd = place_on_ring(lax.axis_index("lat"), self.n) % 2 == 1
        middle = lax.ppermute(jnp.where(odd, behind, ahead), ("lat", "tok"), self.beside)
        ahead_2, behind_2, corner = lax.optimization_barrier((ahead_2, behind_2, corner))
        ahead_3 = lax.ppermute(ahead_2, "lat", self.forward)
        behind_3 = lax.ppermute(behind_2, "lat", self.backward)
        ahead, middle = lax.optimization_barrier((ahead, middle))
        done = beside_third(ahead, behind, ahead_2, behind_2)
        return done, ahead_3, behind_3, corner, middle


def encode_on_ring(residual, enc_weight, enc_bias, threshold, ring):
    tok_rows, depth = residual.shape
    width = enc_weight.shape[1]
    n = ring.n
    weights = enc_weight.reshape(n, depth, width)

    def beside_third(*blocks):
        blocks = blocks[:4]
        hops, later = (1, -1, 2, -2), (0, 3, -3, n // 2)
        kept = jax.ShapeDtypeStruct((len(later),) + weights.shape[1:], weights.dtype)
        return pl.pallas_call(
            functools.partial(first_step, hops, later),
            out_shape=(jax.ShapeDtypeStruct((tok_rows, width), jnp.float32), kept),
            in_specs=[in_vmem] * len(blocks) + [in_hbm],
            out_specs=(in_vmem, in_vmem),
            scratch_shapes=[
                pltpu.VMEM((len(hops),) + weights.shape[1:], weights.dtype),
                pltpu.SemaphoreType.DMA((len(hops) + len(later),)),
            ],
            compiler_params=streaming_params,
            cost_estimate=cost(tok_rows, depth, width, 4),
        )(*blocks, weights)

    x = residual.T
    (total, kept), ahead, behind, corner, middle = ring.gather(x, beside_third)
    return pl.pallas_call(
        last_step,
        out_shape=jax.ShapeDtypeStruct((tok_rows, width), jnp.bfloat16),
        in_specs=[in_vmem] * 9,
        out_specs=in_vmem,
        compiler_params=params,
        cost_estimate=cost(tok_rows, depth, width, 4),
    )(
        x,
        ahead,
        behind,
        corner,
        middle,
        total,
        kept,
        enc_bias.reshape(1, width),
        threshold.reshape(1, width),
    )


def encode_gathered(residual, enc_weight, enc_bias, threshold):
    pre_acts = (
        jnp.dot(
            lax.all_gather(residual, "lat", axis=1, tiled=True),
            enc_weight,
            preferred_element_type=jnp.float32,
        )
        + enc_bias
    )
    return activate(pre_acts, threshold)


def gram_kernel(tok_scale, n, partners, own, own_twin, got, got_twin, out, tiles, sems):
    slots, rows, width = tiles.shape
    me = lax.axis_index("lat")
    columns = pl.ds(pl.multiple_of(lax.axis_index("tok") * rows, rows), rows)
    left = jnp.concatenate([own[:, columns], own_twin[:, columns]], axis=0)

    def tile_of(right, right_twin):
        tile = project(left, jnp.concatenate([right, right_twin], axis=0))
        return (tile * tok_scale).astype(tiles.dtype)

    copies = [pltpu.make_async_copy(tiles.at[k], out.at[0, k], sems.at[k]) for k in range(slots)]
    tiles[0] = tile_of(own[...], own_twin[...])
    copies[0].start()
    for k in range(1, slots):
        live = partners[k, me] < n

        @pl.when(live)
        def _():
            tiles[k] = tile_of(got[k - 1], got_twin[k - 1])

        @pl.when(jnp.logical_not(live))
        def _():
            tiles[k] = jnp.zeros((rows, width), tiles.dtype)

        copies[k].start()
    for copy in copies:
        copy.wait()


def gram(partners, own, own_twin, got, got_twin, tok_scale, halves, n):
    tok_rows, width = own.shape
    slots = partners.shape[0]
    rows = width // halves
    return pl.pallas_call(
        functools.partial(gram_kernel, tok_scale, n),
        out_shape=jax.ShapeDtypeStruct((1, slots, rows, width), own.dtype),
        in_specs=[in_smem] + [in_vmem] * 4,
        out_specs=in_hbm,
        scratch_shapes=[
            pltpu.VMEM((slots, rows, width), own.dtype),
            pltpu.SemaphoreType.DMA((slots,)),
        ],
        compiler_params=params,
    )(partners, own, own_twin, got, got_twin)


def hop_of_slot(partners, k, n):
    me = lax.axis_index("lat")
    row = partners[k : k + 1, :]
    mine = lax.broadcasted_iota(jnp.int32, row.shape, 1) == me
    listed = jnp.sum(jnp.where(mine, row, 0))
    hop = lax.rem(place_on_ring(me, n) + n - place_on_ring(jnp.minimum(listed, n - 1), n), n)
    return jnp.where(listed < n, hop, -1)


def tiles_kernel(tok_scale, n, hops, is_first, partners, *refs):
    count = len(hops)
    if is_first:
        own, own_twin, refs = refs[0], refs[1], refs[2:]
        left, refs = refs[-4], refs[:-4] + refs[-3:]
    else:
        left, refs = refs[0], refs[1:]
    blocks, twins = refs[:count], refs[count : 2 * count]
    out, tiles, sems = refs[-3:]
    rows, width = tiles.shape[1:]
    half = rows // 2
    slots = partners.shape[0]
    if is_first:
        columns = pl.ds(pl.multiple_of(lax.axis_index("tok") * rows, rows), rows)
        left[...] = jnp.concatenate([own[:, columns], own_twin[:, columns]], axis=0).T

    slot_hops = [hop_of_slot(partners, k, n) for k in range(1, slots)]
    copies = []

    def send(place, slot, when, pair):
        both = []
        for i in range(2):
            part = pl.ds(i * half, half)
            sem = sems.at[len(copies), i]
            both.append(
                pltpu.make_async_copy(tiles.at[place, part], out.at[0, slot, part], sem)
            )
        copies.append((both, when))

        @pl.when(when)
        def _():
            if pair is not None:
                right = jnp.concatenate([pair[0][...], pair[1][...]], axis=0)
            for i in range(2):
                part = pl.ds(i * half, half)
                if pair is not None:
                    tile = jnp.dot(left[part, :], right, preferred_element_type=jnp.float32)
                    tiles[place, part, :] = (tile * tok_scale).astype(tiles.dtype)
                both[i].start()

    if is_first:
        always = lax.axis_index("lat") >= 0
        send(count, 0, always, (own, own_twin))
        tiles[count + 1] = jnp.zeros((rows, width), tiles.dtype)
        for k, hop in enumerate(slot_hops):
            send(count + 1, k + 1, hop < 0, None)
    for j, hop in enumerate(hops):
        slot = jnp.int32(0)
        for k, h in enumerate(slot_hops):
            slot = jnp.where(h == hop, jnp.int32(k + 1), slot)
        send(j, slot, slot > 0, (blocks[j], twins[j]))
    for both, when in copies:

        @pl.when(when)
        def _():
            for copy in both:
                copy.wait()


def tiles_of(partners, owns, before, hops, blocks, twins, tok_scale, halves, n):
    tok_rows, width = blocks[0].shape
    slots = partners.shape[0]
    rows = width // halves
    first = before is None
    dtype = blocks[0].dtype
    out_shape = jax.ShapeDtypeStruct((1, slots, rows, width), dtype)
    left_shape = jax.ShapeDtypeStruct((rows, tok_rows * halves), dtype)
    if first:
        operands = (partners, *owns, *blocks, *twins)
    else:
        operands = (partners, before[0], *blocks, *twins, before[1])
    specs = [in_vmem] * len(operands)
    done = pl.pallas_call(
        functools.partial(tiles_kernel, tok_scale, n, hops, first),
        out_shape=(left_shape, out_shape) if first else out_shape,
        in_specs=specs if first else specs[:-1] + [in_hbm],
        out_specs=(in_vmem, in_hbm) if first else in_hbm,
        input_output_aliases={} if first else {len(operands) - 1: 0},
        scratch_shapes=[
            pltpu.VMEM((len(hops) + (2 if first else 0), rows, width), dtype),
            pltpu.SemaphoreType.DMA((len(hops) + (slots if first else 0), 2)),
        ],
        compiler_params=params,
        cost_estimate=pl.CostEstimate(
            flops=4 * rows * width * tok_rows * len(hops),
            bytes_accessed=4 * rows * width * len(hops),
            transcendentals=0,
        ),
    )(*operands)
    return done if first else (before[0], done)


def body(residual, enc_weight, enc_bias, threshold, partners):
    n = lax.axis_size("lat")
    halves = lax.axis_size("tok")
    tok_rows = residual.shape[0]
    width = enc_weight.shape[1]
    slots = partners.shape[1]
    tok_scale = 1.0 / (tok_rows * halves)
    swap = [(i, 1 - i) for i in range(2)]
    by_slot = partners.T
    if n == ring_size:
        ring = Ring(n)
        acts = encode_on_ring(residual, enc_weight, enc_bias, threshold, ring)
        acts_twin = lax.ppermute(acts, "tok", swap)

        def add_tiles(before, hops, blocks):
            twins = [lax.ppermute(block, "tok", swap) for block in blocks]
            owns = (acts, acts_twin)
            return tiles_of(by_slot, owns, before, hops, blocks, twins, tok_scale, halves, n)

        def beside_third(ahead, behind, ahead_2, behind_2):
            return add_tiles(None, (1, n - 1, 2, n - 2), (ahead, behind, ahead_2, behind_2))

        out, *late = ring.gather(acts, beside_third)
        ahead, behind, corner, middle = late
        far = jnp.where(on_corner(n), corner, middle)
        out, ahead, behind = lax.optimization_barrier((out, ahead, behind))
        return add_tiles(out, (3, n - 3, n // 2), (ahead, behind, far))[1]
    acts = encode_gathered(residual, enc_weight, enc_bias, threshold)
    acts_twin = lax.ppermute(acts, "tok", swap)
    slices = lax.all_to_all(acts.reshape(n, tok_rows // n, width), "lat", 0, 0)
    outgoing = jnp.take(slices, jnp.minimum(partners[:, 1:], n - 1), axis=0)
    got = lax.all_to_all(outgoing, "lat", 0, 0)
    got = got.transpose(1, 0, 2, 3).reshape(slots - 1, tok_rows, width)
    got_twin = lax.ppermute(got, "tok", swap)
    return gram(by_slot, acts, acts_twin, got, got_twin, tok_scale, halves, n)


def solution(mesh):
    return jax.shard_map(
        body,
        mesh=mesh,
        in_specs=(P(("parts", "tok"), "lat"), P(None, "lat"), P("lat"), P("lat"), P()),
        out_specs=P(("parts", "lat"), None, "tok", None),
        check_vma=False,
    )
```

```python
import functools

import jax
import jax.numpy as jnp
from jax import lax
from jax.experimental import pallas as pl
from jax.experimental.pallas import tpu as pltpu
from jax.sharding import PartitionSpec as P

ramp_width = 0.25
ring_size = 8

in_vmem = pl.BlockSpec(memory_space=pltpu.VMEM)
in_smem = pl.BlockSpec(memory_space=pltpu.SMEM)
in_hbm = pl.BlockSpec(memory_space=pltpu.HBM)
params = pltpu.CompilerParams(vmem_limit_bytes=24 * 1024 * 1024)
streaming_params = pltpu.CompilerParams(vmem_limit_bytes=53000000)

rows_by_rows = (((0,), (0,)), ((), ()))


def place_on_ring(block, n):
    half = block // 2
    return half + (block % 2) * (n - 1 - 2 * half)


def block_at(place, n):
    up = 2 * place
    if isinstance(place, int):
        return up if place < n // 2 else 2 * n - 1 - up
    return jnp.where(place < n // 2, up, 2 * n - 1 - up)


def origin(hop, n):
    me = place_on_ring(lax.axis_index("lat"), n)
    return block_at(lax.rem(me + n - hop, n), n)


def activate(pre_acts, threshold):
    gate = jnp.clip((pre_acts - threshold) / ramp_width + 0.5, 0.0, 1.0)
    return (pre_acts * gate).astype(jnp.bfloat16)


def project(x, w):
    return lax.dot_general(x, w, rows_by_rows, preferred_element_type=jnp.float32)


def on_corner(n):
    return place_on_ring(lax.axis_index("lat"), n) % (n // 2) % (n // 2 - 1) == 0


def first_step(hops, later, paces, *refs):
    refs = refs[paces:]
    xs, (weights, total, kept, blocks, sems) = refs[:-5], refs[-5:]
    n = weights.shape[0]
    copies = [
        pltpu.make_async_copy(weights.at[origin(hop, n)], into.at[j], sems.at[j + base])
        for into, base, some in ((blocks, 0, hops), (kept, len(hops), later))
        for j, hop in enumerate(some)
    ]
    for copy in copies:
        copy.start()
    for j, x in enumerate(xs):
        copies[j].wait()
        part = project(x[...], blocks[j])
        total[...] = part if j == 0 else total[...] + part
    for copy in copies[len(hops) :]:
        copy.wait()


def last_step(x, x_f, x_b, x_corner, x_middle, before, blocks, bias, threshold, acts):
    x_far = jnp.where(on_corner(2 * blocks.shape[0]), x_corner[...], x_middle[...])
    pre_acts = before[...] + bias[...]
    for j, part in enumerate((x[...], x_f[...], x_b[...], x_far)):
        pre_acts = pre_acts + project(part, blocks[j])
    acts[...] = activate(pre_acts, threshold[...])


def cost(rows, depth, width, blocks):
    return pl.CostEstimate(
        flops=2 * rows * depth * width * blocks,
        bytes_accessed=2 * depth * (rows + width) * blocks + 8 * rows * width,
        transcendentals=0,
    )


class Ring:
    def __init__(self, n):
        walk = [block_at(i, n) for i in range(n)]
        self.n = n
        self.forward = [(walk[i], walk[(i + 1) % n]) for i in range(n)]
        self.backward = [(d, s) for s, d in self.forward]
        beside = [(i, n - 1 - i) for i in range(n) if i % 4 in (1, 2)]
        across = [(i, (i + 4) % n) for i in range(n) if i % 4 in (0, 3)]
        aside = [(2 * walk[i] + t, 2 * walk[j] + t) for i, j in beside for t in range(2)]
        stay = [(2 * walk[i] + t, 2 * walk[i] + 1 - t) for i, _ in across for t in range(2)]
        self.beside = aside + stay
        self.across = [(walk[i], walk[j]) for i, j in across + beside]

    def gather(self, x, beside_second=None, beside_third=None, in_pace=False):
        ahead = lax.ppermute(x, "lat", self.forward)
        behind = lax.ppermute(x, "lat", self.backward)
        corner = lax.ppermute(x, "lat", self.across)
        if in_pace:
            pace = lax.ppermute(x[:16], "tok", [(0, 1), (1, 0)])
            ahead, behind, pace = lax.optimization_barrier((ahead, behind, pace))
        ahead_2 = lax.ppermute(ahead, "lat", self.forward)
        behind_2 = lax.ppermute(behind, "lat", self.backward)
        odd = place_on_ring(lax.axis_index("lat"), self.n) % 2 == 1
        middle = lax.ppermute(jnp.where(odd, behind, ahead), ("lat", "tok"), self.beside)
        done = beside_second(ahead, behind) if beside_second else ()
        ahead_2, behind_2, corner, done = lax.optimization_barrier(
            (ahead_2, behind_2, corner, done)
        )
        ahead_3 = lax.ppermute(ahead_2, "lat", self.forward)
        behind_3 = lax.ppermute(behind_2, "lat", self.backward)
        done, middle = lax.optimization_barrier((done, middle))
        if in_pace:
            done = (pace, done)
        done = beside_third(ahead, behind, ahead_2, behind_2, corner, done)
        return done, ahead_3, behind_3, corner, middle


def encode_on_ring(residual, enc_weight, enc_bias, threshold, ring):
    tok_rows, depth = residual.shape
    width = enc_weight.shape[1]
    n = ring.n
    weights = enc_weight.reshape(n, depth, width)

    def beside_third(*blocks):
        blocks, paces = blocks[:4], jax.tree.leaves(blocks[5])
        hops, later = (1, -1, 2, -2), (0, 3, -3, n // 2)
        kept = jax.ShapeDtypeStruct((len(later),) + weights.shape[1:], weights.dtype)
        return pl.pallas_call(
            functools.partial(first_step, hops, later, len(paces)),
            out_shape=(jax.ShapeDtypeStruct((tok_rows, width), jnp.float32), kept),
            in_specs=[in_vmem] * (len(paces) + len(blocks)) + [in_hbm],
            out_specs=(in_vmem, in_vmem),
            scratch_shapes=[
                pltpu.VMEM((len(hops),) + weights.shape[1:], weights.dtype),
                pltpu.SemaphoreType.DMA((len(hops) + len(later),)),
            ],
            compiler_params=streaming_params,
            cost_estimate=cost(tok_rows, depth, width, 4),
        )(*paces, *blocks, weights)

    x = residual.T
    (total, kept), ahead, behind, corner, middle = ring.gather(x, beside_third=beside_third, in_pace=True)
    return pl.pallas_call(
        last_step,
        out_shape=jax.ShapeDtypeStruct((tok_rows, width), jnp.bfloat16),
        in_specs=[in_vmem] * 9,
        out_specs=in_vmem,
        compiler_params=params,
        cost_estimate=cost(tok_rows, depth, width, 4),
    )(
        x,
        ahead,
        behind,
        corner,
        middle,
        total,
        kept,
        enc_bias.reshape(1, width),
        threshold.reshape(1, width),
    )


def encode_gathered(residual, enc_weight, enc_bias, threshold):
    pre_acts = (
        jnp.dot(
            lax.all_gather(residual, "lat", axis=1, tiled=True),
            enc_weight,
            preferred_element_type=jnp.float32,
        )
        + enc_bias
    )
    return activate(pre_acts, threshold)


def gram_kernel(tok_scale, n, partners, own, own_twin, got, got_twin, out, tiles, sems):
    slots, rows, width = tiles.shape
    me = lax.axis_index("lat")
    columns = pl.ds(pl.multiple_of(lax.axis_index("tok") * rows, rows), rows)
    left = jnp.concatenate([own[:, columns], own_twin[:, columns]], axis=0)

    def tile_of(right, right_twin):
        tile = project(left, jnp.concatenate([right, right_twin], axis=0))
        return (tile * tok_scale).astype(tiles.dtype)

    copies = [pltpu.make_async_copy(tiles.at[k], out.at[0, k], sems.at[k]) for k in range(slots)]
    tiles[0] = tile_of(own[...], own_twin[...])
    copies[0].start()
    for k in range(1, slots):
        live = partners[k, me] < n

        @pl.when(live)
        def _():
            tiles[k] = tile_of(got[k - 1], got_twin[k - 1])

        @pl.when(jnp.logical_not(live))
        def _():
            tiles[k] = jnp.zeros((rows, width), tiles.dtype)

        copies[k].start()
    for copy in copies:
        copy.wait()


def gram(partners, own, own_twin, got, got_twin, tok_scale, halves, n):
    tok_rows, width = own.shape
    slots = partners.shape[0]
    rows = width // halves
    return pl.pallas_call(
        functools.partial(gram_kernel, tok_scale, n),
        out_shape=jax.ShapeDtypeStruct((1, slots, rows, width), own.dtype),
        in_specs=[in_smem] + [in_vmem] * 4,
        out_specs=in_hbm,
        scratch_shapes=[
            pltpu.VMEM((slots, rows, width), own.dtype),
            pltpu.SemaphoreType.DMA((slots,)),
        ],
        compiler_params=params,
    )(partners, own, own_twin, got, got_twin)


def hop_of_slot(partners, k, n):
    me = lax.axis_index("lat")
    row = partners[k : k + 1, :]
    mine = lax.broadcasted_iota(jnp.int32, row.shape, 1) == me
    listed = jnp.sum(jnp.where(mine, row, 0))
    hop = lax.rem(place_on_ring(me, n) + n - place_on_ring(jnp.minimum(listed, n - 1), n), n)
    return jnp.where(listed < n, hop, -1)


def tiles_kernel(tok_scale, n, hops, is_first, partners, *refs):
    count = len(hops)
    if is_first:
        own, own_twin, refs = refs[0], refs[1], refs[2:]
        left, refs = refs[-4], refs[:-4] + refs[-3:]
    else:
        left, refs = refs[0], refs[1:]
    blocks, twins = refs[:count], refs[count : 2 * count]
    out, tiles, sems = refs[-3:]
    rows, width = tiles.shape[1:]
    half = rows // 2
    slots = partners.shape[0]
    if is_first:
        columns = pl.ds(pl.multiple_of(lax.axis_index("tok") * rows, rows), rows)
        left[...] = jnp.concatenate([own[:, columns], own_twin[:, columns]], axis=0).T

    slot_hops = [hop_of_slot(partners, k, n) for k in range(1, slots)]
    copies = []

    def send(place, slot, when, pair):
        both = []
        for i in range(2):
            part = pl.ds(i * half, half)
            sem = sems.at[len(copies), i]
            both.append(
                pltpu.make_async_copy(tiles.at[place, part], out.at[0, slot, part], sem)
            )
        copies.append((both, when))

        @pl.when(when)
        def _():
            if pair is not None:
                right = jnp.concatenate([pair[0][...], pair[1][...]], axis=0)
            for i in range(2):
                part = pl.ds(i * half, half)
                if pair is not None:
                    tile = jnp.dot(left[part, :], right, preferred_element_type=jnp.float32)
                    tiles[place, part, :] = (tile * tok_scale).astype(tiles.dtype)
                both[i].start()

    if is_first:
        always = lax.axis_index("lat") >= 0
        send(count, 0, always, (own, own_twin))
        tiles[count + 1] = jnp.zeros((rows, width), tiles.dtype)
        for k, hop in enumerate(slot_hops):
            send(count + 1, k + 1, hop < 0, None)
    for j, hop in enumerate(hops):
        slot = jnp.int32(0)
        for k, h in enumerate(slot_hops):
            slot = jnp.where(h == hop, jnp.int32(k + 1), slot)
        send(j, slot, slot > 0, (blocks[j], twins[j]))
    for both, when in copies:

        @pl.when(when)
        def _():
            for copy in both:
                copy.wait()


def tiles_of(partners, owns, before, hops, blocks, twins, tok_scale, halves, n):
    tok_rows, width = blocks[0].shape
    slots = partners.shape[0]
    rows = width // halves
    first = before is None
    dtype = blocks[0].dtype
    out_shape = jax.ShapeDtypeStruct((1, slots, rows, width), dtype)
    left_shape = jax.ShapeDtypeStruct((rows, tok_rows * halves), dtype)
    if first:
        operands = (partners, *owns, *blocks, *twins)
    else:
        operands = (partners, before[0], *blocks, *twins, before[1])
    specs = [in_vmem] * len(operands)
    done = pl.pallas_call(
        functools.partial(tiles_kernel, tok_scale, n, hops, first),
        out_shape=(left_shape, out_shape) if first else out_shape,
        in_specs=specs if first else specs[:-1] + [in_hbm],
        out_specs=(in_vmem, in_hbm) if first else in_hbm,
        input_output_aliases={} if first else {len(operands) - 1: 0},
        scratch_shapes=[
            pltpu.VMEM((len(hops) + (2 if first else 0), rows, width), dtype),
            pltpu.SemaphoreType.DMA((len(hops) + (slots if first else 0), 2)),
        ],
        compiler_params=params,
        cost_estimate=pl.CostEstimate(
            flops=4 * rows * width * tok_rows * len(hops),
            bytes_accessed=4 * rows * width * len(hops),
            transcendentals=0,
        ),
    )(*operands)
    return done if first else (before[0], done)


def body(residual, enc_weight, enc_bias, threshold, partners):
    n = lax.axis_size("lat")
    halves = lax.axis_size("tok")
    tok_rows = residual.shape[0]
    width = enc_weight.shape[1]
    slots = partners.shape[1]
    tok_scale = 1.0 / (tok_rows * halves)
    swap = [(i, 1 - i) for i in range(2)]
    by_slot = partners.T
    if n == ring_size:
        ring = Ring(n)
        acts = encode_on_ring(residual, enc_weight, enc_bias, threshold, ring)
        acts_twin = lax.ppermute(acts, "tok", swap)

        def add_tiles(before, hops, blocks):
            twins = [lax.ppermute(block, "tok", swap) for block in blocks]
            owns = (acts, acts_twin)
            return tiles_of(by_slot, owns, before, hops, blocks, twins, tok_scale, halves, n)

        def beside_second(ahead, behind):
            return add_tiles(None, (1, n - 1), (ahead, behind))

        def beside_third(ahead, behind, ahead_2, behind_2, _, before):
            return add_tiles(before, (2, n - 2), (ahead_2, behind_2))

        out, *late = ring.gather(acts, beside_second, beside_third)
        ahead, behind, corner, middle = late
        far = jnp.where(on_corner(n), corner, middle)
        out, ahead, behind = lax.optimization_barrier((out, ahead, behind))
        return add_tiles(out, (3, n - 3, n // 2), (ahead, behind, far))[1]
    acts = encode_gathered(residual, enc_weight, enc_bias, threshold)
    acts_twin = lax.ppermute(acts, "tok", swap)
    slices = lax.all_to_all(acts.reshape(n, tok_rows // n, width), "lat", 0, 0)
    outgoing = jnp.take(slices, jnp.minimum(partners[:, 1:], n - 1), axis=0)
    got = lax.all_to_all(outgoing, "lat", 0, 0)
    got = got.transpose(1, 0, 2, 3).reshape(slots - 1, tok_rows, width)
    got_twin = lax.ppermute(got, "tok", swap)
    return gram(by_slot, acts, acts_twin, got, got_twin, tok_scale, halves, n)


def solution(mesh):
    return jax.shard_map(
        body,
        mesh=mesh,
        in_specs=(P(("parts", "tok"), "lat"), P(None, "lat"), P("lat"), P("lat"), P()),
        out_specs=P(("parts", "lat"), None, "tok", None),
        check_vma=False,
    )
```

```python
import functools

import jax
import jax.numpy as jnp
from jax import lax
from jax.experimental import pallas as pl
from jax.experimental.pallas import tpu as pltpu
from jax.sharding import PartitionSpec as P

ramp_width = 0.25
ring_size = 8

in_vmem = pl.BlockSpec(memory_space=pltpu.VMEM)
in_smem = pl.BlockSpec(memory_space=pltpu.SMEM)
in_hbm = pl.BlockSpec(memory_space=pltpu.HBM)
params = pltpu.CompilerParams(vmem_limit_bytes=24 * 1024 * 1024)
streaming_params = pltpu.CompilerParams(vmem_limit_bytes=53000000)

rows_by_rows = (((0,), (0,)), ((), ()))


def place_on_ring(block, n):
    half = block // 2
    return half + (block % 2) * (n - 1 - 2 * half)


def block_at(place, n):
    up = 2 * place
    if isinstance(place, int):
        return up if place < n // 2 else 2 * n - 1 - up
    return jnp.where(place < n // 2, up, 2 * n - 1 - up)


def origin(hop, n):
    me = place_on_ring(lax.axis_index("lat"), n)
    return block_at(lax.rem(me + n - hop, n), n)


def activate(pre_acts, threshold):
    gate = jnp.clip((pre_acts - threshold) / ramp_width + 0.5, 0.0, 1.0)
    return (pre_acts * gate).astype(jnp.bfloat16)


def project(x, w):
    return lax.dot_general(x, w, rows_by_rows, preferred_element_type=jnp.float32)


def on_corner(n):
    return place_on_ring(lax.axis_index("lat"), n) % (n // 2) % (n // 2 - 1) == 0


def first_step(hops, later, *refs):
    xs, (weights, total, kept, blocks, sems) = refs[:-5], refs[-5:]
    n = weights.shape[0]
    copies = [
        pltpu.make_async_copy(weights.at[origin(hop, n)], into.at[j], sems.at[j + base])
        for into, base, some in ((blocks, 0, hops), (kept, len(hops), later))
        for j, hop in enumerate(some)
    ]
    for copy in copies:
        copy.start()
    for j, x in enumerate(xs):
        copies[j].wait()
        part = project(x[...], blocks[j])
        total[...] = part if j == 0 else total[...] + part
    for copy in copies[len(hops) :]:
        copy.wait()


def last_step(x, x_f, x_b, x_corner, x_middle, before, blocks, bias, threshold, acts):
    x_far = jnp.where(on_corner(2 * blocks.shape[0]), x_corner[...], x_middle[...])
    pre_acts = before[...] + bias[...]
    for j, part in enumerate((x[...], x_f[...], x_b[...], x_far)):
        pre_acts = pre_acts + project(part, blocks[j])
    acts[...] = activate(pre_acts, threshold[...])


def cost(rows, depth, width, blocks):
    return pl.CostEstimate(
        flops=2 * rows * depth * width * blocks,
        bytes_accessed=2 * depth * (rows + width) * blocks + 8 * rows * width,
        transcendentals=0,
    )


class Ring:
    def __init__(self, n):
        walk = [block_at(i, n) for i in range(n)]
        self.n = n
        self.forward = [(walk[i], walk[(i + 1) % n]) for i in range(n)]
        self.backward = [(d, s) for s, d in self.forward]
        beside = [(i, n - 1 - i) for i in range(n) if i % 4 in (1, 2)]
        across = [(i, (i + 4) % n) for i in range(n) if i % 4 in (0, 3)]
        aside = [(2 * walk[i] + t, 2 * walk[j] + t) for i, j in beside for t in range(2)]
        stay = [(2 * walk[i] + t, 2 * walk[i] + 1 - t) for i, _ in across for t in range(2)]
        self.beside = aside + stay
        self.across = [(walk[i], walk[j]) for i, j in across + beside]

    def gather(self, x, beside_second=None, beside_third=None):
        ahead = lax.ppermute(x, "lat", self.forward)
        behind = lax.ppermute(x, "lat", self.backward)
        corner = lax.ppermute(x, "lat", self.across)
        ahead_2 = lax.ppermute(ahead, "lat", self.forward)
        behind_2 = lax.ppermute(behind, "lat", self.backward)
        odd = place_on_ring(lax.axis_index("lat"), self.n) % 2 == 1
        middle = lax.ppermute(jnp.where(odd, behind, ahead), ("lat", "tok"), self.beside)
        done = beside_second(ahead, behind) if beside_second else ()
        ahead_2, behind_2, corner, done = lax.optimization_barrier(
            (ahead_2, behind_2, corner, done)
        )
        ahead_3 = lax.ppermute(ahead_2, "lat", self.forward)
        behind_3 = lax.ppermute(behind_2, "lat", self.backward)
        done, middle = lax.optimization_barrier((done, middle))
        done = beside_third(ahead, behind, ahead_2, behind_2, corner, done)
        return done, ahead_3, behind_3, corner, middle


def encode_on_ring(residual, enc_weight, enc_bias, threshold, ring):
    tok_rows, depth = residual.shape
    width = enc_weight.shape[1]
    n = ring.n
    weights = enc_weight.reshape(n, depth, width)

    def beside_third(*blocks):
        blocks = blocks[:4]
        hops, later = (1, -1, 2, -2), (0, 3, -3, n // 2)
        kept = jax.ShapeDtypeStruct((len(later),) + weights.shape[1:], weights.dtype)
        return pl.pallas_call(
            functools.partial(first_step, hops, later),
            out_shape=(jax.ShapeDtypeStruct((tok_rows, width), jnp.float32), kept),
            in_specs=[in_vmem] * len(blocks) + [in_hbm],
            out_specs=(in_vmem, in_vmem),
            scratch_shapes=[
                pltpu.VMEM((len(hops),) + weights.shape[1:], weights.dtype),
                pltpu.SemaphoreType.DMA((len(hops) + len(later),)),
            ],
            compiler_params=streaming_params,
            cost_estimate=cost(tok_rows, depth, width, 4),
        )(*blocks, weights)

    x = residual.T
    (total, kept), ahead, behind, corner, middle = ring.gather(x, beside_third=beside_third)
    return pl.pallas_call(
        last_step,
        out_shape=jax.ShapeDtypeStruct((tok_rows, width), jnp.bfloat16),
        in_specs=[in_vmem] * 9,
        out_specs=in_vmem,
        compiler_params=params,
        cost_estimate=cost(tok_rows, depth, width, 4),
    )(
        x,
        ahead,
        behind,
        corner,
        middle,
        total,
        kept,
        enc_bias.reshape(1, width),
        threshold.reshape(1, width),
    )


def encode_gathered(residual, enc_weight, enc_bias, threshold):
    pre_acts = (
        jnp.dot(
            lax.all_gather(residual, "lat", axis=1, tiled=True),
            enc_weight,
            preferred_element_type=jnp.float32,
        )
        + enc_bias
    )
    return activate(pre_acts, threshold)


def gram_kernel(tok_scale, n, partners, own, own_twin, got, got_twin, out, tiles, sems):
    slots, rows, width = tiles.shape
    me = lax.axis_index("lat")
    columns = pl.ds(pl.multiple_of(lax.axis_index("tok") * rows, rows), rows)
    left = jnp.concatenate([own[:, columns], own_twin[:, columns]], axis=0)

    def tile_of(right, right_twin):
        tile = project(left, jnp.concatenate([right, right_twin], axis=0))
        return (tile * tok_scale).astype(tiles.dtype)

    copies = [pltpu.make_async_copy(tiles.at[k], out.at[0, k], sems.at[k]) for k in range(slots)]
    tiles[0] = tile_of(own[...], own_twin[...])
    copies[0].start()
    for k in range(1, slots):
        live = partners[k, me] < n

        @pl.when(live)
        def _():
            tiles[k] = tile_of(got[k - 1], got_twin[k - 1])

        @pl.when(jnp.logical_not(live))
        def _():
            tiles[k] = jnp.zeros((rows, width), tiles.dtype)

        copies[k].start()
    for copy in copies:
        copy.wait()


def gram(partners, own, own_twin, got, got_twin, tok_scale, halves, n):
    tok_rows, width = own.shape
    slots = partners.shape[0]
    rows = width // halves
    return pl.pallas_call(
        functools.partial(gram_kernel, tok_scale, n),
        out_shape=jax.ShapeDtypeStruct((1, slots, rows, width), own.dtype),
        in_specs=[in_smem] + [in_vmem] * 4,
        out_specs=in_hbm,
        scratch_shapes=[
            pltpu.VMEM((slots, rows, width), own.dtype),
            pltpu.SemaphoreType.DMA((slots,)),
        ],
        compiler_params=params,
    )(partners, own, own_twin, got, got_twin)


def hop_of_slot(partners, k, n):
    me = lax.axis_index("lat")
    row = partners[k : k + 1, :]
    mine = lax.broadcasted_iota(jnp.int32, row.shape, 1) == me
    listed = jnp.sum(jnp.where(mine, row, 0))
    hop = lax.rem(place_on_ring(me, n) + n - place_on_ring(jnp.minimum(listed, n - 1), n), n)
    return jnp.where(listed < n, hop, -1)


def tiles_kernel(tok_scale, n, hops, is_first, partners, *refs):
    count = len(hops)
    if is_first:
        own, own_twin, refs = refs[0], refs[1], refs[2:]
        left, refs = refs[-4], refs[:-4] + refs[-3:]
    else:
        left, refs = refs[0], refs[1:]
    blocks, twins = refs[:count], refs[count : 2 * count]
    out, tiles, sems = refs[-3:]
    rows, width = tiles.shape[1:]
    half = rows // 2
    slots = partners.shape[0]
    if is_first:
        columns = pl.ds(pl.multiple_of(lax.axis_index("tok") * rows, rows), rows)
        left[...] = jnp.concatenate([own[:, columns], own_twin[:, columns]], axis=0).T

    slot_hops = [hop_of_slot(partners, k, n) for k in range(1, slots)]
    copies = []

    def send(place, slot, when, pair):
        both = []
        for i in range(2):
            part = pl.ds(i * half, half)
            sem = sems.at[len(copies), i]
            both.append(
                pltpu.make_async_copy(tiles.at[place, part], out.at[0, slot, part], sem)
            )
        copies.append((both, when))

        @pl.when(when)
        def _():
            if pair is not None:
                right = jnp.concatenate([pair[0][...], pair[1][...]], axis=0)
            for i in range(2):
                part = pl.ds(i * half, half)
                if pair is not None:
                    tile = jnp.dot(left[part, :], right, preferred_element_type=jnp.float32)
                    tiles[place, part, :] = (tile * tok_scale).astype(tiles.dtype)
                both[i].start()

    if is_first:
        always = lax.axis_index("lat") >= 0
        send(count, 0, always, (own, own_twin))
        tiles[count + 1] = jnp.zeros((rows, width), tiles.dtype)
        for k, hop in enumerate(slot_hops):
            send(count + 1, k + 1, hop < 0, None)
    for j, hop in enumerate(hops):
        slot = jnp.int32(0)
        for k, h in enumerate(slot_hops):
            slot = jnp.where(h == hop, jnp.int32(k + 1), slot)
        send(j, slot, slot > 0, (blocks[j], twins[j]))
    for both, when in copies:

        @pl.when(when)
        def _():
            for copy in both:
                copy.wait()


def tiles_of(partners, owns, before, hops, blocks, twins, tok_scale, halves, n):
    first = before is None
    tok_rows, width = owns[0].shape
    slots = partners.shape[0]
    rows = width // halves
    dtype = owns[0].dtype
    out_shape = jax.ShapeDtypeStruct((1, slots, rows, width), dtype)
    left_shape = jax.ShapeDtypeStruct((rows, tok_rows * halves), dtype)
    if first:
        operands = (partners, *owns, *blocks, *twins)
    else:
        operands = (partners, before[0], *blocks, *twins, before[1])
    specs = [in_vmem] * len(operands)
    done = pl.pallas_call(
        functools.partial(tiles_kernel, tok_scale, n, hops, first),
        out_shape=(left_shape, out_shape) if first else out_shape,
        in_specs=specs if first else specs[:-1] + [in_hbm],
        out_specs=(in_vmem, in_hbm) if first else in_hbm,
        input_output_aliases={} if first else {len(operands) - 1: 0},
        scratch_shapes=[
            pltpu.VMEM((len(hops) + (2 if first else 0), rows, width), dtype),
            pltpu.SemaphoreType.DMA((len(hops) + (slots if first else 0), 2)),
        ],
        compiler_params=params,
        cost_estimate=pl.CostEstimate(
            flops=4 * rows * width * tok_rows * len(hops),
            bytes_accessed=4 * rows * width * len(hops),
            transcendentals=0,
        ),
    )(*operands)
    return done if first else (before[0], done)


def body(residual, enc_weight, enc_bias, threshold, partners):
    n = lax.axis_size("lat")
    halves = lax.axis_size("tok")
    tok_rows = residual.shape[0]
    width = enc_weight.shape[1]
    slots = partners.shape[1]
    tok_scale = 1.0 / (tok_rows * halves)
    swap = [(i, 1 - i) for i in range(2)]
    by_slot = partners.T
    if n == ring_size:
        ring = Ring(n)
        acts = encode_on_ring(residual, enc_weight, enc_bias, threshold, ring)
        acts_twin = lax.ppermute(acts, "tok", swap)

        def add_tiles(before, hops, blocks):
            twins = [lax.ppermute(block, "tok", swap) for block in blocks]
            owns = (acts, acts_twin)
            return tiles_of(by_slot, owns, before, hops, blocks, twins, tok_scale, halves, n)

        def beside_second(*_):
            return add_tiles(None, (), ())

        def beside_third(ahead, behind, ahead_2, behind_2, _, before):
            blocks = (ahead, behind, ahead_2, behind_2)
            return add_tiles(before, (1, n - 1, 2, n - 2), blocks)

        out, *late = ring.gather(acts, beside_second, beside_third)
        ahead, behind, corner, middle = late
        far = jnp.where(on_corner(n), corner, middle)
        out, ahead, behind = lax.optimization_barrier((out, ahead, behind))
        return add_tiles(out, (3, n - 3, n // 2), (ahead, behind, far))[1]
    acts = encode_gathered(residual, enc_weight, enc_bias, threshold)
    acts_twin = lax.ppermute(acts, "tok", swap)
    slices = lax.all_to_all(acts.reshape(n, tok_rows // n, width), "lat", 0, 0)
    outgoing = jnp.take(slices, jnp.minimum(partners[:, 1:], n - 1), axis=0)
    got = lax.all_to_all(outgoing, "lat", 0, 0)
    got = got.transpose(1, 0, 2, 3).reshape(slots - 1, tok_rows, width)
    got_twin = lax.ppermute(got, "tok", swap)
    return gram(by_slot, acts, acts_twin, got, got_twin, tok_scale, halves, n)


def solution(mesh):
    return jax.shard_map(
        body,
        mesh=mesh,
        in_specs=(P(("parts", "tok"), "lat"), P(None, "lat"), P("lat"), P("lat"), P()),
        out_specs=P(("parts", "lat"), None, "tok", None),
        check_vma=False,
    )
```

```python
import functools

import jax
import jax.numpy as jnp
from jax import lax
from jax.experimental import pallas as pl
from jax.experimental.pallas import tpu as pltpu
from jax.sharding import PartitionSpec as P

ramp_width = 0.25
ring_size = 8

in_vmem = pl.BlockSpec(memory_space=pltpu.VMEM)
in_smem = pl.BlockSpec(memory_space=pltpu.SMEM)
in_hbm = pl.BlockSpec(memory_space=pltpu.HBM)
params = pltpu.CompilerParams(vmem_limit_bytes=24 * 1024 * 1024)
streaming_params = pltpu.CompilerParams(vmem_limit_bytes=53000000)

rows_by_rows = (((0,), (0,)), ((), ()))


def place_on_ring(block, n):
    half = block // 2
    return half + (block % 2) * (n - 1 - 2 * half)


def block_at(place, n):
    up = 2 * place
    if isinstance(place, int):
        return up if place < n // 2 else 2 * n - 1 - up
    return jnp.where(place < n // 2, up, 2 * n - 1 - up)


def origin(hop, n):
    me = place_on_ring(lax.axis_index("lat"), n)
    return block_at(lax.rem(me + n - hop, n), n)


def activate(pre_acts, threshold):
    gate = jnp.clip((pre_acts - threshold) / ramp_width + 0.5, 0.0, 1.0)
    return (pre_acts * gate).astype(jnp.bfloat16)


def project(x, w):
    return lax.dot_general(x, w, rows_by_rows, preferred_element_type=jnp.float32)


def on_corner(n):
    return place_on_ring(lax.axis_index("lat"), n) % (n // 2) % (n // 2 - 1) == 0


def first_step(hops, later, *refs):
    xs, (weights, total, kept, blocks, sems) = refs[:-5], refs[-5:]
    n = weights.shape[0]
    copies = [
        pltpu.make_async_copy(weights.at[origin(hop, n)], into.at[j], sems.at[j + base])
        for into, base, some in ((blocks, 0, hops), (kept, len(hops), later))
        for j, hop in enumerate(some)
    ]
    for copy in copies:
        copy.start()
    for j, x in enumerate(xs):
        copies[j].wait()
        part = project(x[...], blocks[j])
        total[...] = part if j == 0 else total[...] + part
    for copy in copies[len(hops) :]:
        copy.wait()


def last_step(x, x_f, x_b, x_corner, x_middle, before, blocks, bias, threshold, acts):
    x_far = jnp.where(on_corner(2 * blocks.shape[0]), x_corner[...], x_middle[...])
    pre_acts = before[...] + bias[...]
    for j, part in enumerate((x[...], x_f[...], x_b[...], x_far)):
        pre_acts = pre_acts + project(part, blocks[j])
    acts[...] = activate(pre_acts, threshold[...])


def cost(rows, depth, width, blocks):
    return pl.CostEstimate(
        flops=2 * rows * depth * width * blocks,
        bytes_accessed=2 * depth * (rows + width) * blocks + 8 * rows * width,
        transcendentals=0,
    )


class Ring:
    def __init__(self, n):
        walk = [block_at(i, n) for i in range(n)]
        self.n = n
        self.forward = [(walk[i], walk[(i + 1) % n]) for i in range(n)]
        self.backward = [(d, s) for s, d in self.forward]
        beside = [(i, n - 1 - i) for i in range(n) if i % 4 in (1, 2)]
        across = [(i, (i + 4) % n) for i in range(n) if i % 4 in (0, 3)]
        aside = [(2 * walk[i] + t, 2 * walk[j] + t) for i, j in beside for t in range(2)]
        stay = [(2 * walk[i] + t, 2 * walk[i] + 1 - t) for i, _ in across for t in range(2)]
        self.beside = aside + stay
        self.across = [(walk[i], walk[j]) for i, j in across + beside]

    def gather(self, x, beside_second=None, beside_third=None):
        ahead = lax.ppermute(x, "lat", self.forward)
        behind = lax.ppermute(x, "lat", self.backward)
        corner = lax.ppermute(x, "lat", self.across)
        ahead_2 = lax.ppermute(ahead, "lat", self.forward)
        behind_2 = lax.ppermute(behind, "lat", self.backward)
        odd = place_on_ring(lax.axis_index("lat"), self.n) % 2 == 1
        middle = lax.ppermute(jnp.where(odd, behind, ahead), ("lat", "tok"), self.beside)
        done = beside_second(ahead, behind) if beside_second else ()
        ahead_2, behind_2, corner, done = lax.optimization_barrier(
            (ahead_2, behind_2, corner, done)
        )
        ahead_3 = lax.ppermute(ahead_2, "lat", self.forward)
        behind_3 = lax.ppermute(behind_2, "lat", self.backward)
        done, middle = lax.optimization_barrier((done, middle))
        done = beside_third(ahead, behind, ahead_2, behind_2, corner, done)
        return done, ahead_3, behind_3, corner, middle


def encode_on_ring(residual, enc_weight, enc_bias, threshold, ring):
    tok_rows, depth = residual.shape
    width = enc_weight.shape[1]
    n = ring.n
    weights = enc_weight.reshape(n, depth, width)

    def beside_third(*blocks):
        blocks = blocks[:4]
        hops, later = (1, -1, 2, -2), (0, 3, -3, n // 2)
        kept = jax.ShapeDtypeStruct((len(later),) + weights.shape[1:], weights.dtype)
        return pl.pallas_call(
            functools.partial(first_step, hops, later),
            out_shape=(jax.ShapeDtypeStruct((tok_rows, width), jnp.float32), kept),
            in_specs=[in_vmem] * len(blocks) + [in_hbm],
            out_specs=(in_vmem, in_vmem),
            scratch_shapes=[
                pltpu.VMEM((len(hops),) + weights.shape[1:], weights.dtype),
                pltpu.SemaphoreType.DMA((len(hops) + len(later),)),
            ],
            compiler_params=streaming_params,
            cost_estimate=cost(tok_rows, depth, width, 4),
        )(*blocks, weights)

    x = residual.T
    (total, kept), ahead, behind, corner, middle = ring.gather(x, beside_third=beside_third)
    return pl.pallas_call(
        last_step,
        out_shape=jax.ShapeDtypeStruct((tok_rows, width), jnp.bfloat16),
        in_specs=[in_vmem] * 9,
        out_specs=in_vmem,
        compiler_params=params,
        cost_estimate=cost(tok_rows, depth, width, 4),
    )(
        x,
        ahead,
        behind,
        corner,
        middle,
        total,
        kept,
        enc_bias.reshape(1, width),
        threshold.reshape(1, width),
    )


def encode_gathered(residual, enc_weight, enc_bias, threshold):
    pre_acts = (
        jnp.dot(
            lax.all_gather(residual, "lat", axis=1, tiled=True),
            enc_weight,
            preferred_element_type=jnp.float32,
        )
        + enc_bias
    )
    return activate(pre_acts, threshold)


def gram_kernel(tok_scale, n, partners, own, own_twin, got, got_twin, out, tiles, sems):
    slots, rows, width = tiles.shape
    me = lax.axis_index("lat")
    columns = pl.ds(pl.multiple_of(lax.axis_index("tok") * rows, rows), rows)
    left = jnp.concatenate([own[:, columns], own_twin[:, columns]], axis=0)

    def tile_of(right, right_twin):
        tile = project(left, jnp.concatenate([right, right_twin], axis=0))
        return (tile * tok_scale).astype(tiles.dtype)

    copies = [pltpu.make_async_copy(tiles.at[k], out.at[0, k], sems.at[k]) for k in range(slots)]
    tiles[0] = tile_of(own[...], own_twin[...])
    copies[0].start()
    for k in range(1, slots):
        live = partners[k, me] < n

        @pl.when(live)
        def _():
            tiles[k] = tile_of(got[k - 1], got_twin[k - 1])

        @pl.when(jnp.logical_not(live))
        def _():
            tiles[k] = jnp.zeros((rows, width), tiles.dtype)

        copies[k].start()
    for copy in copies:
        copy.wait()


def gram(partners, own, own_twin, got, got_twin, tok_scale, halves, n):
    tok_rows, width = own.shape
    slots = partners.shape[0]
    rows = width // halves
    return pl.pallas_call(
        functools.partial(gram_kernel, tok_scale, n),
        out_shape=jax.ShapeDtypeStruct((1, slots, rows, width), own.dtype),
        in_specs=[in_smem] + [in_vmem] * 4,
        out_specs=in_hbm,
        scratch_shapes=[
            pltpu.VMEM((slots, rows, width), own.dtype),
            pltpu.SemaphoreType.DMA((slots,)),
        ],
        compiler_params=params,
    )(partners, own, own_twin, got, got_twin)


def hop_of_slot(partners, k, n):
    me = lax.axis_index("lat")
    row = partners[k : k + 1, :]
    mine = lax.broadcasted_iota(jnp.int32, row.shape, 1) == me
    listed = jnp.sum(jnp.where(mine, row, 0))
    hop = lax.rem(place_on_ring(me, n) + n - place_on_ring(jnp.minimum(listed, n - 1), n), n)
    return jnp.where(listed < n, hop, -1)


def tiles_kernel(tok_scale, n, hops, is_first, partners, *refs):
    count = len(hops)
    if is_first:
        own, own_twin, refs = refs[0], refs[1], refs[2:]
        left, refs = refs[-4], refs[:-4] + refs[-3:]
    else:
        left, refs = refs[0], refs[1:]
    blocks, twins = refs[:count], refs[count : 2 * count]
    out, tiles, sems = refs[-3:]
    rows, width = tiles.shape[1:]
    half = rows // 2
    slots = partners.shape[0]
    if is_first:
        columns = pl.ds(pl.multiple_of(lax.axis_index("tok") * rows, rows), rows)
        left[...] = jnp.concatenate([own[:, columns], own_twin[:, columns]], axis=0).T

    slot_hops = [hop_of_slot(partners, k, n) for k in range(1, slots)]
    copies = []

    def send(place, slot, when, pair):
        both = []
        for i in range(2):
            part = pl.ds(i * half, half)
            sem = sems.at[len(copies), i]
            both.append(
                pltpu.make_async_copy(tiles.at[place, part], out.at[0, slot, part], sem)
            )
        copies.append((both, when))

        @pl.when(when)
        def _():
            if pair is not None:
                right = jnp.concatenate([pair[0][...], pair[1][...]], axis=0)
            for i in range(2):
                part = pl.ds(i * half, half)
                if pair is not None:
                    tile = jnp.dot(left[part, :], right, preferred_element_type=jnp.float32)
                    tiles[place, part, :] = (tile * tok_scale).astype(tiles.dtype)
                both[i].start()

    if is_first:
        always = lax.axis_index("lat") >= 0
        send(count, 0, always, (own, own_twin))
        tiles[count + 1] = jnp.zeros((rows, width), tiles.dtype)
        for k, hop in enumerate(slot_hops):
            send(count + 1, k + 1, hop < 0, None)
    for j, hop in enumerate(hops):
        slot = jnp.int32(0)
        for k, h in enumerate(slot_hops):
            slot = jnp.where(h == hop, jnp.int32(k + 1), slot)
        send(j, slot, slot > 0, (blocks[j], twins[j]))
    for both, when in copies:

        @pl.when(when)
        def _():
            for copy in both:
                copy.wait()


def tiles_of(partners, owns, before, hops, blocks, twins, tok_scale, halves, n):
    first = before is None
    tok_rows, width = owns[0].shape
    slots = partners.shape[0]
    rows = width // halves
    dtype = owns[0].dtype
    out_shape = jax.ShapeDtypeStruct((1, slots, rows, width), dtype)
    left_shape = jax.ShapeDtypeStruct((rows, tok_rows * halves), dtype)
    if first:
        operands = (partners, *owns, *blocks, *twins)
    else:
        operands = (partners, before[0], *blocks, *twins, before[1])
    specs = [in_vmem] * len(operands)
    done = pl.pallas_call(
        functools.partial(tiles_kernel, tok_scale, n, hops, first),
        out_shape=(left_shape, out_shape) if first else out_shape,
        in_specs=specs if first else specs[:-1] + [in_hbm],
        out_specs=(in_vmem, in_hbm) if first else in_hbm,
        input_output_aliases={} if first else {len(operands) - 1: 0},
        scratch_shapes=[
            pltpu.VMEM((len(hops) + (2 if first else 0), rows, width), dtype),
            pltpu.SemaphoreType.DMA((len(hops) + (slots if first else 0), 2)),
        ],
        compiler_params=params,
        cost_estimate=pl.CostEstimate(
            flops=4 * rows * width * tok_rows * len(hops),
            bytes_accessed=4 * rows * width * len(hops),
            transcendentals=0,
        ),
    )(*operands)
    return done if first else (before[0], done)


def body(residual, enc_weight, enc_bias, threshold, partners):
    n = lax.axis_size("lat")
    halves = lax.axis_size("tok")
    tok_rows = residual.shape[0]
    width = enc_weight.shape[1]
    slots = partners.shape[1]
    tok_scale = 1.0 / (tok_rows * halves)
    swap = [(i, 1 - i) for i in range(2)]
    by_slot = partners.T
    if n == ring_size:
        ring = Ring(n)
        acts = encode_on_ring(residual, enc_weight, enc_bias, threshold, ring)
        acts_twin = lax.ppermute(acts, "tok", swap)

        def add_tiles(before, hops, blocks):
            twins = [lax.ppermute(block, "tok", swap) for block in blocks]
            owns = (acts, acts_twin)
            return tiles_of(by_slot, owns, before, hops, blocks, twins, tok_scale, halves, n)

        def beside_second(*_):
            return add_tiles(None, (), ())

        def beside_third(ahead, behind, ahead_2, behind_2, _, before):
            blocks = (ahead, behind, ahead_2, behind_2)
            return add_tiles(before, (1, n - 1, 2, n - 2), blocks)

        out, *late = ring.gather(acts, beside_second, beside_third)
        ahead, behind, corner, middle = late
        far = jnp.where(on_corner(n), corner, middle)
        out, ahead = lax.optimization_barrier((out, ahead))
        out = add_tiles(out, (3, n // 2), (ahead, far))
        return add_tiles(out, (n - 3,), (behind,))[1]
    acts = encode_gathered(residual, enc_weight, enc_bias, threshold)
    acts_twin = lax.ppermute(acts, "tok", swap)
    slices = lax.all_to_all(acts.reshape(n, tok_rows // n, width), "lat", 0, 0)
    outgoing = jnp.take(slices, jnp.minimum(partners[:, 1:], n - 1), axis=0)
    got = lax.all_to_all(outgoing, "lat", 0, 0)
    got = got.transpose(1, 0, 2, 3).reshape(slots - 1, tok_rows, width)
    got_twin = lax.ppermute(got, "tok", swap)
    return gram(by_slot, acts, acts_twin, got, got_twin, tok_scale, halves, n)


def solution(mesh):
    return jax.shard_map(
        body,
        mesh=mesh,
        in_specs=(P(("parts", "tok"), "lat"), P(None, "lat"), P("lat"), P("lat"), P()),
        out_specs=P(("parts", "lat"), None, "tok", None),
        check_vma=False,
    )
```

```python
import functools

import jax
import jax.numpy as jnp
from jax import lax
from jax.experimental import pallas as pl
from jax.experimental.pallas import tpu as pltpu
from jax.sharding import PartitionSpec as P

ramp_width = 0.25
ring_size = 8

in_vmem = pl.BlockSpec(memory_space=pltpu.VMEM)
in_smem = pl.BlockSpec(memory_space=pltpu.SMEM)
in_hbm = pl.BlockSpec(memory_space=pltpu.HBM)
params = pltpu.CompilerParams(vmem_limit_bytes=24 * 1024 * 1024)
streaming_params = pltpu.CompilerParams(vmem_limit_bytes=53000000)

rows_by_rows = (((0,), (0,)), ((), ()))


def place_on_ring(block, n):
    half = block // 2
    return half + (block % 2) * (n - 1 - 2 * half)


def block_at(place, n):
    up = 2 * place
    if isinstance(place, int):
        return up if place < n // 2 else 2 * n - 1 - up
    return jnp.where(place < n // 2, up, 2 * n - 1 - up)


def origin(hop, n):
    me = place_on_ring(lax.axis_index("lat"), n)
    return block_at(lax.rem(me + n - hop, n), n)


def activate(pre_acts, threshold):
    gate = jnp.clip((pre_acts - threshold) / ramp_width + 0.5, 0.0, 1.0)
    return (pre_acts * gate).astype(jnp.bfloat16)


def project(x, w):
    return lax.dot_general(x, w, rows_by_rows, preferred_element_type=jnp.float32)


def on_corner(n):
    return place_on_ring(lax.axis_index("lat"), n) % (n // 2) % (n // 2 - 1) == 0


def first_step(hops, later, *refs):
    xs, (weights, total, kept, blocks, sems) = refs[:-5], refs[-5:]
    n = weights.shape[0]
    copies = [
        pltpu.make_async_copy(weights.at[origin(hop, n)], into.at[j], sems.at[j + base])
        for into, base, some in ((blocks, 0, hops), (kept, len(hops), later))
        for j, hop in enumerate(some)
    ]
    for copy in copies:
        copy.start()
    for j, x in enumerate(xs):
        copies[j].wait()
        part = project(x[...], blocks[j])
        total[...] = part if j == 0 else total[...] + part
    for copy in copies[len(hops) :]:
        copy.wait()


def last_step(x, x_f, x_b, x_corner, x_middle, before, blocks, bias, threshold, acts):
    x_far = jnp.where(on_corner(2 * blocks.shape[0]), x_corner[...], x_middle[...])
    pre_acts = before[...] + bias[...]
    for j, part in enumerate((x[...], x_f[...], x_b[...], x_far)):
        pre_acts = pre_acts + project(part, blocks[j])
    acts[...] = activate(pre_acts, threshold[...])


def cost(rows, depth, width, blocks):
    return pl.CostEstimate(
        flops=2 * rows * depth * width * blocks,
        bytes_accessed=2 * depth * (rows + width) * blocks + 8 * rows * width,
        transcendentals=0,
    )


class Ring:
    def __init__(self, n):
        walk = [block_at(i, n) for i in range(n)]
        self.n = n
        self.forward = [(walk[i], walk[(i + 1) % n]) for i in range(n)]
        self.backward = [(d, s) for s, d in self.forward]
        beside = [(i, n - 1 - i) for i in range(n) if i % 4 in (1, 2)]
        across = [(i, (i + 4) % n) for i in range(n) if i % 4 in (0, 3)]
        aside = [(2 * walk[i] + t, 2 * walk[j] + t) for i, j in beside for t in range(2)]
        stay = [(2 * walk[i] + t, 2 * walk[i] + 1 - t) for i, _ in across for t in range(2)]
        self.beside = aside + stay
        self.across = [(walk[i], walk[j]) for i, j in across + beside]

    def gather(self, x, beside_second=None, beside_third=None):
        ahead = lax.ppermute(x, "lat", self.forward)
        behind = lax.ppermute(x, "lat", self.backward)
        corner = lax.ppermute(x, "lat", self.across)
        ahead_2 = lax.ppermute(ahead, "lat", self.forward)
        behind_2 = lax.ppermute(behind, "lat", self.backward)
        odd = place_on_ring(lax.axis_index("lat"), self.n) % 2 == 1
        middle = lax.ppermute(jnp.where(odd, behind, ahead), ("lat", "tok"), self.beside)
        done = beside_second(ahead, behind) if beside_second else ()
        ahead_2, behind_2, corner, done = lax.optimization_barrier(
            (ahead_2, behind_2, corner, done)
        )
        ahead_3 = lax.ppermute(ahead_2, "lat", self.forward)
        behind_3 = lax.ppermute(behind_2, "lat", self.backward)
        done, middle = lax.optimization_barrier((done, middle))
        done = beside_third(ahead, behind, ahead_2, behind_2, corner, done)
        return done, ahead_3, behind_3, corner, middle


def encode_on_ring(residual, enc_weight, enc_bias, threshold, ring):
    tok_rows, depth = residual.shape
    width = enc_weight.shape[1]
    n = ring.n
    weights = enc_weight.reshape(n, depth, width)

    def beside_third(*blocks):
        blocks = blocks[:4]
        hops, later = (1, -1, 2, -2), (0, 3, -3, n // 2)
        kept = jax.ShapeDtypeStruct((len(later),) + weights.shape[1:], weights.dtype)
        return pl.pallas_call(
            functools.partial(first_step, hops, later),
            out_shape=(jax.ShapeDtypeStruct((tok_rows, width), jnp.float32), kept),
            in_specs=[in_vmem] * len(blocks) + [in_hbm],
            out_specs=(in_vmem, in_vmem),
            scratch_shapes=[
                pltpu.VMEM((len(hops),) + weights.shape[1:], weights.dtype),
                pltpu.SemaphoreType.DMA((len(hops) + len(later),)),
            ],
            compiler_params=streaming_params,
            cost_estimate=cost(tok_rows, depth, width, 4),
        )(*blocks, weights)

    x = residual.T
    (total, kept), ahead, behind, corner, middle = ring.gather(x, beside_third=beside_third)
    return pl.pallas_call(
        last_step,
        out_shape=jax.ShapeDtypeStruct((tok_rows, width), jnp.bfloat16),
        in_specs=[in_vmem] * 9,
        out_specs=in_vmem,
        compiler_params=params,
        cost_estimate=cost(tok_rows, depth, width, 4),
    )(
        x,
        ahead,
        behind,
        corner,
        middle,
        total,
        kept,
        enc_bias.reshape(1, width),
        threshold.reshape(1, width),
    )


def encode_gathered(residual, enc_weight, enc_bias, threshold):
    pre_acts = (
        jnp.dot(
            lax.all_gather(residual, "lat", axis=1, tiled=True),
            enc_weight,
            preferred_element_type=jnp.float32,
        )
        + enc_bias
    )
    return activate(pre_acts, threshold)


def gram_kernel(tok_scale, n, partners, own, own_twin, got, got_twin, out, tiles, sems):
    slots, rows, width = tiles.shape
    me = lax.axis_index("lat")
    columns = pl.ds(pl.multiple_of(lax.axis_index("tok") * rows, rows), rows)
    left = jnp.concatenate([own[:, columns], own_twin[:, columns]], axis=0)

    def tile_of(right, right_twin):
        tile = project(left, jnp.concatenate([right, right_twin], axis=0))
        return (tile * tok_scale).astype(tiles.dtype)

    copies = [pltpu.make_async_copy(tiles.at[k], out.at[0, k], sems.at[k]) for k in range(slots)]
    tiles[0] = tile_of(own[...], own_twin[...])
    copies[0].start()
    for k in range(1, slots):
        live = partners[k, me] < n

        @pl.when(live)
        def _():
            tiles[k] = tile_of(got[k - 1], got_twin[k - 1])

        @pl.when(jnp.logical_not(live))
        def _():
            tiles[k] = jnp.zeros((rows, width), tiles.dtype)

        copies[k].start()
    for copy in copies:
        copy.wait()


def gram(partners, own, own_twin, got, got_twin, tok_scale, halves, n):
    tok_rows, width = own.shape
    slots = partners.shape[0]
    rows = width // halves
    return pl.pallas_call(
        functools.partial(gram_kernel, tok_scale, n),
        out_shape=jax.ShapeDtypeStruct((1, slots, rows, width), own.dtype),
        in_specs=[in_smem] + [in_vmem] * 4,
        out_specs=in_hbm,
        scratch_shapes=[
            pltpu.VMEM((slots, rows, width), own.dtype),
            pltpu.SemaphoreType.DMA((slots,)),
        ],
        compiler_params=params,
    )(partners, own, own_twin, got, got_twin)


def hop_of_slot(partners, k, n):
    me = lax.axis_index("lat")
    row = partners[k : k + 1, :]
    mine = lax.broadcasted_iota(jnp.int32, row.shape, 1) == me
    listed = jnp.sum(jnp.where(mine, row, 0))
    hop = lax.rem(place_on_ring(me, n) + n - place_on_ring(jnp.minimum(listed, n - 1), n), n)
    return jnp.where(listed < n, hop, -1)


def tiles_kernel(tok_scale, n, hops, is_first, partners, *refs):
    count = len(hops)
    if is_first:
        own, own_twin, refs = refs[0], refs[1], refs[2:]
        left, refs = refs[-4], refs[:-4] + refs[-3:]
    else:
        left, refs = refs[0], refs[1:]
    blocks, twins = refs[:count], refs[count : 2 * count]
    out, tiles, sems = refs[-3:]
    rows, width = tiles.shape[1:]
    half = rows // 2
    slots = partners.shape[0]
    if is_first:
        columns = pl.ds(pl.multiple_of(lax.axis_index("tok") * rows, rows), rows)
        left[...] = jnp.concatenate([own[:, columns], own_twin[:, columns]], axis=0).T

    slot_hops = [hop_of_slot(partners, k, n) for k in range(1, slots)]
    copies = []

    def send(place, slot, when, pair):
        both = []
        for i in range(2):
            part = pl.ds(i * half, half)
            sem = sems.at[len(copies), i]
            both.append(
                pltpu.make_async_copy(tiles.at[place, part], out.at[0, slot, part], sem)
            )
        copies.append((both, when))

        @pl.when(when)
        def _():
            if pair is not None:
                right = jnp.concatenate([pair[0][...], pair[1][...]], axis=0)
            for i in range(2):
                part = pl.ds(i * half, half)
                if pair is not None:
                    tile = jnp.dot(left[part, :], right, preferred_element_type=jnp.float32)
                    tiles[place, part, :] = (tile * tok_scale).astype(tiles.dtype)
                both[i].start()

    if is_first:
        always = lax.axis_index("lat") >= 0
        send(count, 0, always, (own, own_twin))
        tiles[count + 1] = jnp.zeros((rows, width), tiles.dtype)
        for k, hop in enumerate(slot_hops):
            send(count + 1, k + 1, hop < 0, None)
    for j, hop in enumerate(hops):
        slot = jnp.int32(0)
        for k, h in enumerate(slot_hops):
            slot = jnp.where(h == hop, jnp.int32(k + 1), slot)
        send(j, slot, slot > 0, (blocks[j], twins[j]))
    for both, when in copies:

        @pl.when(when)
        def _():
            for copy in both:
                copy.wait()


def tiles_of(partners, owns, before, hops, blocks, twins, tok_scale, halves, n):
    first = before is None
    tok_rows, width = owns[0].shape
    slots = partners.shape[0]
    rows = width // halves
    dtype = owns[0].dtype
    out_shape = jax.ShapeDtypeStruct((1, slots, rows, width), dtype)
    left_shape = jax.ShapeDtypeStruct((rows, tok_rows * halves), dtype)
    if first:
        operands = (partners, *owns, *blocks, *twins)
    else:
        operands = (partners, before[0], *blocks, *twins, before[1])
    specs = [in_vmem] * len(operands)
    done = pl.pallas_call(
        functools.partial(tiles_kernel, tok_scale, n, hops, first),
        out_shape=(left_shape, out_shape) if first else out_shape,
        in_specs=specs if first else specs[:-1] + [in_hbm],
        out_specs=(in_vmem, in_hbm) if first else in_hbm,
        input_output_aliases={} if first else {len(operands) - 1: 0},
        scratch_shapes=[
            pltpu.VMEM((len(hops) + (2 if first else 0), rows, width), dtype),
            pltpu.SemaphoreType.DMA((len(hops) + (slots if first else 0), 2)),
        ],
        compiler_params=params,
        cost_estimate=pl.CostEstimate(
            flops=4 * rows * width * tok_rows * len(hops),
            bytes_accessed=4 * rows * width * len(hops),
            transcendentals=0,
        ),
    )(*operands)
    return done if first else (before[0], done)


def body(residual, enc_weight, enc_bias, threshold, partners):
    n = lax.axis_size("lat")
    halves = lax.axis_size("tok")
    tok_rows = residual.shape[0]
    width = enc_weight.shape[1]
    slots = partners.shape[1]
    tok_scale = 1.0 / (tok_rows * halves)
    swap = [(i, 1 - i) for i in range(2)]
    by_slot = partners.T
    if n == ring_size:
        ring = Ring(n)
        acts = encode_on_ring(residual, enc_weight, enc_bias, threshold, ring)
        acts_twin = lax.ppermute(acts, "tok", swap)

        def add_tiles(before, hops, blocks):
            twins = [lax.ppermute(block, "tok", swap) for block in blocks]
            owns = (acts, acts_twin)
            return tiles_of(by_slot, owns, before, hops, blocks, twins, tok_scale, halves, n)

        def beside_second(*_):
            return add_tiles(None, (), ())

        def beside_third(ahead, behind, ahead_2, behind_2, _, before):
            blocks = (ahead, behind, ahead_2, behind_2)
            return add_tiles(before, (1, n - 1, 2, n - 2), blocks)

        out, *late = ring.gather(acts, beside_second, beside_third)
        ahead, behind, corner, middle = late
        far = jnp.where(on_corner(n), corner, middle)
        out = add_tiles(out, (n // 2,), (far,))
        out, ahead = lax.optimization_barrier((out, ahead))
        out = add_tiles(out, (3,), (ahead,))
        return add_tiles(out, (n - 3,), (behind,))[1]
    acts = encode_gathered(residual, enc_weight, enc_bias, threshold)
    acts_twin = lax.ppermute(acts, "tok", swap)
    slices = lax.all_to_all(acts.reshape(n, tok_rows // n, width), "lat", 0, 0)
    outgoing = jnp.take(slices, jnp.minimum(partners[:, 1:], n - 1), axis=0)
    got = lax.all_to_all(outgoing, "lat", 0, 0)
    got = got.transpose(1, 0, 2, 3).reshape(slots - 1, tok_rows, width)
    got_twin = lax.ppermute(got, "tok", swap)
    return gram(by_slot, acts, acts_twin, got, got_twin, tok_scale, halves, n)


def solution(mesh):
    return jax.shard_map(
        body,
        mesh=mesh,
        in_specs=(P(("parts", "tok"), "lat"), P(None, "lat"), P("lat"), P("lat"), P()),
        out_specs=P(("parts", "lat"), None, "tok", None),
        check_vma=False,
    )
```

```python
import functools

import jax
import jax.numpy as jnp
from jax import lax
from jax.experimental import pallas as pl
from jax.experimental.pallas import tpu as pltpu
from jax.sharding import PartitionSpec as P

ramp_width = 0.25
ring_size = 8

in_vmem = pl.BlockSpec(memory_space=pltpu.VMEM)
in_smem = pl.BlockSpec(memory_space=pltpu.SMEM)
in_hbm = pl.BlockSpec(memory_space=pltpu.HBM)
params = pltpu.CompilerParams(vmem_limit_bytes=24 * 1024 * 1024)
streaming_params = pltpu.CompilerParams(vmem_limit_bytes=53000000)

rows_by_rows = (((0,), (0,)), ((), ()))


def place_on_ring(block, n):
    half = block // 2
    return half + (block % 2) * (n - 1 - 2 * half)


def block_at(place, n):
    up = 2 * place
    if isinstance(place, int):
        return up if place < n // 2 else 2 * n - 1 - up
    return jnp.where(place < n // 2, up, 2 * n - 1 - up)


def origin(hop, n):
    me = place_on_ring(lax.axis_index("lat"), n)
    return block_at(lax.rem(me + n - hop, n), n)


def activate(pre_acts, threshold):
    gate = jnp.clip((pre_acts - threshold) / ramp_width + 0.5, 0.0, 1.0)
    return (pre_acts * gate).astype(jnp.bfloat16)


def project(x, w):
    return lax.dot_general(x, w, rows_by_rows, preferred_element_type=jnp.float32)


def on_corner(n):
    return place_on_ring(lax.axis_index("lat"), n) % (n // 2) % (n // 2 - 1) == 0


def first_step(hops, later, *refs):
    xs, (weights, total, kept, blocks, sems) = refs[:-5], refs[-5:]
    n = weights.shape[0]
    copies = [
        pltpu.make_async_copy(weights.at[origin(hop, n)], into.at[j], sems.at[j + base])
        for into, base, some in ((blocks, 0, hops), (kept, len(hops), later))
        for j, hop in enumerate(some)
    ]
    for copy in copies:
        copy.start()
    for j, x in enumerate(xs):
        copies[j].wait()
        part = project(x[...], blocks[j])
        total[...] = part if j == 0 else total[...] + part
    for copy in copies[len(hops) :]:
        copy.wait()


def last_step(x, x_f, x_b, x_corner, x_middle, before, blocks, bias, threshold, acts):
    x_far = jnp.where(on_corner(2 * blocks.shape[0]), x_corner[...], x_middle[...])
    pre_acts = before[...] + bias[...]
    for j, part in enumerate((x[...], x_f[...], x_b[...], x_far)):
        pre_acts = pre_acts + project(part, blocks[j])
    acts[...] = activate(pre_acts, threshold[...])


def cost(rows, depth, width, blocks):
    return pl.CostEstimate(
        flops=2 * rows * depth * width * blocks,
        bytes_accessed=2 * depth * (rows + width) * blocks + 8 * rows * width,
        transcendentals=0,
    )


class Ring:
    def __init__(self, n):
        walk = [block_at(i, n) for i in range(n)]
        self.n = n
        self.forward = [(walk[i], walk[(i + 1) % n]) for i in range(n)]
        self.backward = [(d, s) for s, d in self.forward]
        beside = [(i, n - 1 - i) for i in range(n) if i % 4 in (1, 2)]
        across = [(i, (i + 4) % n) for i in range(n) if i % 4 in (0, 3)]
        aside = [(2 * walk[i] + t, 2 * walk[j] + t) for i, j in beside for t in range(2)]
        stay = [(2 * walk[i] + t, 2 * walk[i] + 1 - t) for i, _ in across for t in range(2)]
        self.beside = aside + stay
        self.across = [(walk[i], walk[j]) for i, j in across + beside]

    def gather(self, x, beside_second=None, beside_third=None):
        ahead = lax.ppermute(x, "lat", self.forward)
        behind = lax.ppermute(x, "lat", self.backward)
        corner = lax.ppermute(x, "lat", self.across)
        ahead_2 = lax.ppermute(ahead, "lat", self.forward)
        behind_2 = lax.ppermute(behind, "lat", self.backward)
        odd = place_on_ring(lax.axis_index("lat"), self.n) % 2 == 1
        middle = lax.ppermute(jnp.where(odd, behind, ahead), ("lat", "tok"), self.beside)
        done = beside_second(ahead, behind) if beside_second else ()
        ahead_2, behind_2, corner, done = lax.optimization_barrier(
            (ahead_2, behind_2, corner, done)
        )
        ahead_3 = lax.ppermute(ahead_2, "lat", self.forward)
        behind_3 = lax.ppermute(behind_2, "lat", self.backward)
        done, middle = lax.optimization_barrier((done, middle))
        done = beside_third(ahead, behind, ahead_2, behind_2, corner, done)
        return done, ahead_3, behind_3, corner, middle


def encode_on_ring(residual, enc_weight, enc_bias, threshold, ring):
    tok_rows, depth = residual.shape
    width = enc_weight.shape[1]
    n = ring.n
    weights = enc_weight.reshape(n, depth, width)

    def beside_third(*blocks):
        blocks = blocks[:4]
        hops, later = (1, -1, 2, -2), (0, 3, -3, n // 2)
        kept = jax.ShapeDtypeStruct((len(later),) + weights.shape[1:], weights.dtype)
        return pl.pallas_call(
            functools.partial(first_step, hops, later),
            out_shape=(jax.ShapeDtypeStruct((tok_rows, width), jnp.float32), kept),
            in_specs=[in_vmem] * len(blocks) + [in_hbm],
            out_specs=(in_vmem, in_vmem),
            scratch_shapes=[
                pltpu.VMEM((len(hops),) + weights.shape[1:], weights.dtype),
                pltpu.SemaphoreType.DMA((len(hops) + len(later),)),
            ],
            compiler_params=streaming_params,
            cost_estimate=cost(tok_rows, depth, width, 4),
        )(*blocks, weights)

    x = residual.T
    (total, kept), ahead, behind, corner, middle = ring.gather(x, beside_third=beside_third)
    return pl.pallas_call(
        last_step,
        out_shape=jax.ShapeDtypeStruct((tok_rows, width), jnp.bfloat16),
        in_specs=[in_vmem] * 9,
        out_specs=in_vmem,
        compiler_params=params,
        cost_estimate=cost(tok_rows, depth, width, 4),
    )(
        x,
        ahead,
        behind,
        corner,
        middle,
        total,
        kept,
        enc_bias.reshape(1, width),
        threshold.reshape(1, width),
    )


def encode_gathered(residual, enc_weight, enc_bias, threshold):
    pre_acts = (
        jnp.dot(
            lax.all_gather(residual, "lat", axis=1, tiled=True),
            enc_weight,
            preferred_element_type=jnp.float32,
        )
        + enc_bias
    )
    return activate(pre_acts, threshold)


def gram_kernel(tok_scale, n, partners, own, own_twin, got, got_twin, out, tiles, sems):
    slots, rows, width = tiles.shape
    me = lax.axis_index("lat")
    columns = pl.ds(pl.multiple_of(lax.axis_index("tok") * rows, rows), rows)
    left = jnp.concatenate([own[:, columns], own_twin[:, columns]], axis=0)

    def tile_of(right, right_twin):
        tile = project(left, jnp.concatenate([right, right_twin], axis=0))
        return (tile * tok_scale).astype(tiles.dtype)

    copies = [pltpu.make_async_copy(tiles.at[k], out.at[0, k], sems.at[k]) for k in range(slots)]
    tiles[0] = tile_of(own[...], own_twin[...])
    copies[0].start()
    for k in range(1, slots):
        live = partners[k, me] < n

        @pl.when(live)
        def _():
            tiles[k] = tile_of(got[k - 1], got_twin[k - 1])

        @pl.when(jnp.logical_not(live))
        def _():
            tiles[k] = jnp.zeros((rows, width), tiles.dtype)

        copies[k].start()
    for copy in copies:
        copy.wait()


def gram(partners, own, own_twin, got, got_twin, tok_scale, halves, n):
    tok_rows, width = own.shape
    slots = partners.shape[0]
    rows = width // halves
    return pl.pallas_call(
        functools.partial(gram_kernel, tok_scale, n),
        out_shape=jax.ShapeDtypeStruct((1, slots, rows, width), own.dtype),
        in_specs=[in_smem] + [in_vmem] * 4,
        out_specs=in_hbm,
        scratch_shapes=[
            pltpu.VMEM((slots, rows, width), own.dtype),
            pltpu.SemaphoreType.DMA((slots,)),
        ],
        compiler_params=params,
    )(partners, own, own_twin, got, got_twin)


def hop_of_slot(partners, k, n):
    me = lax.axis_index("lat")
    row = partners[k : k + 1, :]
    mine = lax.broadcasted_iota(jnp.int32, row.shape, 1) == me
    listed = jnp.sum(jnp.where(mine, row, 0))
    hop = lax.rem(place_on_ring(me, n) + n - place_on_ring(jnp.minimum(listed, n - 1), n), n)
    return jnp.where(listed < n, hop, -1)


def tiles_kernel(tok_scale, n, hops, is_first, partners, *refs):
    count = len(hops)
    if is_first:
        own, own_twin, refs = refs[0], refs[1], refs[2:]
        left, refs = refs[-4], refs[:-4] + refs[-3:]
    else:
        left, refs = refs[0], refs[1:]
    blocks, twins = refs[:count], refs[count : 2 * count]
    out, tiles, sems = refs[-3:]
    rows, width = tiles.shape[1:]
    half = rows // 2
    slots = partners.shape[0]
    if is_first:
        columns = pl.ds(pl.multiple_of(lax.axis_index("tok") * rows, rows), rows)
        left[...] = jnp.concatenate([own[:, columns], own_twin[:, columns]], axis=0).T

    slot_hops = [hop_of_slot(partners, k, n) for k in range(1, slots)]
    copies = []

    def send(place, slot, when, pair):
        both = []
        for i in range(2):
            part = pl.ds(i * half, half)
            sem = sems.at[len(copies), i]
            both.append(
                pltpu.make_async_copy(tiles.at[place, part], out.at[0, slot, part], sem)
            )
        copies.append((both, when))

        @pl.when(when)
        def _():
            if pair is not None:
                right = jnp.concatenate([pair[0][...], pair[1][...]], axis=0)
            for i in range(2):
                part = pl.ds(i * half, half)
                if pair is not None:
                    tile = jnp.dot(left[part, :], right, preferred_element_type=jnp.float32)
                    tiles[place, part, :] = (tile * tok_scale).astype(tiles.dtype)
                both[i].start()

    if is_first:
        always = lax.axis_index("lat") >= 0
        send(count, 0, always, (own, own_twin))
        tiles[count + 1] = jnp.zeros((rows, width), tiles.dtype)
        for k, hop in enumerate(slot_hops):
            send(count + 1, k + 1, hop < 0, None)
    for j, hop in enumerate(hops):
        slot = jnp.int32(0)
        for k, h in enumerate(slot_hops):
            slot = jnp.where(h == hop, jnp.int32(k + 1), slot)
        send(j, slot, slot > 0, (blocks[j], twins[j]))
    for both, when in copies:

        @pl.when(when)
        def _():
            for copy in both:
                copy.wait()


def tiles_of(partners, owns, before, hops, blocks, twins, tok_scale, halves, n):
    first = before is None
    tok_rows, width = owns[0].shape
    slots = partners.shape[0]
    rows = width // halves
    dtype = owns[0].dtype
    out_shape = jax.ShapeDtypeStruct((1, slots, rows, width), dtype)
    left_shape = jax.ShapeDtypeStruct((rows, tok_rows * halves), dtype)
    if first:
        operands = (partners, *owns, *blocks, *twins)
    else:
        operands = (partners, before[0], *blocks, *twins, before[1])
    specs = [in_vmem] * len(operands)
    done = pl.pallas_call(
        functools.partial(tiles_kernel, tok_scale, n, hops, first),
        out_shape=(left_shape, out_shape) if first else out_shape,
        in_specs=specs if first else specs[:-1] + [in_hbm],
        out_specs=(in_vmem, in_hbm) if first else in_hbm,
        input_output_aliases={} if first else {len(operands) - 1: 0},
        scratch_shapes=[
            pltpu.VMEM((len(hops) + (2 if first else 0), rows, width), dtype),
            pltpu.SemaphoreType.DMA((len(hops) + (slots if first else 0), 2)),
        ],
        compiler_params=params,
        cost_estimate=pl.CostEstimate(
            flops=4 * rows * width * tok_rows * len(hops),
            bytes_accessed=4 * rows * width * len(hops),
            transcendentals=0,
        ),
    )(*operands)
    return done if first else (before[0], done)


def body(residual, enc_weight, enc_bias, threshold, partners):
    n = lax.axis_size("lat")
    halves = lax.axis_size("tok")
    tok_rows = residual.shape[0]
    width = enc_weight.shape[1]
    slots = partners.shape[1]
    tok_scale = 1.0 / (tok_rows * halves)
    swap = [(i, 1 - i) for i in range(2)]
    by_slot = partners.T
    if n == ring_size:
        ring = Ring(n)
        acts = encode_on_ring(residual, enc_weight, enc_bias, threshold, ring)
        acts_twin = lax.ppermute(acts, "tok", swap)

        def add_tiles(before, hops, blocks):
            twins = [lax.ppermute(block, "tok", swap) for block in blocks]
            owns = (acts, acts_twin)
            return tiles_of(by_slot, owns, before, hops, blocks, twins, tok_scale, halves, n)

        def beside_second(*_):
            return add_tiles(None, (), ())

        def beside_third(ahead, behind, ahead_2, behind_2, _, before):
            blocks = (ahead, behind, ahead_2, behind_2)
            return add_tiles(before, (1, n - 1, 2, n - 2), blocks)

        out, *late = ring.gather(acts, beside_second, beside_third)
        ahead, behind, corner, middle = late
        far = jnp.where(on_corner(n), corner, middle)
        out = add_tiles(out, (3, n // 2), (ahead, far))
        return add_tiles(out, (n - 3,), (behind,))[1]
    acts = encode_gathered(residual, enc_weight, enc_bias, threshold)
    acts_twin = lax.ppermute(acts, "tok", swap)
    slices = lax.all_to_all(acts.reshape(n, tok_rows // n, width), "lat", 0, 0)
    outgoing = jnp.take(slices, jnp.minimum(partners[:, 1:], n - 1), axis=0)
    got = lax.all_to_all(outgoing, "lat", 0, 0)
    got = got.transpose(1, 0, 2, 3).reshape(slots - 1, tok_rows, width)
    got_twin = lax.ppermute(got, "tok", swap)
    return gram(by_slot, acts, acts_twin, got, got_twin, tok_scale, halves, n)


def solution(mesh):
    return jax.shard_map(
        body,
        mesh=mesh,
        in_specs=(P(("parts", "tok"), "lat"), P(None, "lat"), P("lat"), P("lat"), P()),
        out_specs=P(("parts", "lat"), None, "tok", None),
        check_vma=False,
    )
```

```python
import functools

import jax
import jax.numpy as jnp
from jax import lax
from jax.experimental import pallas as pl
from jax.experimental.pallas import tpu as pltpu
from jax.sharding import PartitionSpec as P

ramp_width = 0.25
ring_size = 8

in_vmem = pl.BlockSpec(memory_space=pltpu.VMEM)
in_smem = pl.BlockSpec(memory_space=pltpu.SMEM)
in_hbm = pl.BlockSpec(memory_space=pltpu.HBM)
params = pltpu.CompilerParams(vmem_limit_bytes=24 * 1024 * 1024)
streaming_params = pltpu.CompilerParams(vmem_limit_bytes=53000000)

rows_by_rows = (((0,), (0,)), ((), ()))


def place_on_ring(block, n):
    half = block // 2
    return half + (block % 2) * (n - 1 - 2 * half)


def block_at(place, n):
    up = 2 * place
    if isinstance(place, int):
        return up if place < n // 2 else 2 * n - 1 - up
    return jnp.where(place < n // 2, up, 2 * n - 1 - up)


def origin(hop, n):
    me = place_on_ring(lax.axis_index("lat"), n)
    return block_at(lax.rem(me + n - hop, n), n)


def activate(pre_acts, threshold):
    gate = jnp.clip((pre_acts - threshold) / ramp_width + 0.5, 0.0, 1.0)
    return (pre_acts * gate).astype(jnp.bfloat16)


def project(x, w):
    return lax.dot_general(x, w, rows_by_rows, preferred_element_type=jnp.float32)


def on_corner(n):
    return place_on_ring(lax.axis_index("lat"), n) % (n // 2) % (n // 2 - 1) == 0


def first_step(hops, later, *refs):
    xs, (weights, total, kept, blocks, sems) = refs[:-5], refs[-5:]
    n = weights.shape[0]
    copies = [
        pltpu.make_async_copy(weights.at[origin(hop, n)], into.at[j], sems.at[j + base])
        for into, base, some in ((blocks, 0, hops), (kept, len(hops), later))
        for j, hop in enumerate(some)
    ]
    for copy in copies:
        copy.start()
    for j, x in enumerate(xs):
        copies[j].wait()
        part = project(x[...], blocks[j])
        total[...] = part if j == 0 else total[...] + part
    for copy in copies[len(hops) :]:
        copy.wait()


def last_step(x, x_f, x_b, x_corner, x_middle, before, blocks, bias, threshold, acts):
    x_far = jnp.where(on_corner(2 * blocks.shape[0]), x_corner[...], x_middle[...])
    pre_acts = before[...] + bias[...]
    for j, part in enumerate((x[...], x_f[...], x_b[...], x_far)):
        pre_acts = pre_acts + project(part, blocks[j])
    acts[...] = activate(pre_acts, threshold[...])


def cost(rows, depth, width, blocks):
    return pl.CostEstimate(
        flops=2 * rows * depth * width * blocks,
        bytes_accessed=2 * depth * (rows + width) * blocks + 8 * rows * width,
        transcendentals=0,
    )


class Ring:
    def __init__(self, n):
        walk = [block_at(i, n) for i in range(n)]
        self.n = n
        self.forward = [(walk[i], walk[(i + 1) % n]) for i in range(n)]
        self.backward = [(d, s) for s, d in self.forward]
        beside = [(i, n - 1 - i) for i in range(n) if i % 4 in (1, 2)]
        across = [(i, (i + 4) % n) for i in range(n) if i % 4 in (0, 3)]
        aside = [(2 * walk[i] + t, 2 * walk[j] + t) for i, j in beside for t in range(2)]
        stay = [(2 * walk[i] + t, 2 * walk[i] + 1 - t) for i, _ in across for t in range(2)]
        self.beside = aside + stay
        self.across = [(walk[i], walk[j]) for i, j in across + beside]

    def gather(self, x, beside_second=None, beside_third=None):
        ahead = lax.ppermute(x, "lat", self.forward)
        behind = lax.ppermute(x, "lat", self.backward)
        corner = lax.ppermute(x, "lat", self.across)
        ahead_2 = lax.ppermute(ahead, "lat", self.forward)
        behind_2 = lax.ppermute(behind, "lat", self.backward)
        odd = place_on_ring(lax.axis_index("lat"), self.n) % 2 == 1
        middle = lax.ppermute(jnp.where(odd, behind, ahead), ("lat", "tok"), self.beside)
        done = beside_second(ahead, behind) if beside_second else ()
        ahead_2, behind_2, corner, done = lax.optimization_barrier(
            (ahead_2, behind_2, corner, done)
        )
        ahead_3 = lax.ppermute(ahead_2, "lat", self.forward)
        behind_3 = lax.ppermute(behind_2, "lat", self.backward)
        done, middle = lax.optimization_barrier((done, middle))
        done = beside_third(ahead, behind, ahead_2, behind_2, corner, done)
        return done, ahead_3, behind_3, corner, middle


def encode_on_ring(residual, enc_weight, enc_bias, threshold, ring):
    tok_rows, depth = residual.shape
    width = enc_weight.shape[1]
    n = ring.n
    weights = enc_weight.reshape(n, depth, width)

    def beside_third(*blocks):
        blocks = blocks[:4]
        hops, later = (1, -1, 2, -2), (0, 3, -3, n // 2)
        kept = jax.ShapeDtypeStruct((len(later),) + weights.shape[1:], weights.dtype)
        return pl.pallas_call(
            functools.partial(first_step, hops, later),
            out_shape=(jax.ShapeDtypeStruct((tok_rows, width), jnp.float32), kept),
            in_specs=[in_vmem] * len(blocks) + [in_hbm],
            out_specs=(in_vmem, in_vmem),
            scratch_shapes=[
                pltpu.VMEM((len(hops),) + weights.shape[1:], weights.dtype),
                pltpu.SemaphoreType.DMA((len(hops) + len(later),)),
            ],
            compiler_params=streaming_params,
            cost_estimate=cost(tok_rows, depth, width, 4),
        )(*blocks, weights)

    x = residual.T
    (total, kept), ahead, behind, corner, middle = ring.gather(x, beside_third=beside_third)
    return pl.pallas_call(
        last_step,
        out_shape=jax.ShapeDtypeStruct((tok_rows, width), jnp.bfloat16),
        in_specs=[in_vmem] * 9,
        out_specs=in_vmem,
        compiler_params=params,
        cost_estimate=cost(tok_rows, depth, width, 4),
    )(
        x,
        ahead,
        behind,
        corner,
        middle,
        total,
        kept,
        enc_bias.reshape(1, width),
        threshold.reshape(1, width),
    )


def encode_gathered(residual, enc_weight, enc_bias, threshold):
    pre_acts = (
        jnp.dot(
            lax.all_gather(residual, "lat", axis=1, tiled=True),
            enc_weight,
            preferred_element_type=jnp.float32,
        )
        + enc_bias
    )
    return activate(pre_acts, threshold)


def gram_kernel(tok_scale, n, partners, own, own_twin, got, got_twin, out, tiles, sems):
    slots, rows, width = tiles.shape
    me = lax.axis_index("lat")
    columns = pl.ds(pl.multiple_of(lax.axis_index("tok") * rows, rows), rows)
    left = jnp.concatenate([own[:, columns], own_twin[:, columns]], axis=0)

    def tile_of(right, right_twin):
        tile = project(left, jnp.concatenate([right, right_twin], axis=0))
        return (tile * tok_scale).astype(tiles.dtype)

    copies = [pltpu.make_async_copy(tiles.at[k], out.at[0, k], sems.at[k]) for k in range(slots)]
    tiles[0] = tile_of(own[...], own_twin[...])
    copies[0].start()
    for k in range(1, slots):
        live = partners[k, me] < n

        @pl.when(live)
        def _():
            tiles[k] = tile_of(got[k - 1], got_twin[k - 1])

        @pl.when(jnp.logical_not(live))
        def _():
            tiles[k] = jnp.zeros((rows, width), tiles.dtype)

        copies[k].start()
    for copy in copies:
        copy.wait()


def gram(partners, own, own_twin, got, got_twin, tok_scale, halves, n):
    tok_rows, width = own.shape
    slots = partners.shape[0]
    rows = width // halves
    return pl.pallas_call(
        functools.partial(gram_kernel, tok_scale, n),
        out_shape=jax.ShapeDtypeStruct((1, slots, rows, width), own.dtype),
        in_specs=[in_smem] + [in_vmem] * 4,
        out_specs=in_hbm,
        scratch_shapes=[
            pltpu.VMEM((slots, rows, width), own.dtype),
            pltpu.SemaphoreType.DMA((slots,)),
        ],
        compiler_params=params,
    )(partners, own, own_twin, got, got_twin)


def hop_of_slot(partners, k, n):
    me = lax.axis_index("lat")
    row = partners[k : k + 1, :]
    mine = lax.broadcasted_iota(jnp.int32, row.shape, 1) == me
    listed = jnp.sum(jnp.where(mine, row, 0))
    hop = lax.rem(place_on_ring(me, n) + n - place_on_ring(jnp.minimum(listed, n - 1), n), n)
    return jnp.where(listed < n, hop, -1)


def tiles_kernel(tok_scale, n, hops, is_first, partners, *refs):
    count = len(hops)
    if is_first:
        own, own_twin, refs = refs[0], refs[1], refs[2:]
        left, refs = refs[-4], refs[:-4] + refs[-3:]
    else:
        left, refs = refs[0], refs[1:]
    blocks, twins = refs[:count], refs[count : 2 * count]
    out, tiles, sems = refs[-3:]
    rows, width = tiles.shape[1:]
    half = rows
    slots = partners.shape[0]
    if is_first:
        columns = pl.ds(pl.multiple_of(lax.axis_index("tok") * rows, rows), rows)
        left[...] = jnp.concatenate([own[:, columns], own_twin[:, columns]], axis=0).T

    slot_hops = [hop_of_slot(partners, k, n) for k in range(1, slots)]
    copies = []

    def send(place, slot, when, pair):
        both = []
        for i in range(1):
            part = pl.ds(i * half, half)
            sem = sems.at[len(copies), i]
            both.append(
                pltpu.make_async_copy(tiles.at[place, part], out.at[0, slot, part], sem)
            )
        copies.append((both, when))

        @pl.when(when)
        def _():
            if pair is not None:
                right = jnp.concatenate([pair[0][...], pair[1][...]], axis=0)
            for i in range(1):
                part = pl.ds(i * half, half)
                if pair is not None:
                    tile = jnp.dot(left[part, :], right, preferred_element_type=jnp.float32)
                    tiles[place, part, :] = (tile * tok_scale).astype(tiles.dtype)
                both[i].start()

    if is_first:
        always = lax.axis_index("lat") >= 0
        send(count, 0, always, (own, own_twin))
        tiles[count + 1] = jnp.zeros((rows, width), tiles.dtype)
        for k, hop in enumerate(slot_hops):
            send(count + 1, k + 1, hop < 0, None)
    for j, hop in enumerate(hops):
        slot = jnp.int32(0)
        for k, h in enumerate(slot_hops):
            slot = jnp.where(h == hop, jnp.int32(k + 1), slot)
        send(j, slot, slot > 0, (blocks[j], twins[j]))
    for both, when in copies:

        @pl.when(when)
        def _():
            for copy in both:
                copy.wait()


def tiles_of(partners, owns, before, hops, blocks, twins, tok_scale, halves, n):
    first = before is None
    tok_rows, width = owns[0].shape
    slots = partners.shape[0]
    rows = width // halves
    dtype = owns[0].dtype
    out_shape = jax.ShapeDtypeStruct((1, slots, rows, width), dtype)
    left_shape = jax.ShapeDtypeStruct((rows, tok_rows * halves), dtype)
    if first:
        operands = (partners, *owns, *blocks, *twins)
    else:
        operands = (partners, before[0], *blocks, *twins, before[1])
    specs = [in_vmem] * len(operands)
    done = pl.pallas_call(
        functools.partial(tiles_kernel, tok_scale, n, hops, first),
        out_shape=(left_shape, out_shape) if first else out_shape,
        in_specs=specs if first else specs[:-1] + [in_hbm],
        out_specs=(in_vmem, in_hbm) if first else in_hbm,
        input_output_aliases={} if first else {len(operands) - 1: 0},
        scratch_shapes=[
            pltpu.VMEM((len(hops) + (2 if first else 0), rows, width), dtype),
            pltpu.SemaphoreType.DMA((len(hops) + (slots if first else 0), 2)),
        ],
        compiler_params=params,
        cost_estimate=pl.CostEstimate(
            flops=4 * rows * width * tok_rows * len(hops),
            bytes_accessed=4 * rows * width * len(hops),
            transcendentals=0,
        ),
    )(*operands)
    return done if first else (before[0], done)


def body(residual, enc_weight, enc_bias, threshold, partners):
    n = lax.axis_size("lat")
    halves = lax.axis_size("tok")
    tok_rows = residual.shape[0]
    width = enc_weight.shape[1]
    slots = partners.shape[1]
    tok_scale = 1.0 / (tok_rows * halves)
    swap = [(i, 1 - i) for i in range(2)]
    by_slot = partners.T
    if n == ring_size:
        ring = Ring(n)
        acts = encode_on_ring(residual, enc_weight, enc_bias, threshold, ring)
        acts_twin = lax.ppermute(acts, "tok", swap)

        def add_tiles(before, hops, blocks):
            twins = [lax.ppermute(block, "tok", swap) for block in blocks]
            owns = (acts, acts_twin)
            return tiles_of(by_slot, owns, before, hops, blocks, twins, tok_scale, halves, n)

        def beside_second(*_):
            return add_tiles(None, (), ())

        def beside_third(ahead, behind, ahead_2, behind_2, _, before):
            blocks = (ahead, behind, ahead_2, behind_2)
            return add_tiles(before, (1, n - 1, 2, n - 2), blocks)

        out, *late = ring.gather(acts, beside_second, beside_third)
        ahead, behind, corner, middle = late
        far = jnp.where(on_corner(n), corner, middle)
        out, ahead = lax.optimization_barrier((out, ahead))
        out = add_tiles(out, (3, n // 2), (ahead, far))
        return add_tiles(out, (n - 3,), (behind,))[1]
    acts = encode_gathered(residual, enc_weight, enc_bias, threshold)
    acts_twin = lax.ppermute(acts, "tok", swap)
    slices = lax.all_to_all(acts.reshape(n, tok_rows // n, width), "lat", 0, 0)
    outgoing = jnp.take(slices, jnp.minimum(partners[:, 1:], n - 1), axis=0)
    got = lax.all_to_all(outgoing, "lat", 0, 0)
    got = got.transpose(1, 0, 2, 3).reshape(slots - 1, tok_rows, width)
    got_twin = lax.ppermute(got, "tok", swap)
    return gram(by_slot, acts, acts_twin, got, got_twin, tok_scale, halves, n)


def solution(mesh):
    return jax.shard_map(
        body,
        mesh=mesh,
        in_specs=(P(("parts", "tok"), "lat"), P(None, "lat"), P("lat"), P("lat"), P()),
        out_specs=P(("parts", "lat"), None, "tok", None),
        check_vma=False,
    )
```
